512 devices in a mesh: ctx: 32 (over x_hi, z), head: 16 (over x_lo, y, core).
Axes of the slice: x: 4 (x_hi: 2, x_lo: 2; x = x_hi * 2 + x_lo), y: 4, z: 16, core: 2. Of those that a mesh axis runs over, the one named last changes fastest.
Arguments:
- queries: bfloat16 [4096, 2048], P('ctx', 'head'), may hold values from -6 to 6
- keys: bfloat16 [16384, 2048], P('ctx', 'head'), may hold values from -1.5 to 1.5
- values: bfloat16 [16384, 2048], P('ctx', 'head'), may hold values from -6 to 6
- d_out: bfloat16 [4096, 2048], P('ctx', 'head'), may hold values from -48 to 48
- key_weight: bfloat16 [2048, 2048], P(None, 'head'), may hold values from -0.1875 to 0.1875
- value_weight: bfloat16 [2048, 2048], P(None, 'head'), may hold values from -0.1875 to 0.1875
- block_lists: int32 [32, 64], replicated, may hold values from 0 to 127, all different within a row
Outputs:
- d_queries: bfloat16 [4096, 2048], P('ctx', 'head')
- d_memory: bfloat16 [16384, 2048], P('ctx', 'head')
The draws below stay inside these ranges and needn't reach their ends.
Inputs may be any that keep to these rules, and one draw needn't show every extreme that they name: `block_lists`: each row names 64 different encoder blocks; every encoder block is named by some row.
All inputs are finite; a program needn't handle non-finite values.
Results may differ from the reference program's by a relative error of at most 0.024.
Values may be sent and summed in bfloat16 or wider, within the bound.
No kernel may reach another device: no remote copies, remote signals or barrier semaphores. Data moves between devices by JAX's collectives and lax.ppermute only.
A program may use at most 64 MiB of HBM per device.

```python
import jax
import jax.numpy as jnp
from jax import lax

D = 2048
HEADS = 32
HEAD_DIM = 64
BLOCK = 128
TGT_TOKENS = 4096
ENC_TOKENS = 16384
TGT_BLOCKS = 32
ENC_BLOCKS = 128
LIST = 64


def draw_queries(key, part):
    key = jax.random.fold_in(key, 3)
    shape = (TGT_TOKENS, HEADS * HEAD_DIM)
    drawn = 0.35 * jnp.clip(jax.random.normal(key, shape, jnp.float32), -4.0, 4.0)
    return drawn.astype(jnp.bfloat16)


def draw_keys(key, part):
    key = jax.random.fold_in(key, 5)
    shape = (ENC_TOKENS, HEADS * HEAD_DIM)
    drawn = 0.35 * jnp.clip(jax.random.normal(key, shape, jnp.float32), -4.2, 4.2)
    return drawn.astype(jnp.bfloat16)


def spiked(entries, rng, source, target, parts, factor):
    owner, partner = [(jnp.arange(entries.shape[axis_at]) // (entries.shape[axis_at] // parts)).reshape([-1 if axis == axis_at else 1 for axis in range(entries.ndim)]) for axis_at in (source, target)]
    chosen = jax.random.permutation(rng, parts)[partner]
    strong = (owner == chosen) | (owner == (partner + parts // 2) % parts)
    return jnp.where(strong, factor * entries, entries)


def steps_of(stream_key, dims, split, low, high):
    loudness = 1.0
    for position, shards_of in split:
        steps = jax.random.uniform(jax.random.fold_in(jax.random.fold_in(stream_key, 6), position), (shards_of,), jnp.float32, low / len(split), high / len(split))
        loudness = loudness * jnp.repeat(jnp.exp(steps), dims[position] // shards_of).reshape((-1,) + (1,) * (len(dims) - 1 - position))
    return loudness


def different_ones(stream_key, rows, number_of, top, lift):
    ranking = jax.random.permutation(jax.random.fold_in(stream_key, 1), number_of)
    pull = ranking
    for power in range(3):
        pull = pull * pull // number_of
    pull = pull * lift // number_of
    tickets = jax.random.randint(jax.random.fold_in(stream_key, 2), (rows, number_of), 0, 4096) + pull
    holders = jax.random.permutation(jax.random.fold_in(stream_key, 3), rows)[jnp.arange(number_of) % rows]
    tickets = jnp.where(jnp.arange(rows)[:, None] == holders[None, :], 1 << 14, tickets)
    priority = tickets * number_of + jnp.arange(number_of)
    return lax.top_k(priority.astype(jnp.int32), top)[1].astype(jnp.int32)


def gaussian(stream_key, dims, width, bound, shards=(), kind=jnp.bfloat16):
    result = jax.random.normal(stream_key, dims, jnp.float32) * width
    if len(shards) > 0:
        result = steps_of(stream_key, dims, shards, -0.22, 0.18) * result
    return jnp.clip(result, min=-bound, max=bound).astype(kind)


def gaussian_with(own_key, extent, width, most, cuts, heavy, kind=jnp.bfloat16):
    entries = width * jax.random.normal(own_key, extent, jnp.float32)
    if cuts:
        entries = entries * steps_of(own_key, extent, cuts, -0.22, 0.18)
    return jnp.clip(spiked(entries, jax.random.fold_in(own_key, 3), *heavy), -most, most).astype(kind)


def setup_inputs(seed: int = 0) -> dict:
    key_of = jax.random.split(jax.random.key(seed), 8)
    queries = draw_queries(jax.random.fold_in(key_of[7], 71), 0)
    keys = draw_keys(jax.random.fold_in(key_of[7], 71), 0)
    values = gaussian(key_of[2], (ENC_TOKENS, HEADS * HEAD_DIM), 1.0, 6.0, ((0, 32), (1, 16)))
    d_out = gaussian(key_of[3], (TGT_TOKENS, HEADS * HEAD_DIM), 8.0, 48.0, ((0, 32), (1, 16)))
    key_weight = gaussian_with(key_of[4], (D, HEADS * HEAD_DIM), (HEADS * HEAD_DIM) ** -0.5, 0.1875, ((1, 16),), (1, 0, 16, 2.0))
    value_weight = gaussian_with(key_of[5], (D, HEADS * HEAD_DIM), (HEADS * HEAD_DIM) ** -0.5, 0.1875, ((1, 16),), (1, 0, 16, 2.0))
    block_lists = different_ones(key_of[6], TGT_BLOCKS, ENC_BLOCKS, LIST, 8192)
    return dict(queries=queries, keys=keys, values=values, d_out=d_out, key_weight=key_weight, value_weight=value_weight, block_lists=block_lists)


def reference(queries, keys, values, d_out, key_weight, value_weight, block_lists):
    query_blocks = queries.reshape(TGT_BLOCKS, BLOCK, HEADS, HEAD_DIM)
    out_blocks = d_out.reshape(TGT_BLOCKS, BLOCK, HEADS, HEAD_DIM)
    key_blocks = keys.reshape(ENC_BLOCKS, BLOCK, HEADS, HEAD_DIM)
    value_blocks = values.reshape(ENC_BLOCKS, BLOCK, HEADS, HEAD_DIM)

    def visit(carry, index):
        grad_key, grad_value = carry
        chosen = block_lists[index]
        query_rows = query_blocks[index].astype(jnp.float32)
        out_rows = out_blocks[index].astype(jnp.float32)
        key_rows = key_blocks[chosen].reshape(LIST * BLOCK, HEADS, HEAD_DIM).astype(jnp.float32)
        value_rows = value_blocks[chosen].reshape(LIST * BLOCK, HEADS, HEAD_DIM).astype(jnp.float32)
        logits = jnp.einsum('qhd,khd->hqk', query_rows, key_rows)
        peak = jnp.max(logits, axis=-1)
        raised = jnp.exp(logits - peak[..., None])
        totals = jnp.sum(raised, axis=-1)
        forward_weights = raised.astype(jnp.bfloat16).astype(jnp.float32)
        attended = jnp.einsum('hqk,khd->qhd', forward_weights, value_rows) / totals.T[:, :, None]
        log_totals = peak + jnp.log(totals)
        delta = jnp.sum(out_rows * attended, axis=-1).T
        chances = jnp.exp(logits - log_totals[..., None])
        rounded_chances = chances.astype(jnp.bfloat16).astype(jnp.float32)
        value_part = jnp.einsum('hqk,qhd->khd', rounded_chances, out_rows)
        grad_prob = jnp.einsum('qhd,khd->hqk', out_rows, value_rows)
        grad_logits = (chances * (grad_prob - delta[..., None])).astype(jnp.bfloat16).astype(jnp.float32)
        query_grad = jnp.einsum('hqk,khd->qhd', grad_logits, key_rows)
        key_part = jnp.einsum('hqk,qhd->khd', grad_logits, query_rows)
        grad_key = grad_key.at[chosen].add(key_part.reshape(LIST, BLOCK, HEADS, HEAD_DIM))
        grad_value = grad_value.at[chosen].add(value_part.reshape(LIST, BLOCK, HEADS, HEAD_DIM))
        return (grad_key, grad_value), query_grad.reshape(BLOCK, HEADS * HEAD_DIM).astype(jnp.bfloat16)

    empty = jnp.zeros((ENC_BLOCKS, BLOCK, HEADS, HEAD_DIM), jnp.float32)
    (grad_key, grad_value), query_grads = lax.scan(visit, (empty, empty), jnp.arange(TGT_BLOCKS, dtype=jnp.int32))
    d_queries = query_grads.reshape(TGT_TOKENS, HEADS * HEAD_DIM)
    rounded_key = grad_key.reshape(ENC_TOKENS, HEADS * HEAD_DIM).astype(jnp.bfloat16)
    rounded_value = grad_value.reshape(ENC_TOKENS, HEADS * HEAD_DIM).astype(jnp.bfloat16)
    memory = jnp.dot(rounded_key, key_weight.T, preferred_element_type=jnp.float32)
    memory = memory + jnp.dot(rounded_value, value_weight.T, preferred_element_type=jnp.float32)
    return d_queries, memory.astype(jnp.bfloat16)
```

```python
from functools import partial

import jax
import jax.numpy as jnp
from jax import lax
from jax.experimental import pallas as pl
from jax.experimental.pallas import tpu as pltpu
from jax.sharding import Mesh, PartitionSpec as P

HEAD_DIM = 64
BLOCK = 128
AXES = ("xh", "z", "xl", "y", "core")
SIZES = (2, 16, 2, 4, 2)
CTX = ("xh", "z")
HEAD = ("xl", "y", "core")
BIG = 1e30

OWN = (4, 0, -4, 8)
LATER = (3, -1, -5, 7, 5, 1, -3, 9, 6, 2, -2, -6)
SLOTS = OWN + LATER

VMEM = pl.BlockSpec(memory_space=pltpu.VMEM)
SMEM = pl.BlockSpec(memory_space=pltpu.SMEM)
ROOM = pltpu.CompilerParams(vmem_limit_bytes=48 * 1024 * 1024)


def dot_nt(a, b):
    return lax.dot_general(a, b, (((1,), (1,)), ((), ())), preferred_element_type=jnp.float32)


def dot_nn(a, b):
    return lax.dot_general(a, b, (((1,), (0,)), ((), ())), preferred_element_type=jnp.float32)


def split_heads(rows):
    low = lax.broadcasted_iota(jnp.int32, rows.shape, 1) < HEAD_DIM
    zero = jnp.zeros_like(rows)
    return jnp.concatenate([jnp.where(low, rows, zero), jnp.where(low, zero, rows)], axis=0)


def load_keys(k_ref, v_ref, far_ref, keys, vals):
    rows = k_ref.shape[0]
    keys[:rows, :] = k_ref[...]
    vals[:rows, :] = v_ref[...]
    keys[rows:, :] = far_ref[:, :BLOCK]
    vals[rows:, :] = far_ref[:, BLOCK:]


def load_targets(pieces, held):
    at = 0
    for piece in pieces:
        held[at : at + piece.shape[0], :] = piece[...]
        at += piece.shape[0]


def away(member, first, second, block, blocks):
    seg = (lax.broadcasted_iota(jnp.int32, (1, 4 * BLOCK), 1) // BLOCK) % 2
    one = jnp.where(member[first * blocks + block] > 0, 0.0, BIG)
    two = jnp.where(member[second * blocks + block] > 0, 0.0, BIG)
    return jnp.where(seg == 0, one, two)


def forward_kernel(base, places, member, k_ref, v_ref, far_ref, *rest):
    *pieces, before, stats, keys, vals, held = rest
    load_keys(k_ref, v_ref, far_ref, keys, vals)
    load_targets(pieces, held)
    blocks = keys.shape[0] // BLOCK
    pairs = held.shape[0] // (2 * BLOCK)
    half = stats.shape[0] // 2
    if before is not None:
        stats[...] = before[...]

    def step(p, carry):
        rows = pl.ds(pl.multiple_of(p * 2 * BLOCK, 2 * BLOCK), 2 * BLOCK)
        first, second = places[base + 2 * p], places[base + 2 * p + 1]
        query = split_heads(held[rows, :BLOCK])
        out = split_heads(held[rows, BLOCK:])
        logits = dot_nt(keys[...], query)
        prob = dot_nt(vals[...], out)
        off = [away(member, first, second, b, blocks) for b in range(blocks)]
        peak = jnp.full((1, 4 * BLOCK), -1e3, jnp.float32)
        for b in range(blocks):
            part = logits[b * BLOCK : (b + 1) * BLOCK]
            peak = jnp.maximum(peak, jnp.max(part, axis=0, keepdims=True) - off[b])
        total = jnp.zeros((1, 4 * BLOCK), jnp.float32)
        weighted = jnp.zeros((1, 4 * BLOCK), jnp.float32)
        for b in range(blocks):
            part = slice(b * BLOCK, (b + 1) * BLOCK)
            raised = jnp.exp(logits[part] - (peak + off[b]))
            total = total + jnp.sum(raised, axis=0, keepdims=True)
            weighted = weighted + jnp.sum(raised * prob[part], axis=0, keepdims=True)
        some = total > 0.0
        log_total = jnp.where(some, peak + jnp.log(jnp.where(some, total, 1.0)), -BIG)
        mean = jnp.where(some, weighted / jnp.where(some, total, 1.0), 0.0)
        for h in range(2):
            for s, place in enumerate((first, second)):
                lanes = slice((2 * h + s) * BLOCK, (2 * h + s + 1) * BLOCK)
                stats[pl.ds(2 * place + h, 1), :] = log_total[:, lanes]
                stats[pl.ds(half + 2 * place + h, 1), :] = mean[:, lanes]
        return carry

    lax.fori_loop(0, pairs, step, 0)


def forward(base, places, member, k, v, far, pieces, before):
    count = len(SLOTS)
    rows = sum(p.shape[0] for p in pieces)
    enc = k.shape[0] + far.shape[0]
    given = [places, member, k, v, far, *pieces]
    specs = [SMEM, SMEM] + [VMEM] * (3 + len(pieces))
    if before is None:
        def kernel(*refs):
            ins, outs = refs[: len(given)], refs[len(given) :]
            forward_kernel(base, *ins, None, *outs)
    else:
        given.append(before)
        specs.append(VMEM)
        kernel = partial(forward_kernel, base)
    return pl.pallas_call(
        kernel,
        out_shape=jax.ShapeDtypeStruct((4 * count, BLOCK), jnp.float32),
        in_specs=specs,
        out_specs=VMEM,
        scratch_shapes=[
            pltpu.VMEM((enc, BLOCK), jnp.bfloat16),
            pltpu.VMEM((enc, BLOCK), jnp.bfloat16),
            pltpu.VMEM((rows, 2 * BLOCK), jnp.bfloat16),
        ],
        compiler_params=ROOM,
        name="forward",
    )(*given)


def backward_kernel(places, member, core, stats, k_ref, v_ref, far_ref, *rest):
    pieces = rest[:5]
    d_query, kept, to_core, to_half, to_both, keys, vals, held, turned, chances, slopes, d_key, d_value = rest[5:]
    load_keys(k_ref, v_ref, far_ref, keys, vals)
    load_targets(pieces, held)
    enc = keys.shape[0]
    blocks = enc // BLOCK
    pairs = held.shape[0] // (2 * BLOCK)
    half = stats.shape[0] // 2
    turned[...] = keys[...].T
    d_key[...] = jnp.zeros_like(d_key)
    d_value[...] = jnp.zeros_like(d_value)

    def step(p, carry):
        rows = pl.ds(pl.multiple_of(p * 2 * BLOCK, 2 * BLOCK), 2 * BLOCK)
        first, second = places[2 * p], places[2 * p + 1]
        query = split_heads(held[rows, :BLOCK])
        out = split_heads(held[rows, BLOCK:])
        spots = [2 * place + h for h in range(2) for place in (first, second)]
        log_total = jnp.concatenate([stats[pl.ds(s, 1), :] for s in spots], axis=1)
        delta = jnp.concatenate([stats[pl.ds(half + s, 1), :] for s in spots], axis=1)
        logits = dot_nt(keys[...], query)
        prob = dot_nt(vals[...], out)
        for b in range(blocks):
            part = slice(b * BLOCK, (b + 1) * BLOCK)
            chance = jnp.exp(logits[part] - (log_total + away(member, first, second, b, blocks)))
            chances[part, :] = chance.astype(jnp.bfloat16)
            slopes[part, :] = (chance * (prob[part] - delta)).astype(jnp.bfloat16)
        d_value[...] += dot_nn(chances[...], out)
        d_key[...] += dot_nn(slopes[...], query)
        both = dot_nn(turned[...], slopes[...]).T
        low = lax.broadcasted_iota(jnp.int32, (2 * BLOCK, BLOCK), 1) < HEAD_DIM
        grad = jnp.where(low, both[: 2 * BLOCK], both[2 * BLOCK :]).astype(jnp.bfloat16)
        d_query[first] = grad[:BLOCK]
        d_query[second] = grad[BLOCK:]
        return carry

    lax.fori_loop(0, pairs, step, 0)
    quarter = enc // 4
    mine = core[0]
    other = 1 - mine

    def put(target, start):
        start = pl.multiple_of(start, quarter)
        target[:, :BLOCK] = d_key[pl.ds(start, quarter), :].astype(target.dtype)
        target[:, BLOCK:] = d_value[pl.ds(start, quarter), :].astype(target.dtype)

    put(kept, mine * quarter)
    put(to_core, other * quarter)
    put(to_half, (2 + mine) * quarter)
    put(to_both, (2 + other) * quarter)


def backward(places, member, core, stats, k, v, far, pieces):
    count = len(SLOTS)
    rows = sum(p.shape[0] for p in pieces)
    enc = k.shape[0] + far.shape[0]
    quarter = (enc // 4, 2 * BLOCK)
    given = [places, member, core, stats, k, v, far, *pieces]
    return pl.pallas_call(
        backward_kernel,
        out_shape=(
            jax.ShapeDtypeStruct((count, BLOCK, BLOCK), jnp.bfloat16),
            jax.ShapeDtypeStruct(quarter, jnp.float32),
            jax.ShapeDtypeStruct(quarter, jnp.bfloat16),
            jax.ShapeDtypeStruct(quarter, jnp.bfloat16),
            jax.ShapeDtypeStruct(quarter, jnp.bfloat16),
        ),
        in_specs=[SMEM] * 3 + [VMEM] * (len(given) - 3),
        out_specs=(VMEM,) * 5,
        scratch_shapes=[
            pltpu.VMEM((enc, BLOCK), jnp.bfloat16),
            pltpu.VMEM((enc, BLOCK), jnp.bfloat16),
            pltpu.VMEM((rows, 2 * BLOCK), jnp.bfloat16),
            pltpu.VMEM((BLOCK, enc), jnp.bfloat16),
            pltpu.VMEM((enc, 4 * BLOCK), jnp.bfloat16),
            pltpu.VMEM((enc, 4 * BLOCK), jnp.bfloat16),
            pltpu.VMEM((enc, BLOCK), jnp.float32),
            pltpu.VMEM((enc, BLOCK), jnp.float32),
        ],
        compiler_params=ROOM,
        name="backward",
    )(*given)


def project_kernel(kept, from_half, from_core, from_both, kw, vw, far_kw, far_vw, memory):
    mine = (kept[...] + from_half[...].astype(jnp.float32)).astype(jnp.bfloat16)
    other = (from_core[...].astype(jnp.float32) + from_both[...].astype(jnp.float32)).astype(jnp.bfloat16)
    for j in range(memory.shape[0]):
        columns = slice(j * BLOCK, (j + 1) * BLOCK)
        total = dot_nt(mine[:, :BLOCK], kw[columns, :]) + dot_nt(mine[:, BLOCK:], vw[columns, :])
        total = total + dot_nt(other[:, :BLOCK], far_kw[columns, :])
        total = total + dot_nt(other[:, BLOCK:], far_vw[columns, :])
        memory[j] = total.astype(jnp.bfloat16)


def moved(value, axis, steps):
    count = lax.axis_size(axis)
    return lax.ppermute(value, axis, [(i, (i + steps) % count) for i in range(count)])


def merged(parts):
    half = parts[0].shape[0] // 2
    logs = [p[:half] for p in parts]
    top = logs[0]
    for log in logs[1:]:
        top = jnp.maximum(top, log)
    weights = [jnp.exp(log - top) for log in logs]
    total = sum(weights[1:], weights[0])
    mean = sum((w * p[half:] for w, p in zip(weights[1:], parts[1:])), weights[0] * parts[0][half:])
    return jnp.concatenate([top + jnp.log(total), mean / total], axis=0)


def body(queries, keys, values, d_out, key_weight, value_weight, block_lists):
    half = lax.axis_index("xh")
    place = lax.axis_index("z")
    core = lax.axis_index("core")
    depth = lax.axis_size("z")
    count = len(SLOTS)
    enc_blocks = keys.shape[0] // BLOCK

    near = jnp.concatenate([queries, d_out], axis=1)
    ahead = moved(near, "z", 4)
    behind = moved(near, "z", -4)
    across = moved(near, "z", 8)
    far = moved(jnp.concatenate([keys, values], axis=1), "xh", 1)

    places = (place + jnp.asarray(SLOTS, jnp.int32)) % depth
    listed = lax.dynamic_slice_in_dim(block_lists, half * count, count, 0)
    step = jnp.arange(enc_blocks, dtype=jnp.int32)
    ids = jnp.concatenate(
        [(half * depth + place) * enc_blocks + step, ((1 - half) * depth + place) * enc_blocks + step]
    )
    member = jnp.any(listed[:, :, None] == ids[None, None, :], axis=1).astype(jnp.int32).reshape(-1)

    bundle = jnp.concatenate([behind, near, ahead, across], axis=0)
    below = moved(bundle, "z", 1)
    above = moved(bundle, "z", -1)
    above2 = moved(bundle[: 2 * BLOCK], "z", -2)
    below2 = moved(bundle[BLOCK : 3 * BLOCK], "z", 2)
    far_kw = moved(key_weight, "core", 1)
    far_vw = moved(value_weight, "core", 1)

    early = forward(0, places, member, keys, values, far, [bundle], None)
    pieces = [below, above, above2, below2]
    stats = forward(len(OWN), places, member, keys, values, far, pieces, early)
    stats = merged([stats, moved(stats, "z", 4), moved(stats, "z", -4), moved(stats, "z", 8)])
    stats = merged([stats, moved(stats, "z", 1), moved(stats, "z", -1), moved(stats, "z", 2)])

    d_query, kept, to_core, to_half, to_both = backward(
        places, member, core[None], stats, keys, values, far, [bundle, *pieces]
    )
    from_half = moved(to_half, "xh", 1)
    from_core = moved(to_core, "core", 1)
    from_both = lax.ppermute(to_both, ("xh", "core"), [(0, 3), (1, 2), (2, 1), (3, 0)])

    chunks = key_weight.shape[0] // BLOCK
    memory = pl.pallas_call(
        project_kernel,
        out_shape=jax.ShapeDtypeStruct((chunks, kept.shape[0], BLOCK), jnp.bfloat16),
        in_specs=[VMEM] * 8,
        out_specs=VMEM,
        compiler_params=ROOM,
        name="project",
    )(kept, from_half, from_core, from_both, key_weight, value_weight, far_kw, far_vw)
    memory = lax.all_to_all(memory, HEAD, 0, 0, tiled=True)
    d_query = lax.all_to_all(d_query, "z", 0, 0, tiled=True)

    cores = lax.axis_size("core")
    memory = memory.reshape(chunks // cores, cores, *memory.shape[1:]).astype(jnp.float32)
    d_memory = jnp.sum(memory, axis=0).reshape(keys.shape).astype(jnp.bfloat16)
    d_queries = jnp.sum(d_query.astype(jnp.float32), axis=0).astype(jnp.bfloat16)
    return d_queries, d_memory


def solution(mesh):
    fine = Mesh(mesh.devices.reshape(SIZES), AXES)
    placed = P(CTX, HEAD)
    return jax.shard_map(
        body,
        mesh=fine,
        in_specs=(placed, placed, placed, placed, P(None, HEAD), P(None, HEAD), P()),
        out_specs=(placed, placed),
        check_vma=False,
    )
```

```python
from functools import partial

import jax
import jax.numpy as jnp
from jax import lax
from jax.experimental import pallas as pl
from jax.experimental.pallas import tpu as pltpu
from jax.sharding import Mesh, PartitionSpec as P

HEAD_DIM = 64
BLOCK = 128
AXES = ("xh", "zh", "zl", "xl", "y", "core")
SIZES = (2, 4, 4, 2, 4, 2)
Z = ("zh", "zl")
CTX = ("xh", "zh", "zl")
HEAD = ("xl", "y", "core")
BIG = 1e30

VMEM = pl.BlockSpec(memory_space=pltpu.VMEM)
SMEM = pl.BlockSpec(memory_space=pltpu.SMEM)
ROOM = pltpu.CompilerParams(vmem_limit_bytes=48 * 1024 * 1024)


def cost(flops, exps):
    return pl.CostEstimate(flops=4 * flops, bytes_accessed=1 << 20, transcendentals=exps)


def dot_nt(a, b):
    return lax.dot_general(a, b, (((1,), (1,)), ((), ())), preferred_element_type=jnp.float32)


def dot_nn(a, b):
    return lax.dot_general(a, b, (((1,), (0,)), ((), ())), preferred_element_type=jnp.float32)


def split_heads(rows):
    low = lax.broadcasted_iota(jnp.int32, rows.shape, 1) < HEAD_DIM
    zero = jnp.zeros_like(rows)
    return jnp.concatenate([jnp.where(low, rows, zero), jnp.where(low, zero, rows)], axis=0)


def load_keys(near_ref, far_ref, keys, vals):
    rows = near_ref.shape[0]
    keys[:rows, :] = near_ref[:, :BLOCK]
    vals[:rows, :] = near_ref[:, BLOCK:]
    keys[rows:, :] = far_ref[:, :BLOCK]
    vals[rows:, :] = far_ref[:, BLOCK:]


def load_targets(pieces, held):
    at = 0
    for piece in pieces:
        held[at : at + piece.shape[0], :] = piece[...]
        at += piece.shape[0]


def away(member, first, second, block, blocks):
    seg = (lax.broadcasted_iota(jnp.int32, (1, 4 * BLOCK), 1) // BLOCK) % 2
    one = jnp.where(member[first * blocks + block] > 0, 0.0, BIG)
    two = jnp.where(member[second * blocks + block] > 0, 0.0, BIG)
    return jnp.where(seg == 0, one, two)


def forward_kernel(base, places, member, near_ref, far_ref, *rest):
    *pieces, before, stats, keys, vals, held = rest
    load_keys(near_ref, far_ref, keys, vals)
    load_targets(pieces, held)
    blocks = keys.shape[0] // BLOCK
    pairs = held.shape[0] // (2 * BLOCK)
    half = stats.shape[0] // 2
    if before is not None:
        stats[...] = before[...]

    def step(p, carry):
        rows = pl.ds(pl.multiple_of(p * 2 * BLOCK, 2 * BLOCK), 2 * BLOCK)
        first, second = places[base + 2 * p], places[base + 2 * p + 1]
        query = split_heads(held[rows, :BLOCK])
        out = split_heads(held[rows, BLOCK:])
        logits = dot_nt(keys[...], query)
        prob = dot_nt(vals[...], out)
        off = [away(member, first, second, b, blocks) for b in range(blocks)]
        peak = jnp.full((1, 4 * BLOCK), -1e3, jnp.float32)
        for b in range(blocks):
            part = logits[b * BLOCK : (b + 1) * BLOCK]
            peak = jnp.maximum(peak, jnp.max(part, axis=0, keepdims=True) - off[b])
        total = jnp.zeros((1, 4 * BLOCK), jnp.float32)
        weighted = jnp.zeros((1, 4 * BLOCK), jnp.float32)
        for b in range(blocks):
            part = slice(b * BLOCK, (b + 1) * BLOCK)
            raised = jnp.exp(logits[part] - (peak + off[b]))
            total = total + jnp.sum(raised, axis=0, keepdims=True)
            weighted = weighted + jnp.sum(raised * prob[part], axis=0, keepdims=True)
        some = total > 0.0
        log_total = jnp.where(some, peak + jnp.log(jnp.where(some, total, 1.0)), -BIG)
        mean = jnp.where(some, weighted / jnp.where(some, total, 1.0), 0.0)
        for h in range(2):
            for s, place in enumerate((first, second)):
                lanes = slice((2 * h + s) * BLOCK, (2 * h + s + 1) * BLOCK)
                stats[pl.ds(2 * place + h, 1), :] = log_total[:, lanes]
                stats[pl.ds(half + 2 * place + h, 1), :] = mean[:, lanes]
        return carry

    def two(i, carry):
        return step(2 * i + 1, step(2 * i, carry))

    lax.fori_loop(0, pairs // 2, two, 0)


def forward(base, places, member, near, far, pieces, before):
    count = places.shape[0]
    rows = sum(p.shape[0] for p in pieces)
    enc = near.shape[0] + far.shape[0]
    given = [places, member, near, far, *pieces]
    specs = [SMEM, SMEM] + [VMEM] * (2 + len(pieces))
    if before is None:
        def kernel(*refs):
            ins, outs = refs[: len(given)], refs[len(given) :]
            forward_kernel(base, *ins, None, *outs)
    else:
        given.append(before)
        specs.append(VMEM)
        kernel = partial(forward_kernel, base)
    return pl.pallas_call(
        kernel,
        out_shape=jax.ShapeDtypeStruct((4 * count, BLOCK), jnp.float32),
        in_specs=specs,
        out_specs=VMEM,
        scratch_shapes=[
            pltpu.VMEM((enc, BLOCK), jnp.bfloat16),
            pltpu.VMEM((enc, BLOCK), jnp.bfloat16),
            pltpu.VMEM((rows, 2 * BLOCK), jnp.bfloat16),
        ],
        compiler_params=ROOM,
        cost_estimate=cost(2 * rows * enc * 4 * BLOCK, rows * enc * 2),
        name="forward",
    )(*given)


def backward_kernel(base, places, member, core, stats, kv_ref, before, *rest):
    pieces = rest[:5]
    d_query, stay, leave, held, turned, chances, slopes, d_key, d_value = rest[5:]
    load_targets(pieces, held)
    enc = kv_ref.shape[0]
    blocks = enc // BLOCK
    pairs = held.shape[0] // (2 * BLOCK)
    half = stats.shape[0] // 2
    turned[...] = kv_ref[:, :BLOCK].T
    d_key[...] = jnp.zeros_like(d_key)
    d_value[...] = jnp.zeros_like(d_value)

    def step(p, u):
        rows = pl.ds(pl.multiple_of(p * 2 * BLOCK, 2 * BLOCK), 2 * BLOCK)
        first, second = places[2 * p], places[2 * p + 1]
        query = split_heads(held[rows, :BLOCK])
        out = split_heads(held[rows, BLOCK:])
        spots = [2 * place + h for h in range(2) for place in (first, second)]
        log_total = jnp.concatenate([stats[pl.ds(s, 1), :] for s in spots], axis=1)
        delta = jnp.concatenate([stats[pl.ds(half + s, 1), :] for s in spots], axis=1)
        logits = dot_nt(kv_ref[:, :BLOCK], query)
        prob = dot_nt(kv_ref[:, BLOCK:], out)
        for b in range(blocks):
            part = slice(b * BLOCK, (b + 1) * BLOCK)
            off = away(member, first, second, base + b, 2 * blocks)
            chance = jnp.exp(logits[part] - (log_total + off))
            chances[u, part, :] = chance.astype(jnp.bfloat16)
            slopes[u, part, :] = (chance * (prob[part] - delta)).astype(jnp.bfloat16)
        d_value[...] += dot_nn(chances[u], out)
        d_key[...] += dot_nn(slopes[u], query)
        both = dot_nn(turned[...], slopes[u]).T
        low = lax.broadcasted_iota(jnp.int32, (2 * BLOCK, BLOCK), 1) < HEAD_DIM
        grad = jnp.where(low, both[: 2 * BLOCK], both[2 * BLOCK :])
        for place, part in ((first, grad[:BLOCK]), (second, grad[BLOCK:])):
            if before is not None:
                part = part + before[place]
            d_query[place] = part.astype(d_query.dtype)

    def two(i, carry):
        step(2 * i, 0)
        step(2 * i + 1, 1)
        return carry

    lax.fori_loop(0, pairs // 2, two, 0)
    mine = core[0]
    for target, part in ((stay, mine), (leave, 1 - mine)):
        rows = pl.ds(pl.multiple_of(part * (enc // 2), enc // 2), enc // 2)
        target[:, :BLOCK] = d_key[rows, :].astype(target.dtype)
        target[:, BLOCK:] = d_value[rows, :].astype(target.dtype)


def backward(base, places, member, core, stats, kv, pieces, before, kinds):
    count = places.shape[0]
    rows = sum(p.shape[0] for p in pieces)
    enc = kv.shape[0]
    shape = (enc // 2, 2 * BLOCK)
    given = [places, member, core, stats, kv]
    fixed = len(given)
    if before is None:
        def kernel(*refs):
            backward_kernel(base, *refs[:fixed], None, *refs[fixed:])
    else:
        given.append(before)
        kernel = partial(backward_kernel, base)
    given += pieces
    return pl.pallas_call(
        kernel,
        out_shape=(
            jax.ShapeDtypeStruct((count, BLOCK, BLOCK), kinds[0]),
            jax.ShapeDtypeStruct(shape, kinds[1]),
            jax.ShapeDtypeStruct(shape, kinds[2]),
        ),
        in_specs=[SMEM] * 3 + [VMEM] * (len(given) - 3),
        out_specs=(VMEM,) * 3,
        scratch_shapes=[
            pltpu.VMEM((rows, 2 * BLOCK), jnp.bfloat16),
            pltpu.VMEM((BLOCK, enc), jnp.bfloat16),
            pltpu.VMEM((2, enc, 4 * BLOCK), jnp.bfloat16),
            pltpu.VMEM((2, enc, 4 * BLOCK), jnp.bfloat16),
            pltpu.VMEM((enc, BLOCK), jnp.float32),
            pltpu.VMEM((enc, BLOCK), jnp.float32),
        ],
        compiler_params=ROOM,
        cost_estimate=cost(5 * rows * enc * 4 * BLOCK, rows * enc * 2),
        name="backward",
    )(*given)


def project_kernel(part, kept, from_half, from_core, from_both, kw, vw, far, *rest):
    *before, memory = rest
    mine = (kept[...] + from_half[...].astype(jnp.float32)).astype(jnp.bfloat16)
    other = (from_core[...].astype(jnp.float32) + from_both[...].astype(jnp.float32)).astype(jnp.bfloat16)
    chunks = memory.shape[0]
    for j in range(chunks):
        rows = pl.ds(pl.multiple_of((part[0] * chunks + j) * BLOCK, BLOCK), BLOCK)
        total = dot_nt(mine[:, :BLOCK], kw[rows, :]) + dot_nt(mine[:, BLOCK:], vw[rows, :])
        total = total + dot_nt(other, far[rows, :])
        for piece in before:
            total = total + piece[j].astype(jnp.float32)
        memory[j] = total.astype(jnp.bfloat16)


def project(part, chunks, *given):
    return pl.pallas_call(
        project_kernel,
        out_shape=jax.ShapeDtypeStruct((chunks, given[0].shape[0], BLOCK), jnp.bfloat16),
        in_specs=[SMEM] + [VMEM] * len(given),
        out_specs=VMEM,
        compiler_params=ROOM,
        name="project",
    )(part[None], *given)


def moved(value, axis, steps):
    count = lax.axis_size(axis)
    return lax.ppermute(value, axis, [(i, (i + steps) % count) for i in range(count)])


def merged(parts):
    half = parts[0].shape[0] // 2
    logs = [p[:half] for p in parts]
    top = logs[0]
    for log in logs[1:]:
        top = jnp.maximum(top, log)
    weights = [jnp.exp(log - top) for log in logs]
    total = sum(weights[1:], weights[0])
    mean = sum((w * p[half:] for w, p in zip(weights[1:], parts[1:])), weights[0] * parts[0][half:])
    return jnp.concatenate([top + jnp.log(total), mean / total], axis=0)


def spread(value, axis):
    count = lax.axis_size(axis)
    return lax.all_to_all(jnp.broadcast_to(value, (count, *value.shape)), axis, 0, 0, tiled=True)


def body(queries, keys, values, d_out, key_weight, value_weight, block_lists):
    half = lax.axis_index("xh")
    place = lax.axis_index(Z)
    core = lax.axis_index("core")
    depth = lax.axis_size(Z)
    high, low = lax.axis_size("zh"), lax.axis_size("zl")
    enc_blocks = keys.shape[0] // BLOCK

    near = jnp.concatenate([queries, d_out], axis=1)
    bundle = spread(near, "zh").reshape(high * BLOCK, 2 * BLOCK)

    strides = low * jnp.arange(high, dtype=jnp.int32)
    places = jnp.concatenate([strides + (place + step) % low for step in (0, -1, 1, 2)])
    listed = lax.dynamic_slice_in_dim(block_lists, half * depth, depth, 0)
    step = jnp.arange(enc_blocks, dtype=jnp.int32)
    ids = jnp.concatenate(
        [(half * depth + place) * enc_blocks + step, ((1 - half) * depth + place) * enc_blocks + step]
    )
    member = jnp.any(listed[:, :, None] == ids[None, None, :], axis=1).astype(jnp.int32).reshape(-1)

    below = moved(bundle, Z, 1)
    above = moved(bundle, Z, -1)
    above2 = moved(bundle[: 2 * BLOCK], Z, -2)
    below2 = moved(bundle[2 * BLOCK :], Z, 2)
    own, bundle = lax.optimization_barrier((jnp.concatenate([keys, values], axis=1), bundle))
    far = moved(own, "xh", 1)

    early = forward(0, places, member, own, far, [bundle], None)
    pieces = [below, above, above2, below2]
    stats = forward(high, places, member, own, far, pieces, early)
    stats = merged(list(spread(stats, "zh")))
    stats = merged([stats, moved(stats, Z, 2)])
    stats = merged([stats, moved(stats, Z, 1)])

    weights, stats = lax.optimization_barrier((jnp.concatenate([key_weight, value_weight], axis=1), stats))
    pieces = [bundle, *pieces]
    f32, bf16 = jnp.float32, jnp.bfloat16
    d_query, to_half, to_both = backward(
        enc_blocks, places, member, core[None], stats, far, pieces, None, (f32, bf16, bf16)
    )
    from_half = moved(to_half, "xh", 1)
    from_both = lax.ppermute(to_both, ("xh", "core"), [(0, 3), (1, 2), (2, 1), (3, 0)])
    far_weights = moved(weights, "core", 1)
    d_query, kept, to_core = backward(
        0, places, member, core[None], stats, own, pieces, d_query, (bf16, f32, bf16)
    )
    d_query, to_core, from_half, from_both, far_weights = lax.optimization_barrier(
        (d_query, to_core, from_half, from_both, far_weights)
    )
    d_query = lax.all_to_all(d_query, Z, 0, 0, tiled=True)
    from_core = moved(to_core, "core", 1)

    side = lax.axis_index("xl")
    sides = lax.axis_size("xl")
    chunks = key_weight.shape[0] // (sides * BLOCK)
    given = (kept, from_half, from_core, from_both, key_weight, value_weight, far_weights)
    if sides > 1:
        given += (moved(project(1 - side, chunks, *given), "xl", 1),)
    memory, d_query = lax.optimization_barrier((project(side, chunks, *given), d_query))
    memory = lax.all_to_all(memory, ("y", "core"), 0, 0, tiled=True)

    cores = lax.axis_size("core")
    memory = memory.reshape(chunks // cores, cores, *memory.shape[1:]).astype(f32)
    d_memory = jnp.sum(memory, axis=0).reshape(keys.shape).astype(bf16)
    d_queries = jnp.sum(d_query.astype(f32), axis=0).astype(bf16)
    return d_queries, d_memory


def solution(mesh):
    fine = Mesh(mesh.devices.reshape(SIZES), AXES)
    placed = P(CTX, HEAD)
    return jax.shard_map(
        body,
        mesh=fine,
        in_specs=(placed, placed, placed, placed, P(None, HEAD), P(None, HEAD), P()),
        out_specs=(placed, placed),
        check_vma=False,
    )
```

```python
from functools import partial

import jax
import jax.numpy as jnp
from jax import lax
from jax.experimental import pallas as pl
from jax.experimental.pallas import tpu as pltpu
from jax.sharding import Mesh, PartitionSpec as P

HEAD_DIM = 64
BLOCK = 128
AXES = ("xh", "z", "xl", "y", "core")
SIZES = (2, 16, 2, 4, 2)
Z = "z"
CTX = ("xh", "z")
HEAD = ("xl", "y", "core")
BIG = 1e30

OWN = (4, 0, -4, 8)
LATER = (3, -1, -5, 7, 5, 1, -3, 9, 6, 2, -2, -6)
SLOTS = OWN + LATER

VMEM = pl.BlockSpec(memory_space=pltpu.VMEM)
SMEM = pl.BlockSpec(memory_space=pltpu.SMEM)
ROOM = pltpu.CompilerParams(vmem_limit_bytes=48 * 1024 * 1024)


def cost(flops, exps):
    return pl.CostEstimate(flops=4 * flops, bytes_accessed=1 << 20, transcendentals=exps)


def dot_nt(a, b):
    return lax.dot_general(a, b, (((1,), (1,)), ((), ())), preferred_element_type=jnp.float32)


def dot_nn(a, b):
    return lax.dot_general(a, b, (((1,), (0,)), ((), ())), preferred_element_type=jnp.float32)


def split_heads(rows):
    low = lax.broadcasted_iota(jnp.int32, rows.shape, 1) < HEAD_DIM
    zero = jnp.zeros_like(rows)
    return jnp.concatenate([jnp.where(low, rows, zero), jnp.where(low, zero, rows)], axis=0)


def load_keys(near_ref, far_ref, keys, vals):
    rows = near_ref.shape[0]
    keys[:rows, :] = near_ref[:, :BLOCK]
    vals[:rows, :] = near_ref[:, BLOCK:]
    keys[rows:, :] = far_ref[:, :BLOCK]
    vals[rows:, :] = far_ref[:, BLOCK:]


def load_targets(pieces, held):
    at = 0
    for piece in pieces:
        held[at : at + piece.shape[0], :] = piece[...]
        at += piece.shape[0]


def away(member, first, second, block, blocks):
    seg = (lax.broadcasted_iota(jnp.int32, (1, 4 * BLOCK), 1) // BLOCK) % 2
    one = jnp.where(member[first * blocks + block] > 0, 0.0, BIG)
    two = jnp.where(member[second * blocks + block] > 0, 0.0, BIG)
    return jnp.where(seg == 0, one, two)


def forward_kernel(base, places, member, near_ref, far_ref, *rest):
    *pieces, before, result, keys, vals, held, stats = rest
    load_keys(near_ref, far_ref, keys, vals)
    load_targets(pieces, held)
    blocks = keys.shape[0] // BLOCK
    pairs = held.shape[0] // (2 * BLOCK)
    half = stats.shape[0] // 2
    if before is not None:
        stats[...] = before[...]

    def step(p, carry):
        rows = pl.ds(pl.multiple_of(p * 2 * BLOCK, 2 * BLOCK), 2 * BLOCK)
        first, second = places[base + 2 * p], places[base + 2 * p + 1]
        query = split_heads(held[rows, :BLOCK])
        out = split_heads(held[rows, BLOCK:])
        logits = dot_nt(keys[...], query)
        prob = dot_nt(vals[...], out)
        off = [away(member, first, second, b, blocks) for b in range(blocks)]
        peak = jnp.full((1, 4 * BLOCK), -1e3, jnp.float32)
        for b in range(blocks):
            part = logits[b * BLOCK : (b + 1) * BLOCK]
            peak = jnp.maximum(peak, jnp.max(part, axis=0, keepdims=True) - off[b])
        total = jnp.zeros((1, 4 * BLOCK), jnp.float32)
        weighted = jnp.zeros((1, 4 * BLOCK), jnp.float32)
        for b in range(blocks):
            part = slice(b * BLOCK, (b + 1) * BLOCK)
            raised = jnp.exp(logits[part] - (peak + off[b]))
            total = total + jnp.sum(raised, axis=0, keepdims=True)
            weighted = weighted + jnp.sum(raised * prob[part], axis=0, keepdims=True)
        some = total > 0.0
        log_total = jnp.where(some, peak + jnp.log(jnp.where(some, total, 1.0)), -BIG)
        mean = jnp.where(some, weighted / jnp.where(some, total, 1.0), 0.0)
        for h in range(2):
            for s, place in enumerate((first, second)):
                lanes = slice((2 * h + s) * BLOCK, (2 * h + s + 1) * BLOCK)
                stats[pl.ds(2 * place + h, 1), :] = log_total[:, lanes]
                stats[pl.ds(half + 2 * place + h, 1), :] = mean[:, lanes]
        return carry

    def two(i, carry):
        return step(2 * i + 1, step(2 * i, carry))

    lax.fori_loop(0, pairs // 2, two, 0)
    if before is None:
        result[...] = stats[...]
    else:
        high = stats[:half, :].astype(jnp.bfloat16)
        low = (stats[:half, :] - high.astype(jnp.float32)).astype(jnp.bfloat16)
        message = jnp.concatenate([high, low, stats[half:, :].astype(jnp.bfloat16)], axis=0)
        for peer in range(result.shape[0]):
            result[peer] = message


def forward(base, places, member, near, far, pieces, before):
    count = places.shape[0]
    rows = sum(p.shape[0] for p in pieces)
    enc = near.shape[0] + far.shape[0]
    given = [places, member, near, far, *pieces]
    specs = [SMEM, SMEM] + [VMEM] * (2 + len(pieces))
    shape = jax.ShapeDtypeStruct((4 * count, BLOCK), jnp.float32)
    if before is None:
        def kernel(*refs):
            ins, outs = refs[: len(given)], refs[len(given) :]
            forward_kernel(base, *ins, None, *outs)
    else:
        given.append(before)
        specs.append(VMEM)
        shape = jax.ShapeDtypeStruct((count, 6 * count, BLOCK), jnp.bfloat16)
        kernel = partial(forward_kernel, base)
    return pl.pallas_call(
        kernel,
        out_shape=shape,
        in_specs=specs,
        out_specs=VMEM,
        scratch_shapes=[
            pltpu.VMEM((enc, BLOCK), jnp.bfloat16),
            pltpu.VMEM((enc, BLOCK), jnp.bfloat16),
            pltpu.VMEM((rows, 2 * BLOCK), jnp.bfloat16),
            pltpu.VMEM((4 * count, BLOCK), jnp.float32),
        ],
        compiler_params=ROOM,
        cost_estimate=cost(2 * rows * enc * 4 * BLOCK, rows * enc * 2),
        name="forward",
    )(*given)


def merge_stats(parts, stats):
    rows = stats.shape[0] // 2
    logs = [
        parts[i, :rows, :].astype(jnp.float32) + parts[i, rows : 2 * rows, :].astype(jnp.float32)
        for i in range(parts.shape[0])
    ]
    top = logs[0]
    for log in logs[1:]:
        top = jnp.maximum(top, log)
    total = jnp.zeros_like(top)
    mean = jnp.zeros_like(top)
    for i, log in enumerate(logs):
        weight = jnp.exp(log - top)
        total = total + weight
        mean = mean + weight * parts[i, 2 * rows :, :].astype(jnp.float32)
    stats[:rows, :] = top + jnp.log(total)
    stats[rows:, :] = mean / total


def backward_kernel(base, whole, places, member, core, parts, kv_ref, before, *rest):
    pieces = rest[:5]
    d_query, *sent, held, turned, chances, slopes, d_key, d_value, stats = rest[5:]
    merge_stats(parts, stats)
    load_targets(pieces, held)
    enc = kv_ref.shape[0]
    blocks = enc // BLOCK
    pairs = held.shape[0] // (2 * BLOCK)
    half = stats.shape[0] // 2
    turned[...] = kv_ref[:, :BLOCK].T
    d_key[...] = jnp.zeros_like(d_key)
    d_value[...] = jnp.zeros_like(d_value)

    def step(p, u):
        rows = pl.ds(pl.multiple_of(p * 2 * BLOCK, 2 * BLOCK), 2 * BLOCK)
        first, second = places[2 * p], places[2 * p + 1]
        query = split_heads(held[rows, :BLOCK])
        out = split_heads(held[rows, BLOCK:])
        spots = [2 * place + h for h in range(2) for place in (first, second)]
        log_total = jnp.concatenate([stats[pl.ds(s, 1), :] for s in spots], axis=1)
        delta = jnp.concatenate([stats[pl.ds(half + s, 1), :] for s in spots], axis=1)
        logits = dot_nt(kv_ref[:, :BLOCK], query)
        prob = dot_nt(kv_ref[:, BLOCK:], out)
        for b in range(blocks):
            part = slice(b * BLOCK, (b + 1) * BLOCK)
            off = away(member, first, second, base + b, 2 * blocks)
            chance = jnp.exp(logits[part] - (log_total + off))
            chances[u, part, :] = chance.astype(jnp.bfloat16)
            slopes[u, part, :] = (chance * (prob[part] - delta)).astype(jnp.bfloat16)
        d_value[...] += dot_nn(chances[u], out)
        d_key[...] += dot_nn(slopes[u], query)
        both = dot_nn(turned[...], slopes[u]).T
        low = lax.broadcasted_iota(jnp.int32, (2 * BLOCK, BLOCK), 1) < HEAD_DIM
        grad = jnp.where(low, both[: 2 * BLOCK], both[2 * BLOCK :])
        for place, part in ((first, grad[:BLOCK]), (second, grad[BLOCK:])):
            if before is not None:
                part = part + before[place]
            d_query[place] = part.astype(d_query.dtype)

    def two(i, carry):
        step(2 * i, 0)
        step(2 * i + 1, 1)
        return carry

    lax.fori_loop(0, pairs // 2, two, 0)
    if whole:
        sent[0][:, :BLOCK] = d_key[...].astype(jnp.bfloat16)
        sent[0][:, BLOCK:] = d_value[...].astype(jnp.bfloat16)
    else:
        for target, part in zip(sent, (core[0], 1 - core[0]), strict=True):
            rows = pl.ds(pl.multiple_of(part * (enc // 2), enc // 2), enc // 2)
            target[:, :BLOCK] = d_key[rows, :]
            target[:, BLOCK:] = d_value[rows, :]


def backward(base, places, member, core, parts, kv, pieces, before):
    whole = before is None
    count = places.shape[0]
    rows = sum(p.shape[0] for p in pieces)
    enc = kv.shape[0]
    given = [places, member, core, parts, kv]
    fixed = len(given)
    if whole:
        sent = [jax.ShapeDtypeStruct((enc, 2 * BLOCK), jnp.bfloat16)]
        def kernel(*refs):
            backward_kernel(base, whole, *refs[:fixed], None, *refs[fixed:])
    else:
        sent = [jax.ShapeDtypeStruct((enc // 2, 2 * BLOCK), jnp.float32)] * 2
        given.append(before)
        kernel = partial(backward_kernel, base, whole)
    given += pieces
    kind = jnp.float32 if whole else jnp.bfloat16
    return pl.pallas_call(
        kernel,
        out_shape=[jax.ShapeDtypeStruct((count, BLOCK, BLOCK), kind), *sent],
        in_specs=[SMEM] * 3 + [VMEM] * (len(given) - 3),
        out_specs=[VMEM] * (1 + len(sent)),
        scratch_shapes=[
            pltpu.VMEM((rows, 2 * BLOCK), jnp.bfloat16),
            pltpu.VMEM((BLOCK, enc), jnp.bfloat16),
            pltpu.VMEM((2, enc, 4 * BLOCK), jnp.bfloat16),
            pltpu.VMEM((2, enc, 4 * BLOCK), jnp.bfloat16),
            pltpu.VMEM((enc, BLOCK), jnp.float32),
            pltpu.VMEM((enc, BLOCK), jnp.float32),
            pltpu.VMEM((4 * count, BLOCK), jnp.float32),
        ],
        compiler_params=ROOM,
        cost_estimate=cost(5 * rows * enc * 4 * BLOCK, rows * enc * 2),
        name="backward",
    )(*given)


def project_kernel(core, chunk, kept, from_half, from_core, kw, vw, far, *rest):
    *before, memory = rest
    rows = kept.shape[0]
    half = from_half[pl.ds(pl.multiple_of(core[0] * rows, rows), rows), :]
    mine = (kept[...] + half.astype(jnp.float32)).astype(jnp.bfloat16)
    other = from_core[...]
    for j in range(memory.shape[0]):
        part = pl.ds(pl.multiple_of(chunk[j] * BLOCK, BLOCK), BLOCK)
        total = dot_nt(mine[:, :BLOCK], kw[part, :]) + dot_nt(mine[:, BLOCK:], vw[part, :])
        total = total + dot_nt(other, far[part, :])
        for piece in before:
            total = total + piece[j].astype(jnp.float32)
        memory[j] = total.astype(jnp.bfloat16)


def project(core, chunk, *given):
    return pl.pallas_call(
        project_kernel,
        out_shape=jax.ShapeDtypeStruct((chunk.shape[0], given[0].shape[0], BLOCK), jnp.bfloat16),
        in_specs=[SMEM] * 2 + [VMEM] * len(given),
        out_specs=VMEM,
        compiler_params=ROOM,
        name="project",
    )(core, chunk, *given)


def moved(value, axis, steps):
    count = lax.axis_size(axis)
    return lax.ppermute(value, axis, [(i, (i + steps) % count) for i in range(count)])


def body(queries, keys, values, d_out, key_weight, value_weight, block_lists):
    f32, bf16 = jnp.float32, jnp.bfloat16
    half = lax.axis_index("xh")
    place = lax.axis_index(Z)
    core = lax.axis_index("core")
    depth = lax.axis_size(Z)
    enc_rows = keys.shape[0]
    enc_blocks = enc_rows // BLOCK

    near = jnp.concatenate([queries, d_out], axis=1)
    ahead = moved(near, Z, 4)
    behind = moved(near, Z, -4)
    across = moved(near, Z, 8)
    own = jnp.concatenate([keys, values], axis=1)
    far = moved(own, "xh", 1)

    places = (place + jnp.asarray(SLOTS, jnp.int32)) % depth
    listed = lax.dynamic_slice_in_dim(block_lists, half * depth, depth, 0)
    step = jnp.arange(enc_blocks, dtype=jnp.int32)
    ids = jnp.concatenate(
        [(half * depth + place) * enc_blocks + step, ((1 - half) * depth + place) * enc_blocks + step]
    )
    member = jnp.any(listed[:, :, None] == ids[None, None, :], axis=1).astype(jnp.int32).reshape(-1)

    bundle = jnp.concatenate([behind, near, ahead, across], axis=0)
    above2 = moved(bundle[: 2 * BLOCK], Z, -2)
    below2 = moved(bundle[BLOCK : 3 * BLOCK], Z, 2)
    below = moved(bundle, Z, 1)
    above = moved(bundle, Z, -1)

    early = forward(0, places, member, own, far, [bundle], None)
    pieces = [below, above, above2, below2]
    parts = forward(len(OWN), places, member, own, far, pieces, early)
    weights, parts = lax.optimization_barrier(
        (jnp.concatenate([key_weight, value_weight], axis=1), parts)
    )
    parts = lax.all_to_all(parts, Z, 0, 0, tiled=True)
    far_weights = moved(weights, "core", 1)
    parts, far_weights = lax.optimization_barrier((parts, far_weights))

    pieces = [bundle, *pieces]
    here = core[None]
    d_query, to_half = backward(enc_blocks, places, member, here, parts, far, pieces, None)
    from_half = moved(to_half, "xh", 1)
    d_query, kept, to_core = backward(0, places, member, here, parts, own, pieces, d_query)
    d_query, to_core, from_half = lax.optimization_barrier((d_query, to_core, from_half))
    d_query = lax.all_to_all(d_query, Z, 0, 0, tiled=True)
    to_core = to_core + lax.dynamic_slice_in_dim(from_half, (1 - core) * (enc_rows // 2), enc_rows // 2, 0).astype(f32)
    from_core = moved(to_core.astype(bf16), "core", 1)

    sides, runs, cores = (lax.axis_size(axis) for axis in HEAD)
    side = lax.axis_index("xl")
    run = (lax.axis_index("y") + jnp.arange(runs, dtype=jnp.int32)) % runs
    both = (core + jnp.arange(cores, dtype=jnp.int32)) % cores
    chunk = (run[:, None] * cores + both[None, :]).reshape(-1)
    given = (kept, from_half, from_core, key_weight, value_weight, far_weights)
    if sides > 1:
        sent = project(here, (1 - side) * runs * cores + chunk, *given)
        given += (moved(sent, "xl", 1),)
    memory = project(here, side * runs * cores + chunk, *given)
    memory = memory.reshape(runs, cores, *memory.shape[1:])
    total = memory[0].astype(f32)
    for away_by in sorted(range(1, runs), key=lambda d: -min(d, runs - d)):
        total = total + moved(memory[away_by], "y", away_by).astype(f32)
    total = total.astype(bf16)
    other = moved(total[1], "core", 1)
    first = core == 0
    d_memory = jnp.concatenate(
        [jnp.where(first, total[0], other), jnp.where(first, other, total[0])], axis=0
    )
    d_queries = jnp.sum(d_query.astype(f32), axis=0).astype(bf16)
    return d_queries, d_memory


def solution(mesh):
    fine = Mesh(mesh.devices.reshape(SIZES), AXES)
    placed = P(CTX, HEAD)
    return jax.shard_map(
        body,
        mesh=fine,
        in_specs=(placed, placed, placed, placed, P(None, HEAD), P(None, HEAD), P()),
        out_specs=(placed, placed),
        check_vma=False,
    )
```

```python
from functools import partial

import jax
import jax.numpy as jnp
from jax import lax
from jax.experimental import pallas as pl
from jax.experimental.pallas import tpu as pltpu
from jax.sharding import Mesh, PartitionSpec as P

HEAD_DIM = 64
BLOCK = 128
AXES = ("xh", "z", "xl", "y", "core")
SIZES = (2, 16, 2, 4, 2)
Z = "z"
CTX = ("xh", "z")
HEAD = ("xl", "y", "core")
BIG = 1e30

OWN = (4, 0, -4, 8)
LATER = (3, -1, -5, 7, 5, 1, -3, 9, 6, 2, -2, -6)
SLOTS = OWN + LATER

VMEM = pl.BlockSpec(memory_space=pltpu.VMEM)
SMEM = pl.BlockSpec(memory_space=pltpu.SMEM)
ROOM = pltpu.CompilerParams(vmem_limit_bytes=48 * 1024 * 1024)


def cost(flops, exps):
    return pl.CostEstimate(flops=4 * flops, bytes_accessed=1 << 20, transcendentals=exps)


def dot_nt(a, b):
    return lax.dot_general(a, b, (((1,), (1,)), ((), ())), preferred_element_type=jnp.float32)


def dot_nn(a, b):
    return lax.dot_general(a, b, (((1,), (0,)), ((), ())), preferred_element_type=jnp.float32)


def split_heads(rows):
    low = lax.broadcasted_iota(jnp.int32, rows.shape, 1) < HEAD_DIM
    zero = jnp.zeros_like(rows)
    return jnp.concatenate([jnp.where(low, rows, zero), jnp.where(low, zero, rows)], axis=0)


def load_keys(near_ref, far_ref, keys, vals):
    rows = near_ref.shape[0]
    keys[:rows, :] = near_ref[:, :BLOCK]
    vals[:rows, :] = near_ref[:, BLOCK:]
    keys[rows:, :] = far_ref[:, :BLOCK]
    vals[rows:, :] = far_ref[:, BLOCK:]


def load_targets(pieces, held):
    at = 0
    for piece in pieces:
        held[at : at + piece.shape[0], :] = piece[...]
        at += piece.shape[0]


def away(member, first, second, block, blocks):
    seg = (lax.broadcasted_iota(jnp.int32, (1, 4 * BLOCK), 1) // BLOCK) % 2
    one = jnp.where(member[first * blocks + block] > 0, 0.0, BIG)
    two = jnp.where(member[second * blocks + block] > 0, 0.0, BIG)
    return jnp.where(seg == 0, one, two)


def forward_kernel(base, places, member, near_ref, far_ref, *rest):
    *pieces, before, result, stats, keys, vals, held = rest
    load_keys(near_ref, far_ref, keys, vals)
    load_targets(pieces, held)
    blocks = keys.shape[0] // BLOCK
    pairs = held.shape[0] // (2 * BLOCK)
    half = stats.shape[0] // 2
    if before is not None:
        stats[...] = before[...]

    def step(p, carry):
        rows = pl.ds(pl.multiple_of(p * 2 * BLOCK, 2 * BLOCK), 2 * BLOCK)
        first, second = places[base + 2 * p], places[base + 2 * p + 1]
        query = split_heads(held[rows, :BLOCK])
        out = split_heads(held[rows, BLOCK:])
        logits = dot_nt(keys[...], query)
        prob = dot_nt(vals[...], out)
        off = [away(member, first, second, b, blocks) for b in range(blocks)]
        peak = jnp.full((1, 4 * BLOCK), -1e3, jnp.float32)
        for b in range(blocks):
            part = logits[b * BLOCK : (b + 1) * BLOCK]
            peak = jnp.maximum(peak, jnp.max(part, axis=0, keepdims=True) - off[b])
        total = jnp.zeros((1, 4 * BLOCK), jnp.float32)
        weighted = jnp.zeros((1, 4 * BLOCK), jnp.float32)
        for b in range(blocks):
            part = slice(b * BLOCK, (b + 1) * BLOCK)
            raised = jnp.exp(logits[part] - (peak + off[b]))
            total = total + jnp.sum(raised, axis=0, keepdims=True)
            weighted = weighted + jnp.sum(raised * prob[part], axis=0, keepdims=True)
        some = total > 0.0
        log_total = jnp.where(some, peak + jnp.log(jnp.where(some, total, 1.0)), -BIG)
        mean = jnp.where(some, weighted / jnp.where(some, total, 1.0), 0.0)
        for h in range(2):
            for s, place in enumerate((first, second)):
                lanes = slice((2 * h + s) * BLOCK, (2 * h + s + 1) * BLOCK)
                stats[pl.ds(2 * place + h, 1), :] = log_total[:, lanes]
                stats[pl.ds(half + 2 * place + h, 1), :] = mean[:, lanes]
        return carry

    def two(i, carry):
        return step(2 * i + 1, step(2 * i, carry))

    lax.fori_loop(0, pairs // 2, two, 0)
    if result is not None:
        high = stats[:half, :].astype(jnp.bfloat16)
        low = (stats[:half, :] - high.astype(jnp.float32)).astype(jnp.bfloat16)
        message = jnp.concatenate([high, low, stats[half:, :].astype(jnp.bfloat16)], axis=0)
        for peer in range(result.shape[0]):
            result[peer] = message


def forward(base, places, member, near, far, pieces, before):
    count = places.shape[0]
    rows = sum(p.shape[0] for p in pieces)
    enc = near.shape[0] + far.shape[0]
    given = [places, member, near, far, *pieces]
    specs = [SMEM, SMEM] + [VMEM] * (2 + len(pieces))
    local = jax.ShapeDtypeStruct((4 * count, BLOCK), jnp.float32)
    if before is None:
        shapes = [local]
        def kernel(*refs):
            ins, outs = refs[: len(given)], refs[len(given) :]
            forward_kernel(base, *ins, None, None, *outs)
    else:
        given.append(before)
        specs.append(VMEM)
        shapes = [jax.ShapeDtypeStruct((count, 6 * count, BLOCK), jnp.bfloat16), local]
        kernel = partial(forward_kernel, base)
    return pl.pallas_call(
        kernel,
        out_shape=shapes,
        in_specs=specs,
        out_specs=[VMEM] * len(shapes),
        scratch_shapes=[
            pltpu.VMEM((enc, BLOCK), jnp.bfloat16),
            pltpu.VMEM((enc, BLOCK), jnp.bfloat16),
            pltpu.VMEM((rows, 2 * BLOCK), jnp.bfloat16),
        ],
        compiler_params=ROOM,
        cost_estimate=cost(2 * rows * enc * 4 * BLOCK, rows * enc * 2),
        name="forward",
    )(*given)


def merge_stats(parts, stats):
    rows = stats.shape[0] // 2
    logs = [
        parts[i, :rows, :].astype(jnp.float32) + parts[i, rows : 2 * rows, :].astype(jnp.float32)
        for i in range(parts.shape[0])
    ]
    top = logs[0]
    for log in logs[1:]:
        top = jnp.maximum(top, log)
    total = jnp.zeros_like(top)
    mean = jnp.zeros_like(top)
    for i, log in enumerate(logs):
        weight = jnp.exp(log - top)
        total = total + weight
        mean = mean + weight * parts[i, 2 * rows :, :].astype(jnp.float32)
    stats[:rows, :] = top + jnp.log(total)
    stats[rows:, :] = mean / total


def lanes_of(stats, first, second, start):
    spots = [start + 2 * place + h for h in range(2) for place in (first, second)]
    return jnp.concatenate([stats[pl.ds(s, 1), :] for s in spots], axis=1)


def local_kernel(places, member, stats, near_ref, far_ref, *rest):
    pieces = rest[:5]
    sums, near_chance, near_slope, far_chance, far_slope, keys, vals, held, turned = rest[5:]
    p = pl.program_id(0)

    @pl.when(p == 0)
    def _():
        load_keys(near_ref, far_ref, keys, vals)
        load_targets(pieces, held)
        turned[...] = keys[...].T

    enc = keys.shape[0]
    blocks = enc // BLOCK
    half = stats.shape[0] // 2
    rows = pl.ds(pl.multiple_of(p * 2 * BLOCK, 2 * BLOCK), 2 * BLOCK)
    first, second = places[2 * p], places[2 * p + 1]
    log_total = lanes_of(stats, first, second, 0)
    log_total = jnp.where(log_total > -0.5 * BIG, log_total, BIG)
    mean = lanes_of(stats, first, second, half)
    logits = dot_nt(keys[...], split_heads(held[rows, :BLOCK]))
    prob = dot_nt(vals[...], split_heads(held[rows, BLOCK:]))
    for b in range(blocks):
        part = slice(b * BLOCK, (b + 1) * BLOCK)
        chance = jnp.exp(logits[part] - (log_total + away(member, first, second, b, blocks)))
        slope = chance * (prob[part] - mean)
        if b < blocks // 2:
            near_chance[0, part, :] = chance.astype(jnp.bfloat16)
            near_slope[0, part, :] = slope.astype(jnp.bfloat16)
        else:
            part = slice((b - blocks // 2) * BLOCK, (b - blocks // 2 + 1) * BLOCK)
            far_chance[0, part, :] = chance.astype(jnp.bfloat16)
            far_slope[0, part, :] = slope.astype(jnp.bfloat16)
    for i, (near, far) in enumerate(((near_slope, far_slope), (near_chance, far_chance))):
        for h in range(2):
            dims = slice(h * HEAD_DIM, (h + 1) * HEAD_DIM)
            lanes = slice(2 * h * BLOCK, 2 * (h + 1) * BLOCK)
            total = dot_nn(turned[dims, : enc // 2], near[0, :, lanes])
            sums[0, i, dims, :] = total + dot_nn(turned[dims, enc // 2 :], far[0, :, lanes])


def local(places, member, stats, near, far, pieces):
    rows = sum(p.shape[0] for p in pieces)
    enc = near.shape[0] + far.shape[0]
    pairs = rows // (2 * BLOCK)
    table = jax.ShapeDtypeStruct((pairs, enc // 2, 4 * BLOCK), jnp.bfloat16)
    given = [places, member, stats, near, far, *pieces]
    return pl.pallas_call(
        local_kernel,
        grid=(pairs,),
        out_shape=[jax.ShapeDtypeStruct((pairs, 2, BLOCK, 2 * BLOCK), jnp.float32)] + [table] * 4,
        in_specs=[SMEM] * 2 + [VMEM] * (len(given) - 2),
        out_specs=[pl.BlockSpec((1, 2, BLOCK, 2 * BLOCK), lambda p: (p, 0, 0, 0))]
        + [pl.BlockSpec((1, enc // 2, 4 * BLOCK), lambda p: (p, 0, 0))] * 4,
        scratch_shapes=[
            pltpu.VMEM((enc, BLOCK), jnp.bfloat16),
            pltpu.VMEM((enc, BLOCK), jnp.bfloat16),
            pltpu.VMEM((rows, 2 * BLOCK), jnp.bfloat16),
            pltpu.VMEM((BLOCK, enc), jnp.bfloat16),
        ],
        compiler_params=ROOM,
        cost_estimate=cost(3 * rows * enc * 4 * BLOCK, rows * enc * 2),
        name="local",
    )(*given)


def scale_kernel(places, parts, stats, sums, *rest):
    pieces = rest[:5]
    d_query, scaled, held, whole = rest[5:]
    merge_stats(parts, whole)
    load_targets(pieces, held)
    half = stats.shape[0] // 2
    pairs = held.shape[0] // (2 * BLOCK)

    def step(p, carry):
        rows = pl.ds(pl.multiple_of(p * 2 * BLOCK, 2 * BLOCK), 2 * BLOCK)
        first, second = places[2 * p], places[2 * p + 1]
        share = jnp.exp(lanes_of(stats, first, second, 0) - lanes_of(whole, first, second, 0))
        shift = lanes_of(whole, first, second, half) - lanes_of(stats, first, second, half)

        def by_dim(row):
            head = (HEAD_DIM, 2 * BLOCK)
            return jnp.concatenate(
                [jnp.broadcast_to(row[:, h * 2 * BLOCK : (h + 1) * 2 * BLOCK], head) for h in range(2)], axis=0
            )

        share, shift = by_dim(share), by_dim(shift)
        grad = (share * (sums[p, 0] - shift * sums[p, 1])).T.astype(jnp.bfloat16)
        d_query[first] = grad[:BLOCK]
        d_query[second] = grad[BLOCK:]
        share, shift = share.T, shift.T
        query = held[rows, :BLOCK].astype(jnp.float32) * share
        out = held[rows, BLOCK:].astype(jnp.float32) * share
        scaled[rows, :BLOCK] = out.astype(jnp.bfloat16)
        scaled[rows, BLOCK : 2 * BLOCK] = (-shift * query).astype(jnp.bfloat16)
        scaled[rows, 2 * BLOCK :] = query.astype(jnp.bfloat16)
        return carry

    lax.fori_loop(0, pairs, step, 0)


def scale(places, parts, stats, sums, pieces):
    count = places.shape[0]
    rows = sum(p.shape[0] for p in pieces)
    given = [places, parts, stats, sums, *pieces]
    return pl.pallas_call(
        scale_kernel,
        out_shape=[
            jax.ShapeDtypeStruct((count, BLOCK, BLOCK), jnp.bfloat16),
            jax.ShapeDtypeStruct((rows, 3 * BLOCK), jnp.bfloat16),
        ],
        in_specs=[SMEM] + [VMEM] * (len(given) - 1),
        out_specs=[VMEM] * 2,
        scratch_shapes=[
            pltpu.VMEM((rows, 2 * BLOCK), jnp.bfloat16),
            pltpu.VMEM((4 * count, BLOCK), jnp.float32),
        ],
        compiler_params=ROOM,
        cost_estimate=cost(1 << 27, 1 << 16),
        name="scale",
    )(*given)


def gather_kernel(core, scaled, chance, slope, *rest):
    *sent, d_key, d_value = rest
    p = pl.program_id(0)
    rows = pl.ds(pl.multiple_of(p * 2 * BLOCK, 2 * BLOCK), 2 * BLOCK)
    out, lack, query = (split_heads(scaled[rows, i * BLOCK : (i + 1) * BLOCK]) for i in range(3))
    both = dot_nn(chance[0], jnp.concatenate([out, lack], axis=1))
    value, key = both[:, :BLOCK], both[:, BLOCK:] + dot_nn(slope[0], query)

    @pl.when(p == 0)
    def _():
        d_value[...] = value
        d_key[...] = key

    @pl.when(p > 0)
    def _():
        d_value[...] += value
        d_key[...] += key

    @pl.when(p == pl.num_programs(0) - 1)
    def _():
        if len(sent) == 1:
            sent[0][:, :BLOCK] = d_key[...].astype(jnp.bfloat16)
            sent[0][:, BLOCK:] = d_value[...].astype(jnp.bfloat16)
        else:
            half = d_key.shape[0] // 2
            for target, part in zip(sent, (core[0], 1 - core[0]), strict=True):
                at = pl.ds(pl.multiple_of(part * half, half), half)
                target[:, :BLOCK] = d_key[at, :]
                target[:, BLOCK:] = d_value[at, :]


def gather(core, scaled, chance, slope, whole):
    pairs, enc, lanes = chance.shape
    if whole:
        sent = [jax.ShapeDtypeStruct((enc, 2 * BLOCK), jnp.bfloat16)]
    else:
        sent = [jax.ShapeDtypeStruct((enc // 2, 2 * BLOCK), jnp.float32)] * 2
    table = pl.BlockSpec((1, enc, lanes), lambda p: (p, 0, 0))
    return pl.pallas_call(
        gather_kernel,
        grid=(pairs,),
        out_shape=sent,
        in_specs=[SMEM, VMEM, table, table],
        out_specs=[VMEM] * len(sent),
        scratch_shapes=[pltpu.VMEM((enc, BLOCK), jnp.float32)] * 2,
        compiler_params=ROOM,
        cost_estimate=cost(3 * pairs * enc * lanes * BLOCK, 0),
        name="gather",
    )(core, scaled, chance, slope)


def project_kernel(core, chunk, kept, from_half, from_core, kw, vw, far_kw, far_vw, memory):
    rows = kept.shape[0]
    half = from_half[pl.ds(pl.multiple_of(core[0] * rows, rows), rows), :]
    mine = (kept[...] + half.astype(jnp.float32)).astype(jnp.bfloat16)
    other = from_core[...]
    for j in range(memory.shape[0]):
        part = pl.ds(pl.multiple_of(chunk[j] * BLOCK, BLOCK), BLOCK)
        total = dot_nt(mine[:, :BLOCK], kw[part, :]) + dot_nt(mine[:, BLOCK:], vw[part, :])
        total = total + dot_nt(other[:, :BLOCK], far_kw[part, :]) + dot_nt(other[:, BLOCK:], far_vw[part, :])
        memory[j] = total.astype(jnp.bfloat16)


def project(core, chunk, *given):
    return pl.pallas_call(
        project_kernel,
        out_shape=jax.ShapeDtypeStruct((chunk.shape[0], given[0].shape[0], BLOCK), jnp.bfloat16),
        in_specs=[SMEM] * 2 + [VMEM] * len(given),
        out_specs=VMEM,
        compiler_params=ROOM,
        name="project",
    )(core, chunk, *given)


def moved(value, axis, steps):
    count = lax.axis_size(axis)
    return lax.ppermute(value, axis, [(i, (i + steps) % count) for i in range(count)])


def body(queries, keys, values, d_out, key_weight, value_weight, block_lists):
    f32, bf16 = jnp.float32, jnp.bfloat16
    half = lax.axis_index("xh")
    place = lax.axis_index(Z)
    core = lax.axis_index("core")
    depth = lax.axis_size(Z)
    enc_rows = keys.shape[0]
    enc_blocks = enc_rows // BLOCK

    near = jnp.concatenate([queries, d_out], axis=1)
    ahead = moved(near, Z, 4)
    behind = moved(near, Z, -4)
    across = moved(near, Z, 8)
    own = jnp.concatenate([keys, values], axis=1)
    far = moved(own, "xh", 1)

    places = (place + jnp.asarray(SLOTS, jnp.int32)) % depth
    listed = lax.dynamic_slice_in_dim(block_lists, half * depth, depth, 0)
    step = jnp.arange(enc_blocks, dtype=jnp.int32)
    ids = jnp.concatenate(
        [(half * depth + place) * enc_blocks + step, ((1 - half) * depth + place) * enc_blocks + step]
    )
    member = jnp.any(listed[:, :, None] == ids[None, None, :], axis=1).astype(jnp.int32).reshape(-1)

    bundle = jnp.concatenate([behind, near, ahead, across], axis=0)
    above2 = moved(bundle[: 2 * BLOCK], Z, -2)
    below2 = moved(bundle[BLOCK : 3 * BLOCK], Z, 2)
    below = moved(bundle, Z, 1)
    above = moved(bundle, Z, -1)

    (early,) = forward(0, places, member, own, far, [bundle], None)
    pieces = [below, above, above2, below2]
    parts, stats = forward(len(OWN), places, member, own, far, pieces, early)
    pieces = [bundle, *pieces]
    key_weight, value_weight, parts, stats = lax.optimization_barrier((key_weight, value_weight, parts, stats))
    parts = lax.all_to_all(parts, Z, 0, 0, tiled=True)
    far_key_weight = moved(key_weight, "core", 1)
    far_value_weight = moved(value_weight, "core", 1)
    sums, *tables = local(places, member, stats, own, far, pieces)
    parts, sums, tables, far_key_weight, far_value_weight = lax.optimization_barrier(
        (parts, sums, tables, far_key_weight, far_value_weight)
    )

    here = core[None]
    d_query, scaled = scale(places, parts, stats, sums, pieces)
    (to_half,) = gather(here, scaled, tables[2], tables[3], True)
    from_half = moved(to_half, "xh", 1)
    kept, to_core = gather(here, scaled, tables[0], tables[1], False)
    d_query = lax.all_to_all(d_query, Z, 0, 0, tiled=True)
    to_core, from_half = lax.optimization_barrier((to_core, from_half))
    to_core = to_core + lax.dynamic_slice_in_dim(from_half, (1 - core) * (enc_rows // 2), enc_rows // 2, 0).astype(f32)
    from_core = moved(to_core.astype(bf16), "core", 1)

    cores = lax.axis_size("core")
    chunk = jnp.arange(key_weight.shape[0] // BLOCK, dtype=jnp.int32)
    weights = (key_weight, value_weight, far_key_weight, far_value_weight)
    memory = project(here, chunk, kept, from_half, from_core, *weights)
    memory, d_query = lax.optimization_barrier((memory, d_query))
    memory = lax.all_to_all(memory, HEAD, 0, 0, tiled=True)
    memory = memory.reshape(-1, cores, *memory.shape[1:]).astype(f32)
    d_memory = jnp.sum(memory, axis=0).reshape(keys.shape).astype(bf16)
    d_queries = jnp.sum(d_query.astype(f32), axis=0).astype(bf16)
    return d_queries, d_memory


def solution(mesh):
    fine = Mesh(mesh.devices.reshape(SIZES), AXES)
    placed = P(CTX, HEAD)
    return jax.shard_map(
        body,
        mesh=fine,
        in_specs=(placed, placed, placed, placed, P(None, HEAD), P(None, HEAD), P()),
        out_specs=(placed, placed),
        check_vma=False,
    )
```

```python
from functools import partial

import jax
import jax.numpy as jnp
from jax import lax
from jax.experimental import pallas as pl
from jax.experimental.pallas import tpu as pltpu
from jax.sharding import Mesh, PartitionSpec as P

HEAD_DIM = 64
BLOCK = 128
AXES = ("xh", "z", "xl", "y", "core")
SIZES = (2, 16, 2, 4, 2)
Z = "z"
CTX = ("xh", "z")
HEAD = ("xl", "y", "core")
BIG = 1e30

OWN = (4, 0, -4, 8)
LATER = (3, -1, -5, 7, 5, 1, -3, 9, 6, 2, -2, -6)
SLOTS = OWN + LATER

VMEM = pl.BlockSpec(memory_space=pltpu.VMEM)
ANY = pl.BlockSpec(memory_space=pl.ANY)
SMEM = pl.BlockSpec(memory_space=pltpu.SMEM)


def cost(flops, exps):
    return pl.CostEstimate(flops=4 * flops, bytes_accessed=1 << 20, transcendentals=exps)


def dot_nt(a, b):
    return lax.dot_general(a, b, (((1,), (1,)), ((), ())), preferred_element_type=jnp.float32)


def dot_nn(a, b):
    return lax.dot_general(a, b, (((1,), (0,)), ((), ())), preferred_element_type=jnp.float32)


def split_heads(rows):
    low = lax.broadcasted_iota(jnp.int32, rows.shape, 1) < HEAD_DIM
    zero = jnp.zeros_like(rows)
    return jnp.concatenate([jnp.where(low, rows, zero), jnp.where(low, zero, rows)], axis=0)


def room(mib):
    return pltpu.CompilerParams(vmem_limit_bytes=mib << 20)


def in_hbm(*arrays):
    return [pltpu.with_memory_space_constraint(x, pltpu.HBM) for x in arrays]


def fetch(pairs, sems):
    copies = [pltpu.make_async_copy(source, target, sems.at[i]) for i, (source, target) in enumerate(pairs)]
    for copy in copies:
        copy.start()
    return copies


def stacked(pieces, held):
    at, pairs = 0, []
    for piece in pieces:
        pairs.append((piece, held.at[pl.ds(at, piece.shape[0])]))
        at += piece.shape[0]
    return pairs


def join_kernel(left, right, out, sems):
    width = left.shape[1]
    for copy in fetch([(left, out.at[:, pl.ds(0, width)]), (right, out.at[:, pl.ds(width, width)])], sems):
        copy.wait()


def join(left, right):
    return pl.pallas_call(
        join_kernel,
        out_shape=jax.ShapeDtypeStruct((left.shape[0], 2 * left.shape[1]), left.dtype),
        in_specs=[ANY] * 2,
        out_specs=VMEM,
        scratch_shapes=[pltpu.SemaphoreType.DMA((2,))],
        compiler_params=room(4),
        name="join",
    )(*in_hbm(left, right))


def load_keys(near_ref, far_ref, keys, vals):
    rows = near_ref.shape[0]
    keys[:rows, :] = near_ref[:, :BLOCK]
    vals[:rows, :] = near_ref[:, BLOCK:]
    keys[rows:, :] = far_ref[:, :BLOCK]
    vals[rows:, :] = far_ref[:, BLOCK:]


def load_targets(pieces, held):
    at = 0
    for piece in pieces:
        held[at : at + piece.shape[0], :] = piece[...]
        at += piece.shape[0]


def away(member, first, second, block, blocks):
    seg = (lax.broadcasted_iota(jnp.int32, (1, 4 * BLOCK), 1) // BLOCK) % 2
    one = jnp.where(member[first * blocks + block] > 0, 0.0, BIG)
    two = jnp.where(member[second * blocks + block] > 0, 0.0, BIG)
    return jnp.where(seg == 0, one, two)


def forward_kernel(base, places, member, near_ref, far_ref, *rest):
    *pieces, before, result, stats, keys, vals, held = rest
    load_keys(near_ref, far_ref, keys, vals)
    load_targets(pieces, held)
    blocks = keys.shape[0] // BLOCK
    pairs = held.shape[0] // (2 * BLOCK)
    half = stats.shape[0] // 2
    if before is not None:
        stats[...] = before[...]

    def step(p, carry):
        rows = pl.ds(pl.multiple_of(p * 2 * BLOCK, 2 * BLOCK), 2 * BLOCK)
        first, second = places[base + 2 * p], places[base + 2 * p + 1]
        query = split_heads(held[rows, :BLOCK])
        out = split_heads(held[rows, BLOCK:])
        logits = dot_nt(keys[...], query)
        prob = dot_nt(vals[...], out)
        off = [away(member, first, second, b, blocks) for b in range(blocks)]
        peak = jnp.full((1, 4 * BLOCK), -1e3, jnp.float32)
        for b in range(blocks):
            part = logits[b * BLOCK : (b + 1) * BLOCK]
            peak = jnp.maximum(peak, jnp.max(part, axis=0, keepdims=True) - off[b])
        total = jnp.zeros((1, 4 * BLOCK), jnp.float32)
        weighted = jnp.zeros((1, 4 * BLOCK), jnp.float32)
        for b in range(blocks):
            part = slice(b * BLOCK, (b + 1) * BLOCK)
            raised = jnp.exp(logits[part] - (peak + off[b]))
            total = total + jnp.sum(raised, axis=0, keepdims=True)
            weighted = weighted + jnp.sum(raised * prob[part], axis=0, keepdims=True)
        some = total > 0.0
        log_total = jnp.where(some, peak + jnp.log(jnp.where(some, total, 1.0)), -BIG)
        mean = jnp.where(some, weighted / jnp.where(some, total, 1.0), 0.0)
        for h in range(2):
            for s, place in enumerate((first, second)):
                lanes = slice((2 * h + s) * BLOCK, (2 * h + s + 1) * BLOCK)
                stats[pl.ds(2 * place + h, 1), :] = log_total[:, lanes]
                stats[pl.ds(half + 2 * place + h, 1), :] = mean[:, lanes]
        return carry

    def two(i, carry):
        return step(2 * i + 1, step(2 * i, carry))

    lax.fori_loop(0, pairs // 2, two, 0)
    if result is not None:
        high = stats[:half, :].astype(jnp.bfloat16)
        low = (stats[:half, :] - high.astype(jnp.float32)).astype(jnp.bfloat16)
        message = jnp.concatenate([high, low, stats[half:, :].astype(jnp.bfloat16)], axis=0)
        for peer in range(result.shape[0]):
            result[peer] = message


def forward(base, places, member, near, far, pieces, before):
    count = places.shape[0]
    rows = sum(p.shape[0] for p in pieces)
    enc = near.shape[0] + far.shape[0]
    given = [places, member, near, far, *pieces]
    specs = [SMEM, SMEM] + [VMEM] * (2 + len(pieces))
    local = jax.ShapeDtypeStruct((4 * count, BLOCK), jnp.float32)
    if before is None:
        shapes = [local]
        def kernel(*refs):
            ins, outs = refs[: len(given)], refs[len(given) :]
            forward_kernel(base, *ins, None, None, *outs)
    else:
        given.append(before)
        specs.append(VMEM)
        shapes = [jax.ShapeDtypeStruct((count, 6 * count, BLOCK), jnp.bfloat16), local]
        kernel = partial(forward_kernel, base)
    return pl.pallas_call(
        kernel,
        out_shape=shapes,
        in_specs=specs,
        out_specs=[VMEM] * len(shapes),
        scratch_shapes=[
            pltpu.VMEM((enc, BLOCK), jnp.bfloat16),
            pltpu.VMEM((enc, BLOCK), jnp.bfloat16),
            pltpu.VMEM((rows, 2 * BLOCK), jnp.bfloat16),
        ],
        compiler_params=room(16),
        cost_estimate=cost(2 * rows * enc * 4 * BLOCK, rows * enc * 2),
        name="forward",
    )(*given)


def merge_stats(parts, stats):
    rows = stats.shape[0] // 2
    logs = [
        parts[i, :rows, :].astype(jnp.float32) + parts[i, rows : 2 * rows, :].astype(jnp.float32)
        for i in range(parts.shape[0])
    ]
    top = logs[0]
    for log in logs[1:]:
        top = jnp.maximum(top, log)
    total = jnp.zeros_like(top)
    mean = jnp.zeros_like(top)
    for i, log in enumerate(logs):
        weight = jnp.exp(log - top)
        total = total + weight
        mean = mean + weight * parts[i, 2 * rows :, :].astype(jnp.float32)
    stats[:rows, :] = top + jnp.log(total)
    stats[rows:, :] = mean / total


def lanes_of(stats, first, second, start):
    spots = [start + 2 * place + h for h in range(2) for place in (first, second)]
    return jnp.concatenate([stats[pl.ds(s, 1), :] for s in spots], axis=1)


def local_kernel(places, member, stats_ref, near_ref, far_ref, *rest):
    pieces = rest[:5]
    sums, near_chance, near_slope, far_chance, far_slope, kv, held, stats, turned, sems = rest[5:]
    p = pl.program_id(0)

    @pl.when(p == 0)
    def _():
        pairs = stacked((near_ref, far_ref), kv) + stacked(pieces, held) + [(stats_ref, stats)]
        for copy in fetch(pairs, sems):
            copy.wait()
        turned[...] = kv[:, :BLOCK].T

    enc = kv.shape[0]
    blocks = enc // BLOCK
    half = stats.shape[0] // 2
    rows = pl.ds(pl.multiple_of(p * 2 * BLOCK, 2 * BLOCK), 2 * BLOCK)
    first, second = places[2 * p], places[2 * p + 1]
    log_total = lanes_of(stats, first, second, 0)
    log_total = jnp.where(log_total > -0.5 * BIG, log_total, BIG)
    mean = lanes_of(stats, first, second, half)
    logits = dot_nt(kv[:, :BLOCK], split_heads(held[rows, :BLOCK]))
    prob = dot_nt(kv[:, BLOCK:], split_heads(held[rows, BLOCK:]))
    for b in range(blocks):
        part = slice(b * BLOCK, (b + 1) * BLOCK)
        chance = jnp.exp(logits[part] - (log_total + away(member, first, second, b, blocks)))
        slope = chance * (prob[part] - mean)
        if b < blocks // 2:
            near_chance[0, part, :] = chance.astype(jnp.bfloat16)
            near_slope[0, part, :] = slope.astype(jnp.bfloat16)
        else:
            part = slice((b - blocks // 2) * BLOCK, (b - blocks // 2 + 1) * BLOCK)
            far_chance[0, part, :] = chance.astype(jnp.bfloat16)
            far_slope[0, part, :] = slope.astype(jnp.bfloat16)
    for i, (near, far) in enumerate(((near_slope, far_slope), (near_chance, far_chance))):
        for h in range(2):
            dims = slice(h * HEAD_DIM, (h + 1) * HEAD_DIM)
            lanes = slice(2 * h * BLOCK, 2 * (h + 1) * BLOCK)
            total = dot_nn(turned[dims, : enc // 2], near[0, :, lanes])
            sums[0, i, dims, :] = total + dot_nn(turned[dims, enc // 2 :], far[0, :, lanes])


def local(places, member, stats, near, far, pieces):
    rows = sum(p.shape[0] for p in pieces)
    enc = near.shape[0] + far.shape[0]
    pairs = rows // (2 * BLOCK)
    table = pltpu.HBM((pairs, enc // 2, 4 * BLOCK), jnp.bfloat16)
    given = in_hbm(places, member, stats, near, far, *pieces)
    return pl.pallas_call(
        local_kernel,
        grid=(pairs,),
        out_shape=[pltpu.HBM((pairs, 2, BLOCK, 2 * BLOCK), jnp.float32)] + [table] * 4,
        in_specs=[SMEM] * 2 + [ANY] * (len(given) - 2),
        out_specs=[pl.BlockSpec((1, 2, BLOCK, 2 * BLOCK), lambda p: (p, 0, 0, 0))]
        + [pl.BlockSpec((1, enc // 2, 4 * BLOCK), lambda p: (p, 0, 0))] * 4,
        scratch_shapes=[
            pltpu.VMEM((enc, 2 * BLOCK), jnp.bfloat16),
            pltpu.VMEM((rows, 2 * BLOCK), jnp.bfloat16),
            pltpu.VMEM(stats.shape, stats.dtype),
            pltpu.VMEM((BLOCK, enc), jnp.bfloat16),
            pltpu.SemaphoreType.DMA((len(given) - 2,)),
        ],
        compiler_params=room(16),
        cost_estimate=cost(3 * rows * enc * 4 * BLOCK, rows * enc * 2),
        name="local",
    )(*given)


def scale_kernel(places, parts, stats_ref, sums_ref, *rest):
    pieces = rest[:5]
    d_query, scaled, held, whole, stats, sums, sems = rest[5:]
    copies = fetch(stacked(pieces, held) + [(stats_ref, stats), (sums_ref, sums)], sems)
    merge_stats(parts, whole)
    for copy in copies:
        copy.wait()
    half = stats.shape[0] // 2
    pairs = held.shape[0] // (2 * BLOCK)

    def step(p, carry):
        rows = pl.ds(pl.multiple_of(p * 2 * BLOCK, 2 * BLOCK), 2 * BLOCK)
        first, second = places[2 * p], places[2 * p + 1]
        share = jnp.exp(lanes_of(stats, first, second, 0) - lanes_of(whole, first, second, 0))
        shift = lanes_of(whole, first, second, half) - lanes_of(stats, first, second, half)

        def by_dim(row):
            head = (HEAD_DIM, 2 * BLOCK)
            return jnp.concatenate(
                [jnp.broadcast_to(row[:, h * 2 * BLOCK : (h + 1) * 2 * BLOCK], head) for h in range(2)], axis=0
            )

        share, shift = by_dim(share), by_dim(shift)
        grad = (share * (sums[p, 0] - shift * sums[p, 1])).T.astype(jnp.bfloat16)
        d_query[first] = grad[:BLOCK]
        d_query[second] = grad[BLOCK:]
        share, shift = share.T, shift.T
        query = held[rows, :BLOCK].astype(jnp.float32) * share
        out = held[rows, BLOCK:].astype(jnp.float32) * share
        scaled[rows, :BLOCK] = out.astype(jnp.bfloat16)
        scaled[rows, BLOCK : 2 * BLOCK] = (-shift * query).astype(jnp.bfloat16)
        scaled[rows, 2 * BLOCK :] = query.astype(jnp.bfloat16)
        return carry

    lax.fori_loop(0, pairs, step, 0)


def scale(places, parts, stats, sums, pieces):
    count = places.shape[0]
    rows = sum(p.shape[0] for p in pieces)
    given = [*in_hbm(places), parts, *in_hbm(stats, sums, *pieces)]
    return pl.pallas_call(
        scale_kernel,
        out_shape=[
            pltpu.HBM((count, BLOCK, BLOCK), jnp.bfloat16),
            pltpu.HBM((rows, 3 * BLOCK), jnp.bfloat16),
        ],
        in_specs=[SMEM, VMEM] + [ANY] * (len(given) - 2),
        out_specs=[VMEM] * 2,
        scratch_shapes=[
            pltpu.VMEM((rows, 2 * BLOCK), jnp.bfloat16),
            pltpu.VMEM((4 * count, BLOCK), jnp.float32),
            pltpu.VMEM(stats.shape, stats.dtype),
            pltpu.VMEM(sums.shape, sums.dtype),
            pltpu.SemaphoreType.DMA((len(given) - 2,)),
        ],
        compiler_params=room(16),
        cost_estimate=cost(1 << 27, 1 << 16),
        name="scale",
    )(*given)


def gather_kernel(core, scaled, chance, slope, *rest):
    *sent, d_key, d_value = rest
    p = pl.program_id(0)
    value = key = None
    for i in range(chance.shape[0]):
        rows = slice(2 * i * BLOCK, 2 * (i + 1) * BLOCK)
        out, lack, query = (split_heads(scaled[rows, j * BLOCK : (j + 1) * BLOCK]) for j in range(3))
        both = dot_nn(chance[i], jnp.concatenate([out, lack], axis=1))
        more, least = both[:, :BLOCK], both[:, BLOCK:] + dot_nn(slope[i], query)
        value, key = (more, least) if value is None else (value + more, key + least)

    @pl.when(p == 0)
    def _():
        d_value[...] = value
        d_key[...] = key

    @pl.when(p > 0)
    def _():
        d_value[...] += value
        d_key[...] += key

    @pl.when(p == pl.num_programs(0) - 1)
    def _():
        if len(sent) == 1:
            sent[0][:, :BLOCK] = d_key[...].astype(jnp.bfloat16)
            sent[0][:, BLOCK:] = d_value[...].astype(jnp.bfloat16)
        else:
            half = d_key.shape[0] // 2
            for target, part in zip(sent, (core[0], 1 - core[0]), strict=True):
                at = pl.ds(pl.multiple_of(part * half, half), half)
                target[:, :BLOCK] = d_key[at, :]
                target[:, BLOCK:] = d_value[at, :]


def gather(core, scaled, chance, slope, whole):
    pairs, enc, lanes = chance.shape
    if whole:
        sent = [jax.ShapeDtypeStruct((enc, 2 * BLOCK), jnp.bfloat16)]
    else:
        sent = [jax.ShapeDtypeStruct((enc // 2, 2 * BLOCK), jnp.float32)] * 2
    step = 2
    table = pl.BlockSpec((step, enc, lanes), lambda p: (p, 0, 0))
    given = in_hbm(scaled, chance, slope)
    return pl.pallas_call(
        gather_kernel,
        grid=(pairs // step,),
        out_shape=sent,
        in_specs=[SMEM, pl.BlockSpec((step * 2 * BLOCK, scaled.shape[1]), lambda p: (p, 0)), table, table],
        out_specs=[VMEM] * len(sent),
        scratch_shapes=[pltpu.VMEM((enc, BLOCK), jnp.float32)] * 2,
        compiler_params=room(16),
        cost_estimate=cost(3 * pairs * enc * lanes * BLOCK, 0),
        name="gather",
    )(core, *given)


def project_kernel(core, chunk, kept, from_half, from_core, kw, vw, far_kw, far_vw, memory):
    rows = kept.shape[0]
    half = from_half[pl.ds(pl.multiple_of(core[0] * rows, rows), rows), :]
    mine = (kept[...] + half.astype(jnp.float32)).astype(jnp.bfloat16)
    other = from_core[...]
    for j in range(memory.shape[0]):
        part = pl.ds(pl.multiple_of(chunk[j] * BLOCK, BLOCK), BLOCK)
        total = dot_nt(mine[:, :BLOCK], kw[part, :]) + dot_nt(mine[:, BLOCK:], vw[part, :])
        total = total + dot_nt(other[:, :BLOCK], far_kw[part, :]) + dot_nt(other[:, BLOCK:], far_vw[part, :])
        memory[j] = total.astype(jnp.bfloat16)


def project(core, chunk, *given):
    return pl.pallas_call(
        project_kernel,
        out_shape=jax.ShapeDtypeStruct((chunk.shape[0], given[0].shape[0], BLOCK), jnp.bfloat16),
        in_specs=[SMEM] * 2 + [VMEM] * len(given),
        out_specs=VMEM,
        compiler_params=room(8),
        name="project",
    )(core, chunk, *given)


def moved(value, axis, steps):
    count = lax.axis_size(axis)
    return lax.ppermute(value, axis, [(i, (i + steps) % count) for i in range(count)])


def body(queries, keys, values, d_out, key_weight, value_weight, block_lists):
    f32, bf16 = jnp.float32, jnp.bfloat16
    half = lax.axis_index("xh")
    place = lax.axis_index(Z)
    core = lax.axis_index("core")
    depth = lax.axis_size(Z)
    enc_rows = keys.shape[0]
    enc_blocks = enc_rows // BLOCK

    near = join(queries, d_out)
    ahead = moved(near, Z, 4)
    behind = moved(near, Z, -4)
    across = moved(near, Z, 8)
    own = join(keys, values)
    far = moved(own, "xh", 1)

    places = (place + jnp.asarray(SLOTS, jnp.int32)) % depth
    listed = lax.dynamic_slice_in_dim(block_lists, half * depth, depth, 0)
    step = jnp.arange(enc_blocks, dtype=jnp.int32)
    ids = jnp.concatenate(
        [(half * depth + place) * enc_blocks + step, ((1 - half) * depth + place) * enc_blocks + step]
    )
    member = jnp.any(listed[:, :, None] == ids[None, None, :], axis=1).astype(jnp.int32).reshape(-1)

    bundle = jnp.concatenate([behind, near, ahead, across], axis=0)
    above2 = moved(bundle[: 2 * BLOCK], Z, -2)
    below2 = moved(bundle[BLOCK : 3 * BLOCK], Z, 2)
    below = moved(bundle, Z, 1)
    above = moved(bundle, Z, -1)

    (early,) = forward(0, places, member, own, far, [bundle], None)
    pieces = [below, above, above2, below2]
    parts, stats = forward(len(OWN), places, member, own, far, pieces, early)
    pieces = [bundle, *pieces]
    key_weight, value_weight, parts, stats = lax.optimization_barrier((key_weight, value_weight, parts, stats))
    parts = lax.all_to_all(parts, Z, 0, 0, tiled=True)
    far_key_weight = moved(key_weight, "core", 1)
    far_value_weight = moved(value_weight, "core", 1)
    sums, *tables = local(places, member, stats, own, far, pieces)
    parts, sums, tables, far_key_weight, far_value_weight = lax.optimization_barrier(
        (parts, sums, tables, far_key_weight, far_value_weight)
    )

    here = core[None]
    d_query, scaled = scale(places, parts, stats, sums, pieces)
    (to_half,) = gather(here, scaled, tables[2], tables[3], True)
    from_half = moved(to_half, "xh", 1)
    kept, to_core = gather(here, scaled, tables[0], tables[1], False)
    d_query = lax.all_to_all(d_query, Z, 0, 0, tiled=True)
    to_core, from_half = lax.optimization_barrier((to_core, from_half))
    to_core = to_core + lax.dynamic_slice_in_dim(from_half, (1 - core) * (enc_rows // 2), enc_rows // 2, 0).astype(f32)
    from_core = moved(to_core.astype(bf16), "core", 1)

    cores = lax.axis_size("core")
    chunk = jnp.arange(key_weight.shape[0] // BLOCK, dtype=jnp.int32)
    weights = (key_weight, value_weight, far_key_weight, far_value_weight)
    memory = project(here, chunk, kept, from_half, from_core, *weights)
    memory, d_query = lax.optimization_barrier((memory, d_query))
    memory = lax.all_to_all(memory, HEAD, 0, 0, tiled=True)
    memory = memory.reshape(-1, cores, *memory.shape[1:]).astype(f32)
    d_memory = jnp.sum(memory, axis=0).reshape(keys.shape).astype(bf16)
    d_queries = jnp.sum(d_query.astype(f32), axis=0).astype(bf16)
    return d_queries, d_memory


def solution(mesh):
    fine = Mesh(mesh.devices.reshape(SIZES), AXES)
    placed = P(CTX, HEAD)
    return jax.shard_map(
        body,
        mesh=fine,
        in_specs=(placed, placed, placed, placed, P(None, HEAD), P(None, HEAD), P()),
        out_specs=(placed, placed),
        check_vma=False,
    )
```

```python
from functools import partial

import jax
import jax.numpy as jnp
from jax import lax
from jax.experimental import pallas as pl
from jax.experimental.pallas import tpu as pltpu
from jax.sharding import Mesh, PartitionSpec as P

HEAD_DIM = 64
BLOCK = 128
AXES = ("xh", "zh", "par", "xl", "y", "core")
SIZES = (2, 8, 2, 2, 4, 2)
Z = ("zh", "par")
CTX = ("xh", "zh", "par")
HEAD = ("xl", "y", "core")
BIG = 1e30

OWN = (2, 0, -2, 4)
LATER = (3, 1, -1, -3)
SLOTS = OWN + LATER

VMEM = pl.BlockSpec(memory_space=pltpu.VMEM)
ANY = pl.BlockSpec(memory_space=pl.ANY)
SMEM = pl.BlockSpec(memory_space=pltpu.SMEM)


def cost(flops, exps):
    return pl.CostEstimate(flops=4 * flops, bytes_accessed=1 << 20, transcendentals=exps)


def dot_nt(a, b):
    return lax.dot_general(a, b, (((1,), (1,)), ((), ())), preferred_element_type=jnp.float32)


def dot_nn(a, b):
    return lax.dot_general(a, b, (((1,), (0,)), ((), ())), preferred_element_type=jnp.float32)


def split_heads(rows):
    low = lax.broadcasted_iota(jnp.int32, rows.shape, 1) < HEAD_DIM
    zero = jnp.zeros_like(rows)
    return jnp.concatenate([jnp.where(low, rows, zero), jnp.where(low, zero, rows)], axis=0)


def room(mib):
    return pltpu.CompilerParams(vmem_limit_bytes=mib << 20)


def in_hbm(*arrays):
    return [pltpu.with_memory_space_constraint(x, pltpu.HBM) for x in arrays]


def fetch(pairs, sems):
    copies = [pltpu.make_async_copy(source, target, sems.at[i]) for i, (source, target) in enumerate(pairs)]
    for copy in copies:
        copy.start()
    return copies


def stacked(pieces, held):
    at, pairs = 0, []
    for piece in pieces:
        pairs.append((piece, held.at[pl.ds(at, piece.shape[0])]))
        at += piece.shape[0]
    return pairs


def join_kernel(left, right, out, sems):
    width = left.shape[1]
    for copy in fetch([(left, out.at[:, pl.ds(0, width)]), (right, out.at[:, pl.ds(width, width)])], sems):
        copy.wait()


def join(left, right):
    return pl.pallas_call(
        join_kernel,
        out_shape=jax.ShapeDtypeStruct((left.shape[0], 2 * left.shape[1]), left.dtype),
        in_specs=[ANY] * 2,
        out_specs=VMEM,
        scratch_shapes=[pltpu.SemaphoreType.DMA((2,))],
        compiler_params=room(4),
        name="join",
    )(*in_hbm(left, right))


def load_targets(pieces, held):
    at = 0
    for piece in pieces:
        held[at : at + piece.shape[0], :] = piece[...]
        at += piece.shape[0]


def away(member, first, second, block, blocks):
    seg = (lax.broadcasted_iota(jnp.int32, (1, 4 * BLOCK), 1) // BLOCK) % 2
    one = jnp.where(member[first * blocks + block] > 0, 0.0, BIG)
    two = jnp.where(member[second * blocks + block] > 0, 0.0, BIG)
    return jnp.where(seg == 0, one, two)


def part_stats(kv, query, out, member, first, second, base, blocks):
    logits = dot_nt(kv[:, :BLOCK], query)
    prob = dot_nt(kv[:, BLOCK:], out)
    here = kv.shape[0] // BLOCK
    off = [away(member, first, second, base + b, blocks) for b in range(here)]
    peak = jnp.full((1, 4 * BLOCK), -1e3, jnp.float32)
    for b in range(here):
        part = logits[b * BLOCK : (b + 1) * BLOCK]
        peak = jnp.maximum(peak, jnp.max(part, axis=0, keepdims=True) - off[b])
    total = jnp.zeros((1, 4 * BLOCK), jnp.float32)
    weighted = jnp.zeros((1, 4 * BLOCK), jnp.float32)
    for b in range(here):
        part = slice(b * BLOCK, (b + 1) * BLOCK)
        raised = jnp.exp(logits[part] - (peak + off[b]))
        total = total + jnp.sum(raised, axis=0, keepdims=True)
        weighted = weighted + jnp.sum(raised * prob[part], axis=0, keepdims=True)
    some = total > 0.0
    log_total = jnp.where(some, peak + jnp.log(jnp.where(some, total, 1.0)), -BIG)
    mean = jnp.where(some, weighted / jnp.where(some, total, 1.0), 0.0)
    return log_total, mean


def union(parts):
    top = parts[0][0]
    for log, _ in parts[1:]:
        top = jnp.maximum(top, log)
    total = jnp.zeros_like(top)
    mean = jnp.zeros_like(top)
    for log, part in parts:
        weight = jnp.exp(log - top)
        total = total + weight
        mean = mean + weight * part
    return top + jnp.log(total), mean / total


def forward_kernel(base, places, member, near_ref, far_ref, *rest):
    *pieces, before, result, stats, held = rest
    load_targets(pieces, held)
    blocks = (near_ref.shape[0] + far_ref.shape[0]) // BLOCK
    pairs = held.shape[0] // (2 * BLOCK)
    half = stats.shape[0] // 2
    if before is not None:
        stats[...] = before[...]

    def step(p, carry):
        rows = pl.ds(pl.multiple_of(p * 2 * BLOCK, 2 * BLOCK), 2 * BLOCK)
        first, second = places[base + 2 * p], places[base + 2 * p + 1]
        query = split_heads(held[rows, :BLOCK])
        out = split_heads(held[rows, BLOCK:])
        log_total, mean = union(
            [
                part_stats(near_ref, query, out, member, first, second, 0, blocks),
                part_stats(far_ref, query, out, member, first, second, blocks // 2, blocks),
            ]
        )
        for h in range(2):
            for s, place in enumerate((first, second)):
                lanes = slice((2 * h + s) * BLOCK, (2 * h + s + 1) * BLOCK)
                stats[pl.ds(2 * place + h, 1), :] = log_total[:, lanes]
                stats[pl.ds(half + 2 * place + h, 1), :] = mean[:, lanes]
        return carry

    lax.fori_loop(0, pairs, step, 0)
    if result is not None:
        high = stats[:half, :].astype(jnp.bfloat16)
        low = (stats[:half, :] - high.astype(jnp.float32)).astype(jnp.bfloat16)
        message = jnp.concatenate([high, low, stats[half:, :].astype(jnp.bfloat16)], axis=0)
        for peer in range(result.shape[0]):
            result[peer] = message


def forward(base, places, member, near, far, pieces, before):
    count = places.shape[0]
    rows = sum(p.shape[0] for p in pieces)
    enc = near.shape[0] + far.shape[0]
    given = [places, member, near, far, *pieces]
    local = jax.ShapeDtypeStruct((4 * count, BLOCK), jnp.float32)
    if before is None:
        shapes = [local]
        def kernel(*refs):
            ins, outs = refs[: len(given)], refs[len(given) :]
            forward_kernel(base, *ins, None, None, *outs)
    else:
        given.append(before)
        shapes = [jax.ShapeDtypeStruct((count, 6 * count, BLOCK), jnp.bfloat16), local]
        kernel = partial(forward_kernel, base)
    return pl.pallas_call(
        kernel,
        out_shape=shapes,
        in_specs=[SMEM] * 2 + [VMEM] * (len(given) - 2),
        out_specs=[VMEM] * len(shapes),
        scratch_shapes=[pltpu.VMEM((rows, 2 * BLOCK), jnp.bfloat16)],
        compiler_params=room(20),
        cost_estimate=cost(2 * rows * enc * 4 * BLOCK, rows * enc * 2),
        name="forward",
    )(*given)


def merge_stats(parts, stats):
    rows = stats.shape[0] // 2
    given = []
    for i in range(parts.shape[0]):
        part = parts[i].astype(jnp.float32)
        given.append((part[:rows] + part[rows : 2 * rows], part[2 * rows :]))
    stats[:rows, :], stats[rows:, :] = union(given)


def lanes_of(stats, first, second, start):
    spots = [start + 2 * place + h for h in range(2) for place in (first, second)]
    return jnp.concatenate([stats[pl.ds(s, 1), :] for s in spots], axis=1)


def local_kernel(places, member, stats_ref, near_ref, far_ref, *rest):
    pieces = rest[:3]
    sums, chances, slopes, kv, held, stats, turned, sems = rest[3:]
    side, p = pl.program_id(0), pl.program_id(1)
    enc = near_ref.shape[0]

    @pl.when((side == 0) & (p == 0))
    def _():
        pairs = [(near_ref, kv.at[0]), (far_ref, kv.at[1]), *stacked(pieces, held), (stats_ref, stats)]
        for copy in fetch(pairs, sems):
            copy.wait()

    @pl.when(p == 0)
    def _():
        turned[...] = kv[side, :, :BLOCK].T

    blocks = enc // BLOCK
    half = stats.shape[0] // 2
    rows = pl.ds(pl.multiple_of(p * 2 * BLOCK, 2 * BLOCK), 2 * BLOCK)
    first, second = places[2 * p], places[2 * p + 1]
    log_total = lanes_of(stats, first, second, 0)
    log_total = jnp.where(log_total > -0.5 * BIG, log_total, BIG)
    mean = lanes_of(stats, first, second, half)
    logits = dot_nt(kv[side, :, :BLOCK], split_heads(held[rows, :BLOCK]))
    prob = dot_nt(kv[side, :, BLOCK:], split_heads(held[rows, BLOCK:]))
    for b in range(blocks):
        part = slice(b * BLOCK, (b + 1) * BLOCK)
        off = away(member, first, second, side * blocks + b, 2 * blocks)
        chance = jnp.exp(logits[part] - (log_total + off))
        chances[0, part, :] = chance.astype(jnp.bfloat16)
        slopes[0, part, :] = (chance * (prob[part] - mean)).astype(jnp.bfloat16)
    for i, table in enumerate((slopes, chances)):
        for h in range(2):
            dims = slice(h * HEAD_DIM, (h + 1) * HEAD_DIM)
            lanes = slice(2 * h * BLOCK, 2 * (h + 1) * BLOCK)
            sums[0, i, dims, :] = dot_nn(turned[dims, :], table[0, :, lanes])


def local(places, member, stats, near, far, pieces):
    rows = sum(p.shape[0] for p in pieces)
    enc = near.shape[0]
    pairs = rows // (2 * BLOCK)
    table = pltpu.HBM((2 * pairs, enc, 4 * BLOCK), jnp.bfloat16)
    given = in_hbm(places, member, stats, near, far, *pieces)
    return pl.pallas_call(
        local_kernel,
        grid=(2, pairs),
        out_shape=[pltpu.HBM((2 * pairs, 2, BLOCK, 2 * BLOCK), jnp.float32)] + [table] * 2,
        in_specs=[SMEM] * 2 + [ANY] * (len(given) - 2),
        out_specs=[pl.BlockSpec((1, 2, BLOCK, 2 * BLOCK), lambda side, p: (side * pairs + p, 0, 0, 0))]
        + [pl.BlockSpec((1, enc, 4 * BLOCK), lambda side, p: (side * pairs + p, 0, 0))] * 2,
        scratch_shapes=[
            pltpu.VMEM((2, enc, 2 * BLOCK), jnp.bfloat16),
            pltpu.VMEM((rows, 2 * BLOCK), jnp.bfloat16),
            pltpu.VMEM(stats.shape, stats.dtype),
            pltpu.VMEM((BLOCK, enc), jnp.bfloat16),
            pltpu.SemaphoreType.DMA((len(given) - 2,)),
        ],
        compiler_params=room(20),
        cost_estimate=cost(3 * rows * 2 * enc * 4 * BLOCK, rows * enc * 4),
        name="local",
    )(*given)


def scale_kernel(places, parts, stats_ref, sums_ref, *rest):
    pieces = rest[:3]
    d_query, scaled, held, whole, stats, sums, sems = rest[3:]
    copies = fetch(stacked(pieces, held) + [(stats_ref, stats), (sums_ref, sums)], sems)
    merge_stats(parts, whole)
    for copy in copies:
        copy.wait()
    half = stats.shape[0] // 2
    pairs = held.shape[0] // (2 * BLOCK)

    def step(p, carry):
        rows = pl.ds(pl.multiple_of(p * 2 * BLOCK, 2 * BLOCK), 2 * BLOCK)
        first, second = places[2 * p], places[2 * p + 1]
        share = jnp.exp(lanes_of(stats, first, second, 0) - lanes_of(whole, first, second, 0))
        shift = lanes_of(whole, first, second, half) - lanes_of(stats, first, second, half)

        def by_dim(row):
            head = (HEAD_DIM, 2 * BLOCK)
            return jnp.concatenate(
                [jnp.broadcast_to(row[:, h * 2 * BLOCK : (h + 1) * 2 * BLOCK], head) for h in range(2)], axis=0
            )

        share, shift = by_dim(share), by_dim(shift)
        slope = sums[p, 0] + sums[pairs + p, 0]
        chance = sums[p, 1] + sums[pairs + p, 1]
        grad = (share * (slope - shift * chance)).T.astype(jnp.bfloat16)
        d_query[first] = grad[:BLOCK]
        d_query[second] = grad[BLOCK:]
        share, shift = share.T, shift.T
        query = held[rows, :BLOCK].astype(jnp.float32) * share
        out = held[rows, BLOCK:].astype(jnp.float32) * share
        scaled[rows, :BLOCK] = out.astype(jnp.bfloat16)
        scaled[rows, BLOCK : 2 * BLOCK] = (-shift * query).astype(jnp.bfloat16)
        scaled[rows, 2 * BLOCK :] = query.astype(jnp.bfloat16)
        return carry

    lax.fori_loop(0, pairs, step, 0)


def scale(places, parts, stats, sums, pieces):
    count = places.shape[0]
    rows = sum(p.shape[0] for p in pieces)
    given = [*in_hbm(places), parts, *in_hbm(stats, sums, *pieces)]
    return pl.pallas_call(
        scale_kernel,
        out_shape=[
            pltpu.HBM((count, BLOCK, BLOCK), jnp.bfloat16),
            pltpu.HBM((rows, 3 * BLOCK), jnp.bfloat16),
        ],
        in_specs=[SMEM, VMEM] + [ANY] * (len(given) - 2),
        out_specs=[VMEM] * 2,
        scratch_shapes=[
            pltpu.VMEM((rows, 2 * BLOCK), jnp.bfloat16),
            pltpu.VMEM((4 * count, BLOCK), jnp.float32),
            pltpu.VMEM(stats.shape, stats.dtype),
            pltpu.VMEM(sums.shape, sums.dtype),
            pltpu.SemaphoreType.DMA((len(given) - 2,)),
        ],
        compiler_params=room(16),
        cost_estimate=cost(1 << 27, 1 << 16),
        name="scale",
    )(*given)


def gather_kernel(scaled, chance, slope, sent, d_key, d_value):
    p = pl.program_id(0)
    value = key = None
    for i in range(chance.shape[0]):
        rows = slice(2 * i * BLOCK, 2 * (i + 1) * BLOCK)
        out, lack, query = (split_heads(scaled[rows, j * BLOCK : (j + 1) * BLOCK]) for j in range(3))
        both = dot_nn(chance[i], jnp.concatenate([out, lack], axis=1))
        more, least = both[:, :BLOCK], both[:, BLOCK:] + dot_nn(slope[i], query)
        value, key = (more, least) if value is None else (value + more, key + least)

    @pl.when(p == 0)
    def _():
        d_value[...] = value
        d_key[...] = key

    @pl.when(p > 0)
    def _():
        d_value[...] += value
        d_key[...] += key

    @pl.when(p == pl.num_programs(0) - 1)
    def _():
        sent[:, :BLOCK] = d_key[...].astype(sent.dtype)
        sent[:, BLOCK:] = d_value[...].astype(sent.dtype)


def gather(scaled, chance, slope, side, kind):
    pairs, enc, lanes = chance.shape
    pairs, step = pairs // 2, 2
    steps = pairs // step
    table = pl.BlockSpec((step, enc, lanes), lambda p: (side * steps + p, 0, 0))
    given = in_hbm(scaled, chance, slope)
    return pl.pallas_call(
        gather_kernel,
        grid=(steps,),
        out_shape=jax.ShapeDtypeStruct((enc, 2 * BLOCK), kind),
        in_specs=[pl.BlockSpec((step * 2 * BLOCK, scaled.shape[1]), lambda p: (p, 0)), table, table],
        out_specs=VMEM,
        scratch_shapes=[pltpu.VMEM((enc, BLOCK), jnp.float32)] * 2,
        compiler_params=room(20),
        cost_estimate=cost(3 * pairs * enc * lanes * BLOCK, 0),
        name="gather",
    )(*given)


def project_kernel(core, chunk, grads, from_core, kw, vw, far_kw, far_vw, memory):
    rows = from_core.shape[0]
    mine = grads[pl.ds(pl.multiple_of(core[0] * rows, rows), rows), :]
    other = from_core[...]
    for j in range(memory.shape[0]):
        part = pl.ds(pl.multiple_of(chunk[j] * BLOCK, BLOCK), BLOCK)
        total = dot_nt(mine[:, :BLOCK], kw[part, :]) + dot_nt(mine[:, BLOCK:], vw[part, :])
        total = total + dot_nt(other[:, :BLOCK], far_kw[part, :]) + dot_nt(other[:, BLOCK:], far_vw[part, :])
        memory[j] = total.astype(jnp.bfloat16)


def project(core, chunk, *given):
    return pl.pallas_call(
        project_kernel,
        out_shape=jax.ShapeDtypeStruct((chunk.shape[0], given[1].shape[0], BLOCK), jnp.bfloat16),
        in_specs=[SMEM] * 2 + [VMEM] * len(given),
        out_specs=VMEM,
        compiler_params=room(8),
        name="project",
    )(core, chunk, *given)


def moved(value, axis, steps):
    count = lax.axis_size(axis)
    return lax.ppermute(value, axis, [(i, (i + steps) % count) for i in range(count)])


def body(queries, keys, values, d_out, key_weight, value_weight, block_lists):
    f32, bf16 = jnp.float32, jnp.bfloat16
    half = lax.axis_index("xh")
    place = lax.axis_index("zh")
    parity = lax.axis_index("par")
    core = lax.axis_index("core")
    depth = lax.axis_size(Z)
    enc_rows = keys.shape[0]
    enc_blocks = enc_rows // BLOCK

    near = join(queries, d_out)
    own = join(keys, values)
    ahead = moved(near, Z, 4)
    behind = moved(near, Z, -4)
    across = moved(near, Z, 8)
    own = jnp.concatenate([own, moved(own, "xh", 1)], axis=0)
    far = moved(own, "par", 1)

    count = lax.axis_size("zh")
    places = (place + jnp.asarray(SLOTS, jnp.int32)) % count
    listed = lax.dynamic_slice_in_dim(block_lists, half * depth, depth, 0).reshape(count, depth // count, -1)
    listed = lax.dynamic_index_in_dim(listed, parity, 1, keepdims=False)
    step = jnp.arange(enc_blocks, dtype=jnp.int32)
    ids = jnp.concatenate(
        [((h * count + place) * 2 + p) * enc_blocks + step for p in (parity, 1 - parity) for h in (half, 1 - half)]
    )
    member = jnp.any(listed[:, :, None] == ids[None, None, :], axis=1).astype(jnp.int32).reshape(-1)

    bundle = jnp.concatenate([behind, near, ahead, across], axis=0)
    above = moved(bundle[: 2 * BLOCK], Z, -2)
    below = moved(bundle[BLOCK : 3 * BLOCK], Z, 2)

    (early,) = forward(0, places, member, own, far, [bundle], None)
    parts, stats = forward(len(OWN), places, member, own, far, [above, below], early)
    pieces = [bundle, above, below]
    parts = lax.all_to_all(parts, "zh", 0, 0, tiled=True)
    sums, chances, slopes = local(places, member, stats, own, far, pieces)
    parts, sums, chances, slopes = lax.optimization_barrier((parts, sums, chances, slopes))

    d_query, scaled = scale(places, parts, stats, sums, pieces)
    from_next = moved(gather(scaled, chances, slopes, 1, bf16), "par", 1)
    grads = gather(scaled, chances, slopes, 0, f32)
    d_query = lax.all_to_all(d_query, "zh", 0, 0, tiled=True)
    grads, from_next, key_weight, value_weight = lax.optimization_barrier(
        (grads, from_next, key_weight, value_weight)
    )
    far_key_weight = moved(key_weight, "core", 1)
    far_value_weight = moved(value_weight, "core", 1)
    from_half = moved((grads[enc_rows:] + from_next[enc_rows:].astype(f32)).astype(bf16), "xh", 1)
    grads = grads[:enc_rows] + from_next[:enc_rows].astype(f32) + from_half.astype(f32)
    grads = grads.astype(bf16)
    from_core = moved(lax.dynamic_slice_in_dim(grads, (1 - core) * (enc_rows // 2), enc_rows // 2, 0), "core", 1)

    cores = lax.axis_size("core")
    chunk = jnp.arange(key_weight.shape[0] // BLOCK, dtype=jnp.int32)
    weights = (key_weight, value_weight, far_key_weight, far_value_weight)
    memory = project(core[None], chunk, grads, from_core, *weights)
    memory, d_query = lax.optimization_barrier((memory, d_query))
    memory = lax.all_to_all(memory, HEAD, 0, 0, tiled=True)
    memory = memory.reshape(-1, cores, *memory.shape[1:]).astype(f32)
    d_memory = jnp.sum(memory, axis=0).reshape(keys.shape).astype(bf16)
    d_queries = jnp.sum(d_query.astype(f32), axis=0).astype(bf16)
    return d_queries, d_memory


def solution(mesh):
    fine = Mesh(mesh.devices.reshape(SIZES), AXES)
    placed = P(CTX, HEAD)
    return jax.shard_map(
        body,
        mesh=fine,
        in_specs=(placed, placed, placed, placed, P(None, HEAD), P(None, HEAD), P()),
        out_specs=(placed, placed),
        check_vma=False,
    )
```

```python
from functools import partial

import jax
import jax.numpy as jnp
from jax import lax
from jax.experimental import pallas as pl
from jax.experimental.pallas import tpu as pltpu
from jax.sharding import Mesh, PartitionSpec as P

HEAD_DIM = 64
BLOCK = 128
AXES = ("xh", "zh", "par", "xl", "y", "core")
SIZES = (2, 8, 2, 2, 4, 2)
Z = ("zh", "par")
CTX = ("xh", "zh", "par")
HEAD = ("xl", "y", "core")
BIG = 1e30

OWN = (2, 0, -2, 4)
LATER = (3, 1, -1, -3)
SLOTS = OWN + LATER

VMEM = pl.BlockSpec(memory_space=pltpu.VMEM)
ANY = pl.BlockSpec(memory_space=pl.ANY)
SMEM = pl.BlockSpec(memory_space=pltpu.SMEM)


def cost(flops, exps):
    return pl.CostEstimate(flops=4 * flops, bytes_accessed=1 << 20, transcendentals=exps)


def dot_nt(a, b):
    return lax.dot_general(a, b, (((1,), (1,)), ((), ())), preferred_element_type=jnp.float32)


def dot_nn(a, b):
    return lax.dot_general(a, b, (((1,), (0,)), ((), ())), preferred_element_type=jnp.float32)


def split_heads(rows):
    low = lax.broadcasted_iota(jnp.int32, rows.shape, 1) < HEAD_DIM
    zero = jnp.zeros_like(rows)
    return jnp.concatenate([jnp.where(low, rows, zero), jnp.where(low, zero, rows)], axis=0)


def room(mib):
    return pltpu.CompilerParams(vmem_limit_bytes=mib << 20)


def in_hbm(*arrays):
    return [pltpu.with_memory_space_constraint(x, pltpu.HBM) for x in arrays]


def fetch(pairs, sems):
    copies = [pltpu.make_async_copy(source, target, sems.at[i]) for i, (source, target) in enumerate(pairs)]
    for copy in copies:
        copy.start()
    return copies


def stacked(pieces, held):
    at, pairs = 0, []
    for piece in pieces:
        pairs.append((piece, held.at[pl.ds(at, piece.shape[0])]))
        at += piece.shape[0]
    return pairs


def join_kernel(left, right, out, sems):
    width = left.shape[1]
    for copy in fetch([(left, out.at[:, pl.ds(0, width)]), (right, out.at[:, pl.ds(width, width)])], sems):
        copy.wait()


def join(left, right):
    return pl.pallas_call(
        join_kernel,
        out_shape=jax.ShapeDtypeStruct((left.shape[0], 2 * left.shape[1]), left.dtype),
        in_specs=[ANY] * 2,
        out_specs=VMEM,
        scratch_shapes=[pltpu.SemaphoreType.DMA((2,))],
        compiler_params=room(4),
        name="join",
    )(*in_hbm(left, right))


def load_targets(pieces, held):
    at = 0
    for piece in pieces:
        held[at : at + piece.shape[0], :] = piece[...]
        at += piece.shape[0]


def away(member, first, second, block, blocks):
    seg = (lax.broadcasted_iota(jnp.int32, (1, 4 * BLOCK), 1) // BLOCK) % 2
    one = jnp.where(member[first * blocks + block] > 0, 0.0, BIG)
    two = jnp.where(member[second * blocks + block] > 0, 0.0, BIG)
    return jnp.where(seg == 0, one, two)


def part_stats(kv, query, out, member, first, second, base, blocks):
    logits = dot_nt(kv[:, :BLOCK], query)
    prob = dot_nt(kv[:, BLOCK:], out)
    here = kv.shape[0] // BLOCK
    off = [away(member, first, second, base + b, blocks) for b in range(here)]
    peak = jnp.full((1, 4 * BLOCK), -1e3, jnp.float32)
    for b in range(here):
        part = logits[b * BLOCK : (b + 1) * BLOCK]
        peak = jnp.maximum(peak, jnp.max(part, axis=0, keepdims=True) - off[b])
    total = jnp.zeros((1, 4 * BLOCK), jnp.float32)
    weighted = jnp.zeros((1, 4 * BLOCK), jnp.float32)
    for b in range(here):
        part = slice(b * BLOCK, (b + 1) * BLOCK)
        raised = jnp.exp(logits[part] - (peak + off[b]))
        total = total + jnp.sum(raised, axis=0, keepdims=True)
        weighted = weighted + jnp.sum(raised * prob[part], axis=0, keepdims=True)
    some = total > 0.0
    log_total = jnp.where(some, peak + jnp.log(jnp.where(some, total, 1.0)), -BIG)
    mean = jnp.where(some, weighted / jnp.where(some, total, 1.0), 0.0)
    return log_total, mean


def union(parts):
    top = parts[0][0]
    for log, _ in parts[1:]:
        top = jnp.maximum(top, log)
    total = jnp.zeros_like(top)
    mean = jnp.zeros_like(top)
    for log, part in parts:
        weight = jnp.exp(log - top)
        total = total + weight
        mean = mean + weight * part
    return top + jnp.log(total), mean / total


def forward_kernel(base, places, member, *rest):
    tables = rest[:4]
    *pieces, before, result, stats, held, kv = rest[4:]
    load_targets(pieces, held)
    load_targets(tables[:2], kv.at[0])
    load_targets(tables[2:], kv.at[1])
    blocks = 2 * kv.shape[1] // BLOCK
    pairs = held.shape[0] // (2 * BLOCK)
    half = stats.shape[0] // 2
    if before is not None:
        stats[...] = before[...]

    def step(p, carry):
        rows = pl.ds(pl.multiple_of(p * 2 * BLOCK, 2 * BLOCK), 2 * BLOCK)
        first, second = places[base + 2 * p], places[base + 2 * p + 1]
        query = split_heads(held[rows, :BLOCK])
        out = split_heads(held[rows, BLOCK:])
        log_total, mean = union(
            [
                part_stats(kv.at[0], query, out, member, first, second, 0, blocks),
                part_stats(kv.at[1], query, out, member, first, second, blocks // 2, blocks),
            ]
        )
        for h in range(2):
            for s, place in enumerate((first, second)):
                lanes = slice((2 * h + s) * BLOCK, (2 * h + s + 1) * BLOCK)
                stats[pl.ds(2 * place + h, 1), :] = log_total[:, lanes]
                stats[pl.ds(half + 2 * place + h, 1), :] = mean[:, lanes]
        return carry

    lax.fori_loop(0, pairs, step, 0)
    if result is not None:
        high = stats[:half, :].astype(jnp.bfloat16)
        low = (stats[:half, :] - high.astype(jnp.float32)).astype(jnp.bfloat16)
        message = jnp.concatenate([high, low, stats[half:, :].astype(jnp.bfloat16)], axis=0)
        for peer in range(result.shape[0]):
            result[peer] = message


def forward(base, places, member, tables, pieces, before):
    count = places.shape[0]
    rows = sum(p.shape[0] for p in pieces)
    enc = sum(t.shape[0] for t in tables)
    given = [places, member, *tables, *pieces]
    local = jax.ShapeDtypeStruct((4 * count, BLOCK), jnp.float32)
    if before is None:
        shapes = [local]
        def kernel(*refs):
            ins, outs = refs[: len(given)], refs[len(given) :]
            forward_kernel(base, *ins, None, None, *outs)
    else:
        given.append(before)
        shapes = [jax.ShapeDtypeStruct((count, 6 * count, BLOCK), jnp.bfloat16), local]
        kernel = partial(forward_kernel, base)
    return pl.pallas_call(
        kernel,
        out_shape=shapes,
        in_specs=[SMEM] * 2 + [VMEM] * (len(given) - 2),
        out_specs=[VMEM] * len(shapes),
        scratch_shapes=[
            pltpu.VMEM((rows, 2 * BLOCK), jnp.bfloat16),
            pltpu.VMEM((2, enc // 2, 2 * BLOCK), jnp.bfloat16),
        ],
        compiler_params=room(20),
        cost_estimate=cost(2 * rows * enc * 4 * BLOCK, rows * enc * 2),
        name="forward",
    )(*given)


def merge_stats(parts, stats):
    rows = stats.shape[0] // 2
    given = []
    for i in range(parts.shape[0]):
        part = parts[i].astype(jnp.float32)
        given.append((part[:rows] + part[rows : 2 * rows], part[2 * rows :]))
    stats[:rows, :], stats[rows:, :] = union(given)


def lanes_of(stats, first, second, start):
    spots = [start + 2 * place + h for h in range(2) for place in (first, second)]
    return jnp.concatenate([stats[pl.ds(s, 1), :] for s in spots], axis=1)


def local_kernel(places, member, stats_ref, *rest):
    tables, pieces = rest[:4], rest[4:7]
    sums, chances, slopes, kv, held, stats, turned, sems = rest[7:]
    side, p = pl.program_id(0), pl.program_id(1)
    enc = kv.shape[1]

    @pl.when((side == 0) & (p == 0))
    def _():
        pairs = stacked(tables[:2], kv.at[0]) + stacked(tables[2:], kv.at[1])
        pairs += stacked(pieces, held) + [(stats_ref, stats)]
        for copy in fetch(pairs, sems):
            copy.wait()

    @pl.when(p == 0)
    def _():
        turned[...] = kv[side, :, :BLOCK].T

    blocks = enc // BLOCK
    half = stats.shape[0] // 2
    rows = pl.ds(pl.multiple_of(p * 2 * BLOCK, 2 * BLOCK), 2 * BLOCK)
    first, second = places[2 * p], places[2 * p + 1]
    log_total = lanes_of(stats, first, second, 0)
    log_total = jnp.where(log_total > -0.5 * BIG, log_total, BIG)
    mean = lanes_of(stats, first, second, half)
    logits = dot_nt(kv[side, :, :BLOCK], split_heads(held[rows, :BLOCK]))
    prob = dot_nt(kv[side, :, BLOCK:], split_heads(held[rows, BLOCK:]))
    for b in range(blocks):
        part = slice(b * BLOCK, (b + 1) * BLOCK)
        off = away(member, first, second, side * blocks + b, 2 * blocks)
        chance = jnp.exp(logits[part] - (log_total + off))
        chances[0, part, :] = chance.astype(jnp.bfloat16)
        slopes[0, part, :] = (chance * (prob[part] - mean)).astype(jnp.bfloat16)
    for i, table in enumerate((slopes, chances)):
        for h in range(2):
            dims = slice(h * HEAD_DIM, (h + 1) * HEAD_DIM)
            lanes = slice(2 * h * BLOCK, 2 * (h + 1) * BLOCK)
            sums[0, i, dims, :] = dot_nn(turned[dims, :], table[0, :, lanes])


def local(places, member, stats, tables, pieces):
    rows = sum(p.shape[0] for p in pieces)
    enc = sum(t.shape[0] for t in tables) // 2
    pairs = rows // (2 * BLOCK)
    table = pltpu.HBM((2 * pairs, enc, 4 * BLOCK), jnp.bfloat16)
    given = in_hbm(places, member, stats, *tables, *pieces)
    return pl.pallas_call(
        local_kernel,
        grid=(2, pairs),
        out_shape=[pltpu.HBM((2 * pairs, 2, BLOCK, 2 * BLOCK), jnp.float32)] + [table] * 2,
        in_specs=[SMEM] * 2 + [ANY] * (len(given) - 2),
        out_specs=[pl.BlockSpec((1, 2, BLOCK, 2 * BLOCK), lambda side, p: (side * pairs + p, 0, 0, 0))]
        + [pl.BlockSpec((1, enc, 4 * BLOCK), lambda side, p: (side * pairs + p, 0, 0))] * 2,
        scratch_shapes=[
            pltpu.VMEM((2, enc, 2 * BLOCK), jnp.bfloat16),
            pltpu.VMEM((rows, 2 * BLOCK), jnp.bfloat16),
            pltpu.VMEM(stats.shape, stats.dtype),
            pltpu.VMEM((BLOCK, enc), jnp.bfloat16),
            pltpu.SemaphoreType.DMA((len(given) - 2,)),
        ],
        compiler_params=room(20),
        cost_estimate=cost(3 * rows * 2 * enc * 4 * BLOCK, rows * enc * 4),
        name="local",
    )(*given)


def scale_kernel(places, parts, stats_ref, sums_ref, *rest):
    pieces = rest[:3]
    d_query, scaled, held, whole, stats, sums, sems = rest[3:]
    copies = fetch(stacked(pieces, held) + [(stats_ref, stats), (sums_ref, sums)], sems)
    merge_stats(parts, whole)
    for copy in copies:
        copy.wait()
    half = stats.shape[0] // 2
    pairs = held.shape[0] // (2 * BLOCK)

    def step(p, carry):
        rows = pl.ds(pl.multiple_of(p * 2 * BLOCK, 2 * BLOCK), 2 * BLOCK)
        first, second = places[2 * p], places[2 * p + 1]
        share = jnp.exp(lanes_of(stats, first, second, 0) - lanes_of(whole, first, second, 0))
        shift = lanes_of(whole, first, second, half) - lanes_of(stats, first, second, half)

        def by_dim(row):
            head = (HEAD_DIM, 2 * BLOCK)
            return jnp.concatenate(
                [jnp.broadcast_to(row[:, h * 2 * BLOCK : (h + 1) * 2 * BLOCK], head) for h in range(2)], axis=0
            )

        share, shift = by_dim(share), by_dim(shift)
        slope = sums[p, 0] + sums[pairs + p, 0]
        chance = sums[p, 1] + sums[pairs + p, 1]
        grad = (share * (slope - shift * chance)).T.astype(jnp.bfloat16)
        d_query[first] = grad[:BLOCK]
        d_query[second] = grad[BLOCK:]
        share, shift = share.T, shift.T
        query = held[rows, :BLOCK].astype(jnp.float32) * share
        out = held[rows, BLOCK:].astype(jnp.float32) * share
        scaled[rows, :BLOCK] = out.astype(jnp.bfloat16)
        scaled[rows, BLOCK : 2 * BLOCK] = (-shift * query).astype(jnp.bfloat16)
        scaled[rows, 2 * BLOCK :] = query.astype(jnp.bfloat16)
        return carry

    lax.fori_loop(0, pairs, step, 0)


def scale(places, parts, stats, sums, pieces):
    count = places.shape[0]
    rows = sum(p.shape[0] for p in pieces)
    given = [*in_hbm(places), parts, *in_hbm(stats, sums, *pieces)]
    return pl.pallas_call(
        scale_kernel,
        out_shape=[
            pltpu.HBM((count, BLOCK, BLOCK), jnp.bfloat16),
            pltpu.HBM((rows, 3 * BLOCK), jnp.bfloat16),
        ],
        in_specs=[SMEM, VMEM] + [ANY] * (len(given) - 2),
        out_specs=[VMEM] * 2,
        scratch_shapes=[
            pltpu.VMEM((rows, 2 * BLOCK), jnp.bfloat16),
            pltpu.VMEM((4 * count, BLOCK), jnp.float32),
            pltpu.VMEM(stats.shape, stats.dtype),
            pltpu.VMEM(sums.shape, sums.dtype),
            pltpu.SemaphoreType.DMA((len(given) - 2,)),
        ],
        compiler_params=room(16),
        cost_estimate=cost(1 << 27, 1 << 16),
        name="scale",
    )(*given)


def gather_kernel(scaled, chance, slope, sent, d_key, d_value):
    p = pl.program_id(0)
    value = key = None
    for i in range(chance.shape[0]):
        rows = slice(2 * i * BLOCK, 2 * (i + 1) * BLOCK)
        out, lack, query = (split_heads(scaled[rows, j * BLOCK : (j + 1) * BLOCK]) for j in range(3))
        both = dot_nn(chance[i], jnp.concatenate([out, lack], axis=1))
        more, least = both[:, :BLOCK], both[:, BLOCK:] + dot_nn(slope[i], query)
        value, key = (more, least) if value is None else (value + more, key + least)

    @pl.when(p == 0)
    def _():
        d_value[...] = value
        d_key[...] = key

    @pl.when(p > 0)
    def _():
        d_value[...] += value
        d_key[...] += key

    @pl.when(p == pl.num_programs(0) - 1)
    def _():
        sent[:, :BLOCK] = d_key[...].astype(sent.dtype)
        sent[:, BLOCK:] = d_value[...].astype(sent.dtype)


def gather(scaled, chance, slope, side, kind):
    pairs, enc, lanes = chance.shape
    pairs, step = pairs // 2, 2
    steps = pairs // step
    table = pl.BlockSpec((step, enc, lanes), lambda p: (side * steps + p, 0, 0))
    given = in_hbm(scaled, chance, slope)
    return pl.pallas_call(
        gather_kernel,
        grid=(steps,),
        out_shape=jax.ShapeDtypeStruct((enc, 2 * BLOCK), kind),
        in_specs=[pl.BlockSpec((step * 2 * BLOCK, scaled.shape[1]), lambda p: (p, 0)), table, table],
        out_specs=VMEM,
        scratch_shapes=[pltpu.VMEM((enc, BLOCK), jnp.float32)] * 2,
        compiler_params=room(20),
        cost_estimate=cost(3 * pairs * enc * lanes * BLOCK, 0),
        name="gather",
    )(*given)


def project_kernel(core, chunk, grads, from_core, kw, vw, far_kw, far_vw, memory):
    rows = from_core.shape[0]
    mine = grads[pl.ds(pl.multiple_of(core[0] * rows, rows), rows), :]
    other = from_core[...]
    for j in range(memory.shape[0]):
        part = pl.ds(pl.multiple_of(chunk[j] * BLOCK, BLOCK), BLOCK)
        total = dot_nt(mine[:, :BLOCK], kw[part, :]) + dot_nt(mine[:, BLOCK:], vw[part, :])
        total = total + dot_nt(other[:, :BLOCK], far_kw[part, :]) + dot_nt(other[:, BLOCK:], far_vw[part, :])
        memory[j] = total.astype(jnp.bfloat16)


def project(core, chunk, *given):
    return pl.pallas_call(
        project_kernel,
        out_shape=jax.ShapeDtypeStruct((chunk.shape[0], given[1].shape[0], BLOCK), jnp.bfloat16),
        in_specs=[SMEM] * 2 + [VMEM] * len(given),
        out_specs=VMEM,
        compiler_params=room(8),
        name="project",
    )(core, chunk, *given)


def moved(value, axis, steps):
    count = lax.axis_size(axis)
    return lax.ppermute(value, axis, [(i, (i + steps) % count) for i in range(count)])


def body(queries, keys, values, d_out, key_weight, value_weight, block_lists):
    f32, bf16 = jnp.float32, jnp.bfloat16
    half = lax.axis_index("xh")
    place = lax.axis_index("zh")
    parity = lax.axis_index("par")
    core = lax.axis_index("core")
    depth = lax.axis_size(Z)
    enc_rows = keys.shape[0]
    enc_blocks = enc_rows // BLOCK

    near = join(queries, d_out)
    ahead = moved(near, Z, 4)
    behind = moved(near, Z, -4)
    across = moved(near, Z, 8)
    own = join(keys, values)
    late, ahead, behind = lax.optimization_barrier((own, ahead, behind))
    tables = [
        own,
        moved(own, "xh", 1),
        moved(own, "par", 1),
        lax.ppermute(late, ("xh", "par"), [(0, 3), (1, 2), (2, 1), (3, 0)]),
    ]

    count = lax.axis_size("zh")
    places = (place + jnp.asarray(SLOTS, jnp.int32)) % count
    listed = lax.dynamic_slice_in_dim(block_lists, half * depth, depth, 0).reshape(count, depth // count, -1)
    listed = lax.dynamic_index_in_dim(listed, parity, 1, keepdims=False)
    step = jnp.arange(enc_blocks, dtype=jnp.int32)
    ids = jnp.concatenate(
        [((h * count + place) * 2 + p) * enc_blocks + step for p in (parity, 1 - parity) for h in (half, 1 - half)]
    )
    member = jnp.any(listed[:, :, None] == ids[None, None, :], axis=1).astype(jnp.int32).reshape(-1)

    bundle = jnp.concatenate([behind, near, ahead, across], axis=0)
    above = moved(bundle[: 2 * BLOCK], Z, -2)
    below = moved(bundle[BLOCK : 3 * BLOCK], Z, 2)

    (early,) = forward(0, places, member, tables, [bundle], None)
    parts, stats = forward(len(OWN), places, member, tables, [above, below], early)
    pieces = [bundle, above, below]
    parts = lax.all_to_all(parts, "zh", 0, 0, tiled=True)
    sums, chances, slopes = local(places, member, stats, tables, pieces)
    parts, sums, chances, slopes = lax.optimization_barrier((parts, sums, chances, slopes))

    d_query, scaled = scale(places, parts, stats, sums, pieces)
    from_next = moved(gather(scaled, chances, slopes, 1, bf16), "par", 1)
    grads = gather(scaled, chances, slopes, 0, f32)
    d_query, grads = lax.optimization_barrier((d_query, grads))
    d_query = lax.all_to_all(d_query, "zh", 0, 0, tiled=True)
    grads, from_next, key_weight, value_weight = lax.optimization_barrier(
        (grads, from_next, key_weight, value_weight)
    )
    far_key_weight = moved(key_weight, "core", 1)
    far_value_weight = moved(value_weight, "core", 1)
    from_half = moved((grads[enc_rows:] + from_next[enc_rows:].astype(f32)).astype(bf16), "xh", 1)
    grads = grads[:enc_rows] + from_next[:enc_rows].astype(f32) + from_half.astype(f32)
    grads = grads.astype(bf16)
    from_core = moved(lax.dynamic_slice_in_dim(grads, (1 - core) * (enc_rows // 2), enc_rows // 2, 0), "core", 1)

    cores = lax.axis_size("core")
    chunk = jnp.arange(key_weight.shape[0] // BLOCK, dtype=jnp.int32)
    weights = (key_weight, value_weight, far_key_weight, far_value_weight)
    memory = project(core[None], chunk, grads, from_core, *weights)
    memory, d_query = lax.optimization_barrier((memory, d_query))
    memory = lax.all_to_all(memory, HEAD, 0, 0, tiled=True)
    memory = memory.reshape(-1, cores, *memory.shape[1:]).astype(f32)
    d_memory = jnp.sum(memory, axis=0).reshape(keys.shape).astype(bf16)
    d_queries = jnp.sum(d_query.astype(f32), axis=0).astype(bf16)
    return d_queries, d_memory


def solution(mesh):
    fine = Mesh(mesh.devices.reshape(SIZES), AXES)
    placed = P(CTX, HEAD)
    return jax.shard_map(
        body,
        mesh=fine,
        in_specs=(placed, placed, placed, placed, P(None, HEAD), P(None, HEAD), P()),
        out_specs=(placed, placed),
        check_vma=False,
    )
```

```python
from functools import partial

import jax
import jax.numpy as jnp
from jax import lax
from jax.experimental import pallas as pl
from jax.experimental.pallas import tpu as pltpu
from jax.sharding import Mesh, PartitionSpec as P

HEAD_DIM = 64
BLOCK = 128
AXES = ("xh", "z2", "z4", "par", "xl", "y", "core")
SIZES = (2, 2, 4, 2, 2, 4, 2)
ZH = ("z2", "z4")
Z = ("z2", "z4", "par")
CTX = ("xh", "z2", "z4", "par")
HEAD = ("xl", "y", "core")
BIG = 1e30

OWN = (2, 0, -2, 4)
LATER = (3, 1, -1, -3)
SLOTS = OWN + LATER

VMEM = pl.BlockSpec(memory_space=pltpu.VMEM)
ANY = pl.BlockSpec(memory_space=pl.ANY)
SMEM = pl.BlockSpec(memory_space=pltpu.SMEM)


def cost(flops, exps):
    return pl.CostEstimate(flops=4 * flops, bytes_accessed=1 << 20, transcendentals=exps)


def dot_nt(a, b):
    return lax.dot_general(a, b, (((1,), (1,)), ((), ())), preferred_element_type=jnp.float32)


def dot_nn(a, b):
    return lax.dot_general(a, b, (((1,), (0,)), ((), ())), preferred_element_type=jnp.float32)


def split_heads(rows):
    low = lax.broadcasted_iota(jnp.int32, rows.shape, 1) < HEAD_DIM
    zero = jnp.zeros_like(rows)
    return jnp.concatenate([jnp.where(low, rows, zero), jnp.where(low, zero, rows)], axis=0)


def room(mib):
    return pltpu.CompilerParams(vmem_limit_bytes=mib << 20)


def in_hbm(*arrays):
    return [pltpu.with_memory_space_constraint(x, pltpu.HBM) for x in arrays]


def fetch(pairs, sems):
    copies = [pltpu.make_async_copy(source, target, sems.at[i]) for i, (source, target) in enumerate(pairs)]
    for copy in copies:
        copy.start()
    return copies


def stacked(pieces, held):
    at, pairs = 0, []
    for piece in pieces:
        pairs.append((piece, held.at[pl.ds(at, piece.shape[0])]))
        at += piece.shape[0]
    return pairs


def join_kernel(left, right, out, sems):
    width = left.shape[1]
    for copy in fetch([(left, out.at[:, pl.ds(0, width)]), (right, out.at[:, pl.ds(width, width)])], sems):
        copy.wait()


def join(left, right):
    return pl.pallas_call(
        join_kernel,
        out_shape=jax.ShapeDtypeStruct((left.shape[0], 2 * left.shape[1]), left.dtype),
        in_specs=[ANY] * 2,
        out_specs=VMEM,
        scratch_shapes=[pltpu.SemaphoreType.DMA((2,))],
        compiler_params=room(4),
        name="join",
    )(*in_hbm(left, right))


def load_targets(pieces, held):
    at = 0
    for piece in pieces:
        held[at : at + piece.shape[0], :] = piece[...]
        at += piece.shape[0]


def away(member, first, second, block, blocks):
    seg = (lax.broadcasted_iota(jnp.int32, (1, 4 * BLOCK), 1) // BLOCK) % 2
    one = jnp.where(member[first * blocks + block] > 0, 0.0, BIG)
    two = jnp.where(member[second * blocks + block] > 0, 0.0, BIG)
    return jnp.where(seg == 0, one, two)


def part_stats(kv, query, out, member, first, second, base, blocks):
    logits = dot_nt(kv[:, :BLOCK], query)
    prob = dot_nt(kv[:, BLOCK:], out)
    here = kv.shape[0] // BLOCK
    off = [away(member, first, second, base + b, blocks) for b in range(here)]
    peak = jnp.full((1, 4 * BLOCK), -1e3, jnp.float32)
    for b in range(here):
        part = logits[b * BLOCK : (b + 1) * BLOCK]
        peak = jnp.maximum(peak, jnp.max(part, axis=0, keepdims=True) - off[b])
    total = jnp.zeros((1, 4 * BLOCK), jnp.float32)
    weighted = jnp.zeros((1, 4 * BLOCK), jnp.float32)
    for b in range(here):
        part = slice(b * BLOCK, (b + 1) * BLOCK)
        raised = jnp.exp(logits[part] - (peak + off[b]))
        total = total + jnp.sum(raised, axis=0, keepdims=True)
        weighted = weighted + jnp.sum(raised * prob[part], axis=0, keepdims=True)
    some = total > 0.0
    log_total = jnp.where(some, peak + jnp.log(jnp.where(some, total, 1.0)), -BIG)
    mean = jnp.where(some, weighted / jnp.where(some, total, 1.0), 0.0)
    return log_total, mean


def union(parts):
    top = parts[0][0]
    for log, _ in parts[1:]:
        top = jnp.maximum(top, log)
    total = jnp.zeros_like(top)
    mean = jnp.zeros_like(top)
    for log, part in parts:
        weight = jnp.exp(log - top)
        total = total + weight
        mean = mean + weight * part
    return top + jnp.log(total), mean / total


def store_stats(stats, first, second, given):
    half = stats.shape[0] // 2
    for start, row in zip((0, half), given, strict=True):
        for h in range(2):
            for s, place in enumerate((first, second)):
                stats[pl.ds(start + 2 * place + h, 1), :] = row[:, (2 * h + s) * BLOCK : (2 * h + s + 1) * BLOCK]


def early_kernel(places, member, near_ref, side_ref, piece, stats, kv):
    load_targets((near_ref, side_ref), kv)
    blocks = 2 * kv.shape[0] // BLOCK

    def step(p, carry):
        rows = pl.ds(pl.multiple_of(p * 2 * BLOCK, 2 * BLOCK), 2 * BLOCK)
        first, second = places[2 * p], places[2 * p + 1]
        query, out = split_heads(piece[rows, :BLOCK]), split_heads(piece[rows, BLOCK:])
        store_stats(stats, first, second, part_stats(kv, query, out, member, first, second, 0, blocks))
        return carry

    lax.fori_loop(0, piece.shape[0] // (2 * BLOCK), step, 0)


def forward_kernel(places, member, *rest):
    tables, pieces = rest[:4], rest[4:7]
    before, result, stats, held, kv = rest[7:]
    load_targets(pieces, held)
    load_targets(tables[:2], kv.at[0])
    load_targets(tables[2:], kv.at[1])
    blocks = 2 * kv.shape[1] // BLOCK
    pairs = held.shape[0] // (2 * BLOCK)
    known = pieces[0].shape[0] // (2 * BLOCK)
    half = stats.shape[0] // 2

    def step(p, done):
        rows = pl.ds(pl.multiple_of(p * 2 * BLOCK, 2 * BLOCK), 2 * BLOCK)
        first, second = places[2 * p], places[2 * p + 1]
        query, out = split_heads(held[rows, :BLOCK]), split_heads(held[rows, BLOCK:])
        if done:
            one = lanes_of(before, first, second, 0), lanes_of(before, first, second, half)
        else:
            one = part_stats(kv.at[0], query, out, member, first, second, 0, blocks)
        two = part_stats(kv.at[1], query, out, member, first, second, blocks // 2, blocks)
        store_stats(stats, first, second, union([one, two]))

    def step_known(p, carry):
        step(p, True)
        return carry

    def step_new(p, carry):
        step(p, False)
        return carry

    lax.fori_loop(0, known, step_known, 0)
    lax.fori_loop(known, pairs, step_new, 0)
    high = stats[:half, :].astype(jnp.bfloat16)
    low = (stats[:half, :] - high.astype(jnp.float32)).astype(jnp.bfloat16)
    message = jnp.concatenate([high, low, stats[half:, :].astype(jnp.bfloat16)], axis=0)
    for peer in range(result.shape[0]):
        result[peer] = message


def forward(places, member, tables, pieces, before):
    count = places.shape[0]
    rows = sum(p.shape[0] for p in pieces)
    enc = sum(t.shape[0] for t in tables)
    local = jax.ShapeDtypeStruct((4 * count, BLOCK), jnp.float32)
    if before is None:
        kernel, shapes = early_kernel, local
        scratch = [pltpu.VMEM((enc, 2 * BLOCK), jnp.bfloat16)]
        given = [places, member, *tables, *pieces]
    else:
        kernel, shapes = forward_kernel, [jax.ShapeDtypeStruct((count, 6 * count, BLOCK), jnp.bfloat16), local]
        scratch = [
            pltpu.VMEM((rows, 2 * BLOCK), jnp.bfloat16),
            pltpu.VMEM((2, enc // 2, 2 * BLOCK), jnp.bfloat16),
        ]
        given = [places, member, *tables, *pieces, before]
    return pl.pallas_call(
        kernel,
        out_shape=shapes,
        in_specs=[SMEM] * 2 + [VMEM] * (len(given) - 2),
        out_specs=VMEM if before is None else [VMEM] * 2,
        scratch_shapes=scratch,
        compiler_params=room(20),
        cost_estimate=cost(2 * rows * enc * 4 * BLOCK, rows * enc * 2),
        name="forward",
    )(*given)


def merge_stats(parts, stats):
    rows = stats.shape[0] // 2
    given = []
    for i in range(parts.shape[0]):
        part = parts[i].astype(jnp.float32)
        given.append((part[:rows] + part[rows : 2 * rows], part[2 * rows :]))
    stats[:rows, :], stats[rows:, :] = union(given)


def lanes_of(stats, first, second, start):
    spots = [start + 2 * place + h for h in range(2) for place in (first, second)]
    return jnp.concatenate([stats[pl.ds(s, 1), :] for s in spots], axis=1)


def local_kernel(places, member, stats_ref, *rest):
    tables, pieces = rest[:4], rest[4:7]
    sums, chances, slopes, kv, held, stats, turned, sems = rest[7:]
    side, p = pl.program_id(0), pl.program_id(1)
    enc = kv.shape[1]

    @pl.when((side == 0) & (p == 0))
    def _():
        pairs = stacked(tables[:2], kv.at[0]) + stacked(tables[2:], kv.at[1])
        pairs += stacked(pieces, held) + [(stats_ref, stats)]
        for copy in fetch(pairs, sems):
            copy.wait()

    @pl.when(p == 0)
    def _():
        turned[...] = kv[side, :, :BLOCK].T

    blocks = enc // BLOCK
    half = stats.shape[0] // 2
    rows = pl.ds(pl.multiple_of(p * 2 * BLOCK, 2 * BLOCK), 2 * BLOCK)
    first, second = places[2 * p], places[2 * p + 1]
    log_total = lanes_of(stats, first, second, 0)
    log_total = jnp.where(log_total > -0.5 * BIG, log_total, BIG)
    mean = lanes_of(stats, first, second, half)
    logits = dot_nt(kv[side, :, :BLOCK], split_heads(held[rows, :BLOCK]))
    prob = dot_nt(kv[side, :, BLOCK:], split_heads(held[rows, BLOCK:]))
    for b in range(blocks):
        part = slice(b * BLOCK, (b + 1) * BLOCK)
        off = away(member, first, second, side * blocks + b, 2 * blocks)
        chance = jnp.exp(logits[part] - (log_total + off))
        chances[0, part, :] = chance.astype(jnp.bfloat16)
        slopes[0, part, :] = (chance * (prob[part] - mean)).astype(jnp.bfloat16)
    for i, table in enumerate((slopes, chances)):
        for h in range(2):
            dims = slice(h * HEAD_DIM, (h + 1) * HEAD_DIM)
            lanes = slice(2 * h * BLOCK, 2 * (h + 1) * BLOCK)
            sums[0, i, dims, :] = dot_nn(turned[dims, :], table[0, :, lanes])


def local(places, member, stats, tables, pieces):
    rows = sum(p.shape[0] for p in pieces)
    enc = sum(t.shape[0] for t in tables) // 2
    pairs = rows // (2 * BLOCK)
    table = pltpu.HBM((2 * pairs, enc, 4 * BLOCK), jnp.bfloat16)
    given = in_hbm(places, member, stats, *tables, *pieces)
    return pl.pallas_call(
        local_kernel,
        grid=(2, pairs),
        out_shape=[pltpu.HBM((2 * pairs, 2, BLOCK, 2 * BLOCK), jnp.float32)] + [table] * 2,
        in_specs=[SMEM] * 2 + [ANY] * (len(given) - 2),
        out_specs=[pl.BlockSpec((1, 2, BLOCK, 2 * BLOCK), lambda side, p: (side * pairs + p, 0, 0, 0))]
        + [pl.BlockSpec((1, enc, 4 * BLOCK), lambda side, p: (side * pairs + p, 0, 0))] * 2,
        scratch_shapes=[
            pltpu.VMEM((2, enc, 2 * BLOCK), jnp.bfloat16),
            pltpu.VMEM((rows, 2 * BLOCK), jnp.bfloat16),
            pltpu.VMEM(stats.shape, stats.dtype),
            pltpu.VMEM((BLOCK, enc), jnp.bfloat16),
            pltpu.SemaphoreType.DMA((len(given) - 2,)),
        ],
        compiler_params=room(20),
        cost_estimate=cost(3 * rows * 2 * enc * 4 * BLOCK, rows * enc * 4),
        name="local",
    )(*given)


def scale_kernel(places, parts, stats_ref, sums_ref, *rest):
    pieces = rest[:3]
    d_query, scaled, held, whole, stats, sums, sems = rest[3:]
    copies = fetch(stacked(pieces, held) + [(stats_ref, stats), (sums_ref, sums)], sems)
    merge_stats(parts, whole)
    for copy in copies:
        copy.wait()
    half = stats.shape[0] // 2
    pairs = held.shape[0] // (2 * BLOCK)

    def step(p, carry):
        rows = pl.ds(pl.multiple_of(p * 2 * BLOCK, 2 * BLOCK), 2 * BLOCK)
        first, second = places[2 * p], places[2 * p + 1]
        share = jnp.exp(lanes_of(stats, first, second, 0) - lanes_of(whole, first, second, 0))
        shift = lanes_of(whole, first, second, half) - lanes_of(stats, first, second, half)

        def by_dim(row):
            head = (HEAD_DIM, 2 * BLOCK)
            return jnp.concatenate(
                [jnp.broadcast_to(row[:, h * 2 * BLOCK : (h + 1) * 2 * BLOCK], head) for h in range(2)], axis=0
            )

        share, shift = by_dim(share), by_dim(shift)
        slope = sums[p, 0] + sums[pairs + p, 0]
        chance = sums[p, 1] + sums[pairs + p, 1]
        grad = (share * (slope - shift * chance)).T
        far = d_query.shape[0] // 2
        for place, part in ((first, grad[:BLOCK]), (second, grad[BLOCK:])):
            d_query[2 * (place % far) + place // far] = part
        share, shift = share.T, shift.T
        query = held[rows, :BLOCK].astype(jnp.float32) * share
        out = held[rows, BLOCK:].astype(jnp.float32) * share
        scaled[rows, :BLOCK] = out.astype(jnp.bfloat16)
        scaled[rows, BLOCK : 2 * BLOCK] = (-shift * query).astype(jnp.bfloat16)
        scaled[rows, 2 * BLOCK :] = query.astype(jnp.bfloat16)
        return carry

    lax.fori_loop(0, pairs, step, 0)


def scale(places, parts, stats, sums, pieces):
    count = places.shape[0]
    rows = sum(p.shape[0] for p in pieces)
    given = [*in_hbm(places), parts, *in_hbm(stats, sums, *pieces)]
    return pl.pallas_call(
        scale_kernel,
        out_shape=[
            pltpu.HBM((count, BLOCK, BLOCK), jnp.float32),
            pltpu.HBM((rows, 3 * BLOCK), jnp.bfloat16),
        ],
        in_specs=[SMEM, VMEM] + [ANY] * (len(given) - 2),
        out_specs=[VMEM] * 2,
        scratch_shapes=[
            pltpu.VMEM((rows, 2 * BLOCK), jnp.bfloat16),
            pltpu.VMEM((4 * count, BLOCK), jnp.float32),
            pltpu.VMEM(stats.shape, stats.dtype),
            pltpu.VMEM(sums.shape, sums.dtype),
            pltpu.SemaphoreType.DMA((len(given) - 2,)),
        ],
        compiler_params=room(16),
        cost_estimate=cost(1 << 27, 1 << 16),
        name="scale",
    )(*given)


def gather_kernel(scaled, chance, slope, *rest):
    *sent, d_key, d_value = rest
    p = pl.program_id(0)
    value = key = None
    for i in range(chance.shape[0]):
        rows = slice(2 * i * BLOCK, 2 * (i + 1) * BLOCK)
        out, lack, query = (split_heads(scaled[rows, j * BLOCK : (j + 1) * BLOCK]) for j in range(3))
        both = dot_nn(chance[i], jnp.concatenate([out, lack], axis=1))
        more, least = both[:, :BLOCK], both[:, BLOCK:] + dot_nn(slope[i], query)
        value, key = (more, least) if value is None else (value + more, key + least)

    @pl.when(p == 0)
    def _():
        d_value[...] = value
        d_key[...] = key

    @pl.when(p > 0)
    def _():
        d_value[...] += value
        d_key[...] += key

    @pl.when(p == pl.num_programs(0) - 1)
    def _():
        half = d_key.shape[0] // 2
        for i, target in enumerate(sent):
            rows = slice(i * half, (i + 1) * half)
            target[:, :BLOCK] = d_key[rows, :].astype(target.dtype)
            target[:, BLOCK:] = d_value[rows, :].astype(target.dtype)


def gather(scaled, chance, slope, side, kind):
    pairs, enc, lanes = chance.shape
    pairs, step = pairs // 2, 2
    steps = pairs // step
    table = pl.BlockSpec((step, enc, lanes), lambda p: (side * steps + p, 0, 0))
    given = in_hbm(scaled, chance, slope)
    return pl.pallas_call(
        gather_kernel,
        grid=(steps,),
        out_shape=[jax.ShapeDtypeStruct((enc // 2, 2 * BLOCK), kind)] * 2,
        in_specs=[pl.BlockSpec((step * 2 * BLOCK, scaled.shape[1]), lambda p: (p, 0)), table, table],
        out_specs=[VMEM] * 2,
        scratch_shapes=[pltpu.VMEM((enc, BLOCK), jnp.float32)] * 2,
        compiler_params=room(20),
        cost_estimate=cost(3 * pairs * enc * lanes * BLOCK, 0),
        name="gather",
    )(*given)


def project_kernel(core, grads, from_core, kw, vw, far_kw, far_vw, memory):
    rows = from_core.shape[0]
    mine = grads[pl.ds(pl.multiple_of(core[0] * rows, rows), rows), :]
    other = from_core[...]
    for j in range(0, memory.shape[0], 2):
        part = slice(j * BLOCK, (j + 2) * BLOCK)
        total = dot_nt(mine[:, :BLOCK], kw[part, :]) + dot_nt(mine[:, BLOCK:], vw[part, :])
        total = total + dot_nt(other[:, :BLOCK], far_kw[part, :]) + dot_nt(other[:, BLOCK:], far_vw[part, :])
        memory[j] = total[:, :BLOCK].astype(jnp.bfloat16)
        memory[j + 1] = total[:, BLOCK:].astype(jnp.bfloat16)


def project(core, *given):
    return pl.pallas_call(
        project_kernel,
        out_shape=jax.ShapeDtypeStruct((given[2].shape[0] // BLOCK, given[1].shape[0], BLOCK), jnp.bfloat16),
        in_specs=[SMEM] + [VMEM] * len(given),
        out_specs=VMEM,
        compiler_params=room(8),
        name="project",
    )(core, *given)


def moved(value, axis, steps):
    count = lax.axis_size(axis)
    return lax.ppermute(value, axis, [(i, (i + steps) % count) for i in range(count)])


def body(queries, keys, values, d_out, key_weight, value_weight, block_lists):
    f32, bf16 = jnp.float32, jnp.bfloat16
    half = lax.axis_index("xh")
    place = lax.axis_index(ZH)
    parity = lax.axis_index("par")
    core = lax.axis_index("core")
    depth = lax.axis_size(Z)
    enc_rows = keys.shape[0]
    enc_blocks = enc_rows // BLOCK

    own = join(keys, values)
    side = moved(own, "xh", 1)
    next_ = moved(own, "par", 1)
    near, own = lax.optimization_barrier((join(queries, d_out), own))
    ahead = moved(near, Z, 4)
    behind = moved(near, Z, -4)
    across = moved(near, Z, 8)
    late, ahead, behind = lax.optimization_barrier((own, ahead, behind))
    tables = [own, side, next_, lax.ppermute(late, ("xh", "par"), [(0, 3), (1, 2), (2, 1), (3, 0)])]

    count = lax.axis_size(ZH)
    places = (place + jnp.asarray(SLOTS, jnp.int32)) % count
    listed = lax.dynamic_slice_in_dim(block_lists, half * depth, depth, 0).reshape(count, depth // count, -1)
    listed = lax.dynamic_index_in_dim(listed, parity, 1, keepdims=False)
    step = jnp.arange(enc_blocks, dtype=jnp.int32)
    ids = jnp.concatenate(
        [((h * count + place) * 2 + p) * enc_blocks + step for p in (parity, 1 - parity) for h in (half, 1 - half)]
    )
    member = jnp.any(listed[:, :, None] == ids[None, None, :], axis=1).astype(jnp.int32).reshape(-1)

    bundle = jnp.concatenate([behind, near, ahead, across], axis=0)
    above = moved(bundle[: 2 * BLOCK], Z, -2)
    below = moved(bundle[BLOCK : 3 * BLOCK], Z, 2)

    early = forward(places, member, tables[:2], [bundle], None)
    pieces = [bundle, above, below]
    parts, stats = forward(places, member, tables, pieces, early)
    parts = lax.all_to_all(parts, ZH, 0, 0, tiled=True)
    sums, chances, slopes = local(places, member, stats, tables, pieces)
    parts, sums, chances, slopes = lax.optimization_barrier((parts, sums, chances, slopes))

    d_query, scaled = scale(places, parts, stats, sums, pieces)
    d_query = lax.psum_scatter(d_query.reshape(-1, BLOCK), "z4", scatter_dimension=0, tiled=True)
    onward, next_ = (moved(part, "par", 1) for part in reversed(gather(scaled, chances, slopes, 1, bf16)))
    grads, side = gather(scaled, chances, slopes, 0, f32)
    side, onward = lax.optimization_barrier((side, onward))
    from_half = moved((side + onward.astype(f32)).astype(bf16), "xh", 1)
    grads, key_weight, value_weight = lax.optimization_barrier((grads, key_weight, value_weight))
    far_key_weight = moved(key_weight, "core", 1)
    far_value_weight = moved(value_weight, "core", 1)
    grads = (grads + next_.astype(f32) + from_half.astype(f32)).astype(bf16)
    from_core = moved(lax.dynamic_slice_in_dim(grads, (1 - core) * (enc_rows // 2), enc_rows // 2, 0), "core", 1)

    cores = lax.axis_size("core")
    weights = (key_weight, value_weight, far_key_weight, far_value_weight)
    from_core, d_query = lax.optimization_barrier((from_core, d_query))
    memory = project(core[None], grads, from_core, *weights)
    d_query = lax.psum_scatter(d_query, "z2", scatter_dimension=0, tiled=True)
    memory = lax.all_to_all(memory, HEAD, 0, 0, tiled=True)
    memory = memory.reshape(-1, cores, *memory.shape[1:]).astype(f32)
    d_memory = jnp.sum(memory, axis=0).reshape(keys.shape).astype(bf16)
    d_queries = d_query.astype(bf16)
    return d_queries, d_memory


def solution(mesh):
    fine = Mesh(mesh.devices.reshape(SIZES), AXES)
    placed = P(CTX, HEAD)
    return jax.shard_map(
        body,
        mesh=fine,
        in_specs=(placed, placed, placed, placed, P(None, HEAD), P(None, HEAD), P()),
        out_specs=(placed, placed),
        check_vma=False,
    )
```

```python
from functools import partial

import jax
import jax.numpy as jnp
from jax import lax
from jax.experimental import pallas as pl
from jax.experimental.pallas import tpu as pltpu
from jax.sharding import Mesh, PartitionSpec as P

HEAD_DIM = 64
BLOCK = 128
AXES = ("xh", "zh", "par", "xl", "y", "core")
SIZES = (2, 8, 2, 2, 4, 2)
ZH = "zh"
Z = ("zh", "par")
CTX = ("xh", "zh", "par")
HEAD = ("xl", "y", "core")
BIG = 1e30

OWN = (2, 0, -2, 4)
LATER = (3, 1, -1, -3)
SLOTS = OWN + LATER

VMEM = pl.BlockSpec(memory_space=pltpu.VMEM)
ANY = pl.BlockSpec(memory_space=pl.ANY)
SMEM = pl.BlockSpec(memory_space=pltpu.SMEM)


def cost(flops, exps):
    return pl.CostEstimate(flops=4 * flops, bytes_accessed=1 << 20, transcendentals=exps)


def dot_nt(a, b):
    return lax.dot_general(a, b, (((1,), (1,)), ((), ())), preferred_element_type=jnp.float32)


def dot_nn(a, b):
    return lax.dot_general(a, b, (((1,), (0,)), ((), ())), preferred_element_type=jnp.float32)


def split_heads(rows):
    low = lax.broadcasted_iota(jnp.int32, rows.shape, 1) < HEAD_DIM
    zero = jnp.zeros_like(rows)
    return jnp.concatenate([jnp.where(low, rows, zero), jnp.where(low, zero, rows)], axis=0)


def room(mib):
    return pltpu.CompilerParams(vmem_limit_bytes=mib << 20)


def in_hbm(*arrays):
    return [pltpu.with_memory_space_constraint(x, pltpu.HBM) for x in arrays]


def fetch(pairs, sems):
    copies = [pltpu.make_async_copy(source, target, sems.at[i]) for i, (source, target) in enumerate(pairs)]
    for copy in copies:
        copy.start()
    return copies


def stacked(pieces, held):
    at, pairs = 0, []
    for piece in pieces:
        pairs.append((piece, held.at[pl.ds(at, piece.shape[0])]))
        at += piece.shape[0]
    return pairs


def join_kernel(*refs):
    *given, first, second, sems = refs
    pairs = []
    for i, source in enumerate(given):
        width = source.shape[1]
        pairs.append((source, (first, second)[i // 2].at[:, pl.ds(i % 2 * width, width)]))
    for copy in fetch(pairs, sems):
        copy.wait()


def join(*given):
    return pl.pallas_call(
        join_kernel,
        out_shape=[jax.ShapeDtypeStruct((x.shape[0], 2 * x.shape[1]), x.dtype) for x in given[::2]],
        in_specs=[ANY] * 4,
        out_specs=[VMEM] * 2,
        scratch_shapes=[pltpu.SemaphoreType.DMA((4,))],
        compiler_params=room(4),
        name="join",
    )(*in_hbm(*given))


def pair_places(p):
    here, count = lax.axis_index("zh"), lax.axis_size("zh")
    found = []
    for steps in (SLOTS[::2], SLOTS[1::2]):
        step = jnp.int32(steps[-1])
        for i, other in enumerate(steps[:-1]):
            step = jnp.where(p == i, other, step)
        found.append(lax.rem(here + step + count, count))
    return found


def load_targets(pieces, held):
    at = 0
    for piece in pieces:
        held[at : at + piece.shape[0], :] = piece[...]
        at += piece.shape[0]


def away(member, first, second, block, blocks):
    seg = (lax.broadcasted_iota(jnp.int32, (1, 4 * BLOCK), 1) // BLOCK) % 2
    one = jnp.where(member[first * blocks + block] > 0, 0.0, BIG)
    two = jnp.where(member[second * blocks + block] > 0, 0.0, BIG)
    return jnp.where(seg == 0, one, two)


def part_stats(kv, query, out, member, first, second, base, blocks):
    logits = dot_nt(kv[:, :BLOCK], query)
    prob = dot_nt(kv[:, BLOCK:], out)
    here = kv.shape[0] // BLOCK
    off = [away(member, first, second, base + b, blocks) for b in range(here)]
    peak = jnp.full((1, 4 * BLOCK), -1e3, jnp.float32)
    for b in range(here):
        part = logits[b * BLOCK : (b + 1) * BLOCK]
        peak = jnp.maximum(peak, jnp.max(part, axis=0, keepdims=True) - off[b])
    total = jnp.zeros((1, 4 * BLOCK), jnp.float32)
    weighted = jnp.zeros((1, 4 * BLOCK), jnp.float32)
    for b in range(here):
        part = slice(b * BLOCK, (b + 1) * BLOCK)
        raised = jnp.exp(logits[part] - (peak + off[b]))
        total = total + jnp.sum(raised, axis=0, keepdims=True)
        weighted = weighted + jnp.sum(raised * prob[part], axis=0, keepdims=True)
    some = total > 0.0
    log_total = jnp.where(some, peak + jnp.log(jnp.where(some, total, 1.0)), -BIG)
    mean = jnp.where(some, weighted / jnp.where(some, total, 1.0), 0.0)
    return log_total, mean


def union(parts):
    top = parts[0][0]
    for log, _ in parts[1:]:
        top = jnp.maximum(top, log)
    total = jnp.zeros_like(top)
    mean = jnp.zeros_like(top)
    for log, part in parts:
        weight = jnp.exp(log - top)
        total = total + weight
        mean = mean + weight * part
    return top + jnp.log(total), mean / total


def store_stats(stats, first, second, given):
    half = stats.shape[0] // 2
    for start, row in zip((0, half), given, strict=True):
        for h in range(2):
            for s, place in enumerate((first, second)):
                stats[pl.ds(start + 2 * place + h, 1), :] = row[:, (2 * h + s) * BLOCK : (2 * h + s + 1) * BLOCK]


def early_kernel(member, near_ref, side_ref, piece, stats, kv):
    load_targets((near_ref, side_ref), kv)
    blocks = 2 * kv.shape[0] // BLOCK

    def step(p, carry):
        rows = pl.ds(pl.multiple_of(p * 2 * BLOCK, 2 * BLOCK), 2 * BLOCK)
        first, second = pair_places(p)
        query, out = split_heads(piece[rows, :BLOCK]), split_heads(piece[rows, BLOCK:])
        store_stats(stats, first, second, part_stats(kv, query, out, member, first, second, 0, blocks))
        return carry

    lax.fori_loop(0, piece.shape[0] // (2 * BLOCK), step, 0)


def forward_kernel(member, *rest):
    tables, pieces = rest[:4], rest[4:7]
    before, result, stats, held, kv = rest[7:]
    load_targets(pieces, held)
    load_targets(tables[:2], kv.at[0])
    load_targets(tables[2:], kv.at[1])
    blocks = 2 * kv.shape[1] // BLOCK
    pairs = held.shape[0] // (2 * BLOCK)
    known = pieces[0].shape[0] // (2 * BLOCK)
    half = stats.shape[0] // 2

    def step(p, done):
        rows = pl.ds(pl.multiple_of(p * 2 * BLOCK, 2 * BLOCK), 2 * BLOCK)
        first, second = pair_places(p)
        query, out = split_heads(held[rows, :BLOCK]), split_heads(held[rows, BLOCK:])
        if done:
            one = lanes_of(before, first, second, 0), lanes_of(before, first, second, half)
        else:
            one = part_stats(kv.at[0], query, out, member, first, second, 0, blocks)
        two = part_stats(kv.at[1], query, out, member, first, second, blocks // 2, blocks)
        store_stats(stats, first, second, union([one, two]))

    def step_known(p, carry):
        step(p, True)
        return carry

    def step_new(p, carry):
        step(p, False)
        return carry

    lax.fori_loop(0, known, step_known, 0)
    lax.fori_loop(known, pairs, step_new, 0)
    high = stats[:half, :].astype(jnp.bfloat16)
    low = (stats[:half, :] - high.astype(jnp.float32)).astype(jnp.bfloat16)
    message = jnp.concatenate([high, low, stats[half:, :].astype(jnp.bfloat16)], axis=0)
    for peer in range(result.shape[0]):
        result[peer] = message


def forward(member, tables, pieces, before):
    count = len(SLOTS)
    rows = sum(p.shape[0] for p in pieces)
    enc = sum(t.shape[0] for t in tables)
    local = jax.ShapeDtypeStruct((4 * count, BLOCK), jnp.float32)
    if before is None:
        kernel, shapes = early_kernel, local
        scratch = [pltpu.VMEM((enc, 2 * BLOCK), jnp.bfloat16)]
        given = [member, *tables, *pieces]
    else:
        kernel, shapes = forward_kernel, [jax.ShapeDtypeStruct((count, 6 * count, BLOCK), jnp.bfloat16), local]
        scratch = [
            pltpu.VMEM((rows, 2 * BLOCK), jnp.bfloat16),
            pltpu.VMEM((2, enc // 2, 2 * BLOCK), jnp.bfloat16),
        ]
        given = [member, *tables, *pieces, before]
    return pl.pallas_call(
        kernel,
        out_shape=shapes,
        in_specs=[SMEM] + [VMEM] * (len(given) - 1),
        out_specs=VMEM if before is None else [VMEM] * 2,
        scratch_shapes=scratch,
        compiler_params=room(20),
        cost_estimate=cost(2 * rows * enc * 4 * BLOCK, rows * enc * 2),
        name="forward",
    )(*given)


def merge_stats(parts, stats):
    rows = stats.shape[0] // 2
    given = []
    for i in range(parts.shape[0]):
        part = parts[i].astype(jnp.float32)
        given.append((part[:rows] + part[rows : 2 * rows], part[2 * rows :]))
    stats[:rows, :], stats[rows:, :] = union(given)


def lanes_of(stats, first, second, start):
    spots = [start + 2 * place + h for h in range(2) for place in (first, second)]
    return jnp.concatenate([stats[pl.ds(s, 1), :] for s in spots], axis=1)


def local_kernel(member, stats_ref, *rest):
    tables, pieces = rest[:4], rest[4:7]
    sums, chances, slopes, kv, held, stats, turned, sems = rest[7:]
    side, p = pl.program_id(0), pl.program_id(1)
    enc = kv.shape[1]

    @pl.when((side == 0) & (p == 0))
    def _():
        pairs = stacked(tables[:2], kv.at[0]) + stacked(tables[2:], kv.at[1])
        pairs += stacked(pieces, held) + [(stats_ref, stats)]
        for copy in fetch(pairs, sems):
            copy.wait()

    @pl.when(p == 0)
    def _():
        turned[...] = kv[side, :, :BLOCK].T

    blocks = enc // BLOCK
    half = stats.shape[0] // 2
    rows = pl.ds(pl.multiple_of(p * 2 * BLOCK, 2 * BLOCK), 2 * BLOCK)
    first, second = pair_places(p)
    log_total = lanes_of(stats, first, second, 0)
    log_total = jnp.where(log_total > -0.5 * BIG, log_total, BIG)
    mean = lanes_of(stats, first, second, half)
    logits = dot_nt(kv[side, :, :BLOCK], split_heads(held[rows, :BLOCK]))
    prob = dot_nt(kv[side, :, BLOCK:], split_heads(held[rows, BLOCK:]))
    for b in range(blocks):
        part = slice(b * BLOCK, (b + 1) * BLOCK)
        off = away(member, first, second, side * blocks + b, 2 * blocks)
        chance = jnp.exp(logits[part] - (log_total + off))
        chances[0, part, :] = chance.astype(jnp.bfloat16)
        slopes[0, part, :] = (chance * (prob[part] - mean)).astype(jnp.bfloat16)
    for i, table in enumerate((slopes, chances)):
        for h in range(2):
            dims = slice(h * HEAD_DIM, (h + 1) * HEAD_DIM)
            lanes = slice(2 * h * BLOCK, 2 * (h + 1) * BLOCK)
            sums[0, i, dims, :] = dot_nn(turned[dims, :], table[0, :, lanes])


def local(member, stats, tables, pieces):
    rows = sum(p.shape[0] for p in pieces)
    enc = sum(t.shape[0] for t in tables) // 2
    pairs = rows // (2 * BLOCK)
    table = pltpu.HBM((2 * pairs, enc, 4 * BLOCK), jnp.bfloat16)
    given = in_hbm(member, stats, *tables, *pieces)
    return pl.pallas_call(
        local_kernel,
        grid=(2, pairs),
        out_shape=[pltpu.HBM((2 * pairs, 2, BLOCK, 2 * BLOCK), jnp.float32)] + [table] * 2,
        in_specs=[SMEM] + [ANY] * (len(given) - 1),
        out_specs=[pl.BlockSpec((1, 2, BLOCK, 2 * BLOCK), lambda side, p: (side * pairs + p, 0, 0, 0))]
        + [pl.BlockSpec((1, enc, 4 * BLOCK), lambda side, p: (side * pairs + p, 0, 0))] * 2,
        scratch_shapes=[
            pltpu.VMEM((2, enc, 2 * BLOCK), jnp.bfloat16),
            pltpu.VMEM((rows, 2 * BLOCK), jnp.bfloat16),
            pltpu.VMEM(stats.shape, stats.dtype),
            pltpu.VMEM((BLOCK, enc), jnp.bfloat16),
            pltpu.SemaphoreType.DMA((len(given) - 1,)),
        ],
        compiler_params=room(20),
        cost_estimate=cost(3 * rows * 2 * enc * 4 * BLOCK, rows * enc * 4),
        name="local",
    )(*given)


def scale_kernel(parts, stats_ref, sums_ref, *rest):
    pieces = rest[:3]
    d_query, scaled, held, whole, stats, sums, sems = rest[3:]
    copies = fetch(stacked(pieces, held) + [(stats_ref, stats), (sums_ref, sums)], sems)
    merge_stats(parts, whole)
    for copy in copies:
        copy.wait()
    half = stats.shape[0] // 2
    pairs = held.shape[0] // (2 * BLOCK)

    def step(p, carry):
        rows = pl.ds(pl.multiple_of(p * 2 * BLOCK, 2 * BLOCK), 2 * BLOCK)
        first, second = pair_places(p)
        share = jnp.exp(lanes_of(stats, first, second, 0) - lanes_of(whole, first, second, 0))
        shift = lanes_of(whole, first, second, half) - lanes_of(stats, first, second, half)

        def by_dim(row):
            head = (HEAD_DIM, 2 * BLOCK)
            return jnp.concatenate(
                [jnp.broadcast_to(row[:, h * 2 * BLOCK : (h + 1) * 2 * BLOCK], head) for h in range(2)], axis=0
            )

        share, shift = by_dim(share), by_dim(shift)
        slope = sums[p, 0] + sums[pairs + p, 0]
        chance = sums[p, 1] + sums[pairs + p, 1]
        grad = (share * (slope - shift * chance)).T.astype(jnp.bfloat16)
        d_query[first] = grad[:BLOCK]
        d_query[second] = grad[BLOCK:]
        share, shift = share.T, shift.T
        query = held[rows, :BLOCK].astype(jnp.float32) * share
        out = held[rows, BLOCK:].astype(jnp.float32) * share
        scaled[rows, :BLOCK] = out.astype(jnp.bfloat16)
        scaled[rows, BLOCK : 2 * BLOCK] = (-shift * query).astype(jnp.bfloat16)
        scaled[rows, 2 * BLOCK :] = query.astype(jnp.bfloat16)
        return carry

    lax.fori_loop(0, pairs, step, 0)


def scale(parts, stats, sums, pieces):
    count = len(SLOTS)
    rows = sum(p.shape[0] for p in pieces)
    given = [parts, *in_hbm(stats, sums, *pieces)]
    return pl.pallas_call(
        scale_kernel,
        out_shape=[
            pltpu.HBM((count, BLOCK, BLOCK), jnp.bfloat16),
            pltpu.HBM((rows, 3 * BLOCK), jnp.bfloat16),
        ],
        in_specs=[VMEM] + [ANY] * (len(given) - 1),
        out_specs=[VMEM] * 2,
        scratch_shapes=[
            pltpu.VMEM((rows, 2 * BLOCK), jnp.bfloat16),
            pltpu.VMEM((4 * count, BLOCK), jnp.float32),
            pltpu.VMEM(stats.shape, stats.dtype),
            pltpu.VMEM(sums.shape, sums.dtype),
            pltpu.SemaphoreType.DMA((len(given) - 1,)),
        ],
        compiler_params=room(16),
        cost_estimate=cost(1 << 27, 1 << 16),
        name="scale",
    )(*given)


def gather_kernel(scaled, chance, slope, *rest):
    *sent, d_key, d_value = rest
    p = pl.program_id(0)
    value = key = None
    for i in range(chance.shape[0]):
        rows = slice(2 * i * BLOCK, 2 * (i + 1) * BLOCK)
        out, lack, query = (split_heads(scaled[rows, j * BLOCK : (j + 1) * BLOCK]) for j in range(3))
        both = dot_nn(chance[i], jnp.concatenate([out, lack], axis=1))
        more, least = both[:, :BLOCK], both[:, BLOCK:] + dot_nn(slope[i], query)
        value, key = (more, least) if value is None else (value + more, key + least)

    @pl.when(p == 0)
    def _():
        d_value[...] = value
        d_key[...] = key

    @pl.when(p > 0)
    def _():
        d_value[...] += value
        d_key[...] += key

    @pl.when(p == pl.num_programs(0) - 1)
    def _():
        half = d_key.shape[0] // 2
        for i, target in enumerate(sent):
            rows = slice(i * half, (i + 1) * half)
            target[:, :BLOCK] = d_key[rows, :].astype(target.dtype)
            target[:, BLOCK:] = d_value[rows, :].astype(target.dtype)


def gather(scaled, chance, slope, side, kind):
    pairs, enc, lanes = chance.shape
    pairs, step = pairs // 2, 1
    steps = pairs // step
    table = pl.BlockSpec((step, enc, lanes), lambda p: (side * steps + p, 0, 0))
    given = in_hbm(scaled, chance, slope)
    return pl.pallas_call(
        gather_kernel,
        grid=(steps,),
        out_shape=[jax.ShapeDtypeStruct((enc // 2, 2 * BLOCK), kind)] * 2,
        in_specs=[pl.BlockSpec((step * 2 * BLOCK, scaled.shape[1]), lambda p: (p, 0)), table, table],
        out_specs=[VMEM] * 2,
        scratch_shapes=[pltpu.VMEM((enc, BLOCK), jnp.float32)] * 2,
        compiler_params=room(20),
        cost_estimate=cost(3 * pairs * enc * lanes * BLOCK, 0),
        name="gather",
    )(*given)


def project_kernel(core, grads, from_core, kw, vw, far_kw, far_vw, memory):
    rows = from_core.shape[0]
    mine = grads[pl.ds(pl.multiple_of(core[0] * rows, rows), rows), :]
    other = from_core[...]
    for j in range(0, memory.shape[0], 2):
        part = slice(j * BLOCK, (j + 2) * BLOCK)
        total = dot_nt(mine[:, :BLOCK], kw[part, :]) + dot_nt(mine[:, BLOCK:], vw[part, :])
        total = total + dot_nt(other[:, :BLOCK], far_kw[part, :]) + dot_nt(other[:, BLOCK:], far_vw[part, :])
        memory[j] = total[:, :BLOCK].astype(jnp.bfloat16)
        memory[j + 1] = total[:, BLOCK:].astype(jnp.bfloat16)


def project(core, *given):
    return pl.pallas_call(
        project_kernel,
        out_shape=jax.ShapeDtypeStruct((given[2].shape[0] // BLOCK, given[1].shape[0], BLOCK), jnp.bfloat16),
        in_specs=[SMEM] + [VMEM] * len(given),
        out_specs=VMEM,
        compiler_params=room(8),
        name="project",
    )(core, *given)


def moved(value, axis, steps):
    count = lax.axis_size(axis)
    return lax.ppermute(value, axis, [(i, (i + steps) % count) for i in range(count)])


def body(queries, keys, values, d_out, key_weight, value_weight, block_lists):
    f32, bf16 = jnp.float32, jnp.bfloat16
    half = lax.axis_index("xh")
    place = lax.axis_index(ZH)
    parity = lax.axis_index("par")
    core = lax.axis_index("core")
    depth = lax.axis_size(Z)
    enc_rows = keys.shape[0]
    enc_blocks = enc_rows // BLOCK

    near, own = join(queries, d_out, keys, values)
    side = moved(own, "xh", 1)
    next_ = moved(own, "par", 1)
    ahead = moved(near, Z, 4)
    behind = moved(near, Z, -4)
    across = moved(near, Z, 8)
    late, ahead, behind = lax.optimization_barrier((own, ahead, behind))
    tables = [own, side, next_, lax.ppermute(late, ("xh", "par"), [(0, 3), (1, 2), (2, 1), (3, 0)])]

    count = lax.axis_size(ZH)
    listed = lax.dynamic_slice_in_dim(block_lists, half * depth, depth, 0).reshape(count, depth // count, -1)
    listed = lax.dynamic_index_in_dim(listed, parity, 1, keepdims=False)
    step = jnp.arange(enc_blocks, dtype=jnp.int32)
    ids = jnp.concatenate(
        [((h * count + place) * 2 + p) * enc_blocks + step for p in (parity, 1 - parity) for h in (half, 1 - half)]
    )
    member = jnp.any(listed[:, :, None] == ids[None, None, :], axis=1).astype(jnp.int32).reshape(-1)

    bundle = jnp.concatenate([behind, near, ahead, across], axis=0)
    above = moved(bundle[: 2 * BLOCK], Z, -2)
    below = moved(bundle[BLOCK : 3 * BLOCK], Z, 2)

    early = forward(member, tables[:2], [bundle], None)
    pieces = [bundle, above, below]
    parts, stats = forward(member, tables, pieces, early)
    parts = lax.all_to_all(parts, ZH, 0, 0, tiled=True)
    sums, chances, slopes = local(member, stats, tables, pieces)
    parts, sums, chances, slopes = lax.optimization_barrier((parts, sums, chances, slopes))

    d_query, scaled = scale(parts, stats, sums, pieces)
    d_query = lax.all_to_all(d_query, ZH, 0, 0, tiled=True)
    onward, next_ = (moved(part, "par", 1) for part in reversed(gather(scaled, chances, slopes, 1, bf16)))
    grads, side = gather(scaled, chances, slopes, 0, f32)
    side, onward, d_query = lax.optimization_barrier((side, onward, d_query))
    from_half = moved((side + onward.astype(f32)).astype(bf16), "xh", 1)
    grads, key_weight, value_weight = lax.optimization_barrier((grads, key_weight, value_weight))
    far_key_weight = moved(key_weight, "core", 1)
    far_value_weight = moved(value_weight, "core", 1)
    grads = (grads + next_.astype(f32) + from_half.astype(f32)).astype(bf16)
    from_core = moved(lax.dynamic_slice_in_dim(grads, (1 - core) * (enc_rows // 2), enc_rows // 2, 0), "core", 1)

    cores = lax.axis_size("core")
    weights = (key_weight, value_weight, far_key_weight, far_value_weight)
    memory = project(core[None], grads, from_core, *weights)
    memory = lax.all_to_all(memory, HEAD, 0, 0, tiled=True)
    memory = memory.reshape(-1, cores, *memory.shape[1:]).astype(f32)
    d_memory = jnp.sum(memory, axis=0).reshape(keys.shape).astype(bf16)
    d_queries = jnp.sum(d_query.astype(f32), axis=0).astype(bf16)
    return d_queries, d_memory


def solution(mesh):
    fine = Mesh(mesh.devices.reshape(SIZES), AXES)
    placed = P(CTX, HEAD)
    return jax.shard_map(
        body,
        mesh=fine,
        in_specs=(placed, placed, placed, placed, P(None, HEAD), P(None, HEAD), P()),
        out_specs=(placed, placed),
        check_vma=False,
    )
```

```python
from functools import partial

import jax
import jax.numpy as jnp
from jax import lax
from jax.experimental import pallas as pl
from jax.experimental.pallas import tpu as pltpu
from jax.sharding import Mesh, PartitionSpec as P

HEAD_DIM = 64
BLOCK = 128
AXES = ("xh", "zh", "par", "xl", "y", "core")
SIZES = (2, 8, 2, 2, 4, 2)
ZH = "zh"
Z = ("zh", "par")
CTX = ("xh", "zh", "par")
HEAD = ("xl", "y", "core")
BIG = 1e30

OWN = (2, 0, -2, 4)
LATER = (3, 1, -1, -3)
SLOTS = OWN + LATER

VMEM = pl.BlockSpec(memory_space=pltpu.VMEM)
ANY = pl.BlockSpec(memory_space=pl.ANY)
SMEM = pl.BlockSpec(memory_space=pltpu.SMEM)


def cost(flops, exps):
    return pl.CostEstimate(flops=4 * flops, bytes_accessed=1 << 20, transcendentals=exps)


def dot_nt(a, b):
    return lax.dot_general(a, b, (((1,), (1,)), ((), ())), preferred_element_type=jnp.float32)


def dot_nn(a, b):
    return lax.dot_general(a, b, (((1,), (0,)), ((), ())), preferred_element_type=jnp.float32)


def split_heads(rows):
    low = lax.broadcasted_iota(jnp.int32, rows.shape, 1) < HEAD_DIM
    zero = jnp.zeros_like(rows)
    return jnp.concatenate([jnp.where(low, rows, zero), jnp.where(low, zero, rows)], axis=0)


def room(mib):
    return pltpu.CompilerParams(vmem_limit_bytes=mib << 20)


def in_hbm(*arrays):
    return [pltpu.with_memory_space_constraint(x, pltpu.HBM) for x in arrays]


def fetch(pairs, sems):
    copies = [pltpu.make_async_copy(source, target, sems.at[i]) for i, (source, target) in enumerate(pairs)]
    for copy in copies:
        copy.start()
    return copies


def stacked(pieces, held):
    at, pairs = 0, []
    for piece in pieces:
        pairs.append((piece, held.at[pl.ds(at, piece.shape[0])]))
        at += piece.shape[0]
    return pairs


def join_kernel(*refs):
    *given, first, second, sems = refs
    pairs = []
    for i, source in enumerate(given):
        width = source.shape[1]
        pairs.append((source, (first, second)[i // 2].at[:, pl.ds(i % 2 * width, width)]))
    for copy in fetch(pairs, sems):
        copy.wait()


def join(*given):
    return pl.pallas_call(
        join_kernel,
        out_shape=[jax.ShapeDtypeStruct((x.shape[0], 2 * x.shape[1]), x.dtype) for x in given[::2]],
        in_specs=[ANY] * 4,
        out_specs=[VMEM] * 2,
        scratch_shapes=[pltpu.SemaphoreType.DMA((4,))],
        compiler_params=room(4),
        name="join",
    )(*in_hbm(*given))


def pair_places(p):
    here, count = lax.axis_index("zh"), lax.axis_size("zh")
    found = []
    for steps in (SLOTS[::2], SLOTS[1::2]):
        step = jnp.int32(steps[-1])
        for i, other in enumerate(steps[:-1]):
            step = jnp.where(p == i, other, step)
        found.append(lax.rem(here + step + count, count))
    return found


def load_targets(pieces, held):
    at = 0
    for piece in pieces:
        held[at : at + piece.shape[0], :] = piece[...]
        at += piece.shape[0]


def away(member, first, second, block, blocks):
    seg = (lax.broadcasted_iota(jnp.int32, (1, 4 * BLOCK), 1) // BLOCK) % 2
    one = jnp.where(member[first * blocks + block] > 0, 0.0, BIG)
    two = jnp.where(member[second * blocks + block] > 0, 0.0, BIG)
    return jnp.where(seg == 0, one, two)


def part_stats(kv, query, out, member, first, second, base, blocks):
    logits = dot_nt(kv[:, :BLOCK], query)
    prob = dot_nt(kv[:, BLOCK:], out)
    here = kv.shape[0] // BLOCK
    off = [away(member, first, second, base + b, blocks) for b in range(here)]
    peak = jnp.full((1, 4 * BLOCK), -1e3, jnp.float32)
    for b in range(here):
        part = logits[b * BLOCK : (b + 1) * BLOCK]
        peak = jnp.maximum(peak, jnp.max(part, axis=0, keepdims=True) - off[b])
    total = jnp.zeros((1, 4 * BLOCK), jnp.float32)
    weighted = jnp.zeros((1, 4 * BLOCK), jnp.float32)
    for b in range(here):
        part = slice(b * BLOCK, (b + 1) * BLOCK)
        raised = jnp.exp(logits[part] - (peak + off[b]))
        total = total + jnp.sum(raised, axis=0, keepdims=True)
        weighted = weighted + jnp.sum(raised * prob[part], axis=0, keepdims=True)
    some = total > 0.0
    log_total = jnp.where(some, peak + jnp.log(jnp.where(some, total, 1.0)), -BIG)
    mean = jnp.where(some, weighted / jnp.where(some, total, 1.0), 0.0)
    return log_total, mean


def union(parts):
    top = parts[0][0]
    for log, _ in parts[1:]:
        top = jnp.maximum(top, log)
    total = jnp.zeros_like(top)
    mean = jnp.zeros_like(top)
    for log, part in parts:
        weight = jnp.exp(log - top)
        total = total + weight
        mean = mean + weight * part
    return top + jnp.log(total), mean / total


def store_stats(stats, first, second, given):
    half = stats.shape[0] // 2
    for start, row in zip((0, half), given, strict=True):
        for h in range(2):
            for s, place in enumerate((first, second)):
                stats[pl.ds(start + 2 * place + h, 1), :] = row[:, (2 * h + s) * BLOCK : (2 * h + s + 1) * BLOCK]


def early_kernel(member, near_ref, side_ref, piece, stats, kv):
    load_targets((near_ref, side_ref), kv)
    blocks = 2 * kv.shape[0] // BLOCK

    def step(p, carry):
        rows = pl.ds(pl.multiple_of(p * 2 * BLOCK, 2 * BLOCK), 2 * BLOCK)
        first, second = pair_places(p)
        query, out = split_heads(piece[rows, :BLOCK]), split_heads(piece[rows, BLOCK:])
        store_stats(stats, first, second, part_stats(kv, query, out, member, first, second, 0, blocks))
        return carry

    lax.fori_loop(0, piece.shape[0] // (2 * BLOCK), step, 0)


def forward_kernel(member, *rest):
    tables, pieces = rest[:4], rest[4:7]
    before, result, stats, held, kv = rest[7:]
    load_targets(pieces, held)
    load_targets(tables[:2], kv.at[0])
    load_targets(tables[2:], kv.at[1])
    blocks = 2 * kv.shape[1] // BLOCK
    pairs = held.shape[0] // (2 * BLOCK)
    known = pieces[0].shape[0] // (2 * BLOCK)
    half = stats.shape[0] // 2

    def step(p, done):
        rows = pl.ds(pl.multiple_of(p * 2 * BLOCK, 2 * BLOCK), 2 * BLOCK)
        first, second = pair_places(p)
        query, out = split_heads(held[rows, :BLOCK]), split_heads(held[rows, BLOCK:])
        if done:
            one = lanes_of(before, first, second, 0), lanes_of(before, first, second, half)
        else:
            one = part_stats(kv.at[0], query, out, member, first, second, 0, blocks)
        two = part_stats(kv.at[1], query, out, member, first, second, blocks // 2, blocks)
        store_stats(stats, first, second, union([one, two]))

    def step_known(p, carry):
        step(p, True)
        return carry

    def step_new(p, carry):
        step(p, False)
        return carry

    lax.fori_loop(0, known, step_known, 0)
    lax.fori_loop(known, pairs, step_new, 0)
    high = stats[:half, :].astype(jnp.bfloat16)
    low = (stats[:half, :] - high.astype(jnp.float32)).astype(jnp.bfloat16)
    message = jnp.concatenate([high, low, stats[half:, :].astype(jnp.bfloat16)], axis=0)
    for peer in range(result.shape[0]):
        result[peer] = message


def forward(member, tables, pieces, before):
    count = len(SLOTS)
    rows = sum(p.shape[0] for p in pieces)
    enc = sum(t.shape[0] for t in tables)
    local = jax.ShapeDtypeStruct((4 * count, BLOCK), jnp.float32)
    if before is None:
        kernel, shapes = early_kernel, local
        scratch = [pltpu.VMEM((enc, 2 * BLOCK), jnp.bfloat16)]
        given = [member, *tables, *pieces]
    else:
        kernel, shapes = forward_kernel, [jax.ShapeDtypeStruct((count, 6 * count, BLOCK), jnp.bfloat16), local]
        scratch = [
            pltpu.VMEM((rows, 2 * BLOCK), jnp.bfloat16),
            pltpu.VMEM((2, enc // 2, 2 * BLOCK), jnp.bfloat16),
        ]
        given = [member, *tables, *pieces, before]
    return pl.pallas_call(
        kernel,
        out_shape=shapes,
        in_specs=[SMEM] + [VMEM] * (len(given) - 1),
        out_specs=VMEM if before is None else [VMEM] * 2,
        scratch_shapes=scratch,
        compiler_params=room(20),
        cost_estimate=cost(2 * rows * enc * 4 * BLOCK, rows * enc * 2),
        name="forward",
    )(*given)


def merge_stats(parts, stats):
    rows = stats.shape[0] // 2
    given = []
    for i in range(parts.shape[0]):
        part = parts[i].astype(jnp.float32)
        given.append((part[:rows] + part[rows : 2 * rows], part[2 * rows :]))
    stats[:rows, :], stats[rows:, :] = union(given)


def lanes_of(stats, first, second, start):
    spots = [start + 2 * place + h for h in range(2) for place in (first, second)]
    return jnp.concatenate([stats[pl.ds(s, 1), :] for s in spots], axis=1)


def local_kernel(member, stats_ref, *rest):
    tables, pieces = rest[:4], rest[4:7]
    sums, chances, slopes, kv, held, stats, turned, sems = rest[7:]
    side, p = pl.program_id(0), pl.program_id(1)
    enc = kv.shape[1]

    @pl.when((side == 0) & (p == 0))
    def _():
        pairs = stacked(tables[:2], kv.at[0]) + stacked(tables[2:], kv.at[1])
        pairs += stacked(pieces, held) + [(stats_ref, stats)]
        for copy in fetch(pairs, sems):
            copy.wait()

    @pl.when(p == 0)
    def _():
        turned[...] = kv[side, :, :BLOCK].T

    blocks = enc // BLOCK
    half = stats.shape[0] // 2
    rows = pl.ds(pl.multiple_of(p * 2 * BLOCK, 2 * BLOCK), 2 * BLOCK)
    first, second = pair_places(p)
    log_total = lanes_of(stats, first, second, 0)
    log_total = jnp.where(log_total > -0.5 * BIG, log_total, BIG)
    mean = lanes_of(stats, first, second, half)
    logits = dot_nt(kv[side, :, :BLOCK], split_heads(held[rows, :BLOCK]))
    prob = dot_nt(kv[side, :, BLOCK:], split_heads(held[rows, BLOCK:]))
    for b in range(blocks):
        part = slice(b * BLOCK, (b + 1) * BLOCK)
        off = away(member, first, second, side * blocks + b, 2 * blocks)
        chance = jnp.exp(logits[part] - (log_total + off))
        chances[0, part, :] = chance.astype(jnp.bfloat16)
        slopes[0, part, :] = (chance * (prob[part] - mean)).astype(jnp.bfloat16)
    for i, table in enumerate((slopes, chances)):
        for h in range(2):
            dims = slice(h * HEAD_DIM, (h + 1) * HEAD_DIM)
            lanes = slice(2 * h * BLOCK, 2 * (h + 1) * BLOCK)
            sums[0, i, dims, :] = dot_nn(turned[dims, :], table[0, :, lanes])


def local(member, stats, tables, pieces):
    rows = sum(p.shape[0] for p in pieces)
    enc = sum(t.shape[0] for t in tables) // 2
    pairs = rows // (2 * BLOCK)
    table = pltpu.HBM((2 * pairs, enc, 4 * BLOCK), jnp.bfloat16)
    given = in_hbm(member, stats, *tables, *pieces)
    return pl.pallas_call(
        local_kernel,
        grid=(2, pairs),
        out_shape=[pltpu.HBM((2 * pairs, 2, BLOCK, 2 * BLOCK), jnp.float32)] + [table] * 2,
        in_specs=[SMEM] + [ANY] * (len(given) - 1),
        out_specs=[pl.BlockSpec((1, 2, BLOCK, 2 * BLOCK), lambda side, p: (side * pairs + p, 0, 0, 0))]
        + [pl.BlockSpec((1, enc, 4 * BLOCK), lambda side, p: (side * pairs + p, 0, 0))] * 2,
        scratch_shapes=[
            pltpu.VMEM((2, enc, 2 * BLOCK), jnp.bfloat16),
            pltpu.VMEM((rows, 2 * BLOCK), jnp.bfloat16),
            pltpu.VMEM(stats.shape, stats.dtype),
            pltpu.VMEM((BLOCK, enc), jnp.bfloat16),
            pltpu.SemaphoreType.DMA((len(given) - 1,)),
        ],
        compiler_params=room(20),
        cost_estimate=cost(3 * rows * 2 * enc * 4 * BLOCK, rows * enc * 4),
        name="local",
    )(*given)


def scale_kernel(parts, stats_ref, sums_ref, *rest):
    pieces = rest[:3]
    d_query, scaled, held, whole, stats, sums, sems = rest[3:]
    copies = fetch(stacked(pieces, held) + [(stats_ref, stats), (sums_ref, sums)], sems)
    merge_stats(parts, whole)
    for copy in copies:
        copy.wait()
    half = stats.shape[0] // 2
    pairs = held.shape[0] // (2 * BLOCK)

    def step(p, carry):
        rows = pl.ds(pl.multiple_of(p * 2 * BLOCK, 2 * BLOCK), 2 * BLOCK)
        first, second = pair_places(p)
        share = jnp.exp(lanes_of(stats, first, second, 0) - lanes_of(whole, first, second, 0))
        shift = lanes_of(whole, first, second, half) - lanes_of(stats, first, second, half)

        def by_dim(row):
            head = (HEAD_DIM, 2 * BLOCK)
            return jnp.concatenate(
                [jnp.broadcast_to(row[:, h * 2 * BLOCK : (h + 1) * 2 * BLOCK], head) for h in range(2)], axis=0
            )

        share, shift = by_dim(share), by_dim(shift)
        slope = sums[p, 0] + sums[pairs + p, 0]
        chance = sums[p, 1] + sums[pairs + p, 1]
        grad = (share * (slope - shift * chance)).T.astype(jnp.bfloat16)
        d_query[first] = grad[:BLOCK]
        d_query[second] = grad[BLOCK:]
        share, shift = share.T, shift.T
        query = held[rows, :BLOCK].astype(jnp.float32) * share
        out = held[rows, BLOCK:].astype(jnp.float32) * share
        scaled[rows, :BLOCK] = out.astype(jnp.bfloat16)
        scaled[rows, BLOCK : 2 * BLOCK] = (-shift * query).astype(jnp.bfloat16)
        scaled[rows, 2 * BLOCK :] = query.astype(jnp.bfloat16)
        return carry

    lax.fori_loop(0, pairs, step, 0)


def scale(parts, stats, sums, pieces):
    count = len(SLOTS)
    rows = sum(p.shape[0] for p in pieces)
    given = [parts, *in_hbm(stats, sums, *pieces)]
    return pl.pallas_call(
        scale_kernel,
        out_shape=[
            pltpu.HBM((count, BLOCK, BLOCK), jnp.bfloat16),
            pltpu.HBM((rows, 3 * BLOCK), jnp.bfloat16),
        ],
        in_specs=[VMEM] + [ANY] * (len(given) - 1),
        out_specs=[VMEM] * 2,
        scratch_shapes=[
            pltpu.VMEM((rows, 2 * BLOCK), jnp.bfloat16),
            pltpu.VMEM((4 * count, BLOCK), jnp.float32),
            pltpu.VMEM(stats.shape, stats.dtype),
            pltpu.VMEM(sums.shape, sums.dtype),
            pltpu.SemaphoreType.DMA((len(given) - 1,)),
        ],
        compiler_params=room(16),
        cost_estimate=cost(1 << 27, 1 << 16),
        name="scale",
    )(*given)


def gather_kernel(scaled, chance, slope, *rest):
    *sent, d_key, d_value = rest
    p = pl.program_id(0)
    value = key = None
    for i in range(chance.shape[0]):
        rows = slice(2 * i * BLOCK, 2 * (i + 1) * BLOCK)
        out, lack, query = (split_heads(scaled[rows, j * BLOCK : (j + 1) * BLOCK]) for j in range(3))
        both = dot_nn(chance[i], jnp.concatenate([out, lack], axis=1))
        more, least = both[:, :BLOCK], both[:, BLOCK:] + dot_nn(slope[i], query)
        value, key = (more, least) if value is None else (value + more, key + least)

    @pl.when(p == 0)
    def _():
        d_value[...] = value
        d_key[...] = key

    @pl.when(p > 0)
    def _():
        d_value[...] += value
        d_key[...] += key

    @pl.when(p == pl.num_programs(0) - 1)
    def _():
        size = sent[0].shape[0]
        for i, target in enumerate(sent):
            rows = slice(i * size, (i + 1) * size)
            target[:, :BLOCK] = d_key[rows, :].astype(target.dtype)
            target[:, BLOCK:] = d_value[rows, :].astype(target.dtype)


def gather(scaled, chance, slope, side, kind, parts):
    pairs, enc, lanes = chance.shape
    pairs, step = pairs // 2, 2
    steps = pairs // step
    table = pl.BlockSpec((step, enc, lanes), lambda p: (side * steps + p, 0, 0))
    given = in_hbm(scaled, chance, slope)
    return pl.pallas_call(
        gather_kernel,
        grid=(steps,),
        out_shape=[jax.ShapeDtypeStruct((enc // parts, 2 * BLOCK), kind)] * parts,
        in_specs=[pl.BlockSpec((step * 2 * BLOCK, scaled.shape[1]), lambda p: (p, 0)), table, table],
        out_specs=[VMEM] * parts,
        scratch_shapes=[pltpu.VMEM((enc, BLOCK), jnp.float32)] * 2,
        compiler_params=room(20),
        cost_estimate=cost(3 * pairs * enc * lanes * BLOCK, 0),
        name="gather",
    )(*given)


def project_kernel(core, grads, from_core, kw, vw, far_kw, far_vw, memory):
    rows = from_core.shape[0]
    mine = grads[pl.ds(pl.multiple_of(core[0] * rows, rows), rows), :]
    other = from_core[...]
    for j in range(0, memory.shape[0], 2):
        part = slice(j * BLOCK, (j + 2) * BLOCK)
        total = dot_nt(mine[:, :BLOCK], kw[part, :]) + dot_nt(mine[:, BLOCK:], vw[part, :])
        total = total + dot_nt(other[:, :BLOCK], far_kw[part, :]) + dot_nt(other[:, BLOCK:], far_vw[part, :])
        memory[j] = total[:, :BLOCK].astype(jnp.bfloat16)
        memory[j + 1] = total[:, BLOCK:].astype(jnp.bfloat16)


def project(core, *given):
    return pl.pallas_call(
        project_kernel,
        out_shape=jax.ShapeDtypeStruct((given[2].shape[0] // BLOCK, given[1].shape[0], BLOCK), jnp.bfloat16),
        in_specs=[SMEM] + [VMEM] * len(given),
        out_specs=VMEM,
        compiler_params=room(8),
        name="project",
    )(core, *given)


def moved(value, axis, steps):
    count = lax.axis_size(axis)
    return lax.ppermute(value, axis, [(i, (i + steps) % count) for i in range(count)])


def body(queries, keys, values, d_out, key_weight, value_weight, block_lists):
    f32, bf16 = jnp.float32, jnp.bfloat16
    half = lax.axis_index("xh")
    place = lax.axis_index(ZH)
    parity = lax.axis_index("par")
    core = lax.axis_index("core")
    depth = lax.axis_size(Z)
    enc_rows = keys.shape[0]
    enc_blocks = enc_rows // BLOCK

    near, own = join(queries, d_out, keys, values)
    side = moved(own, "xh", 1)
    next_ = moved(own, "par", 1)
    ahead = moved(near, Z, 4)
    behind = moved(near, Z, -4)
    middle = ahead.shape[0] // 2
    across = jnp.concatenate([moved(ahead[:middle], Z, 4), moved(behind[middle:], Z, -4)], axis=0)
    late, ahead, behind = lax.optimization_barrier((own, ahead, behind))
    tables = [own, side, next_, lax.ppermute(late, ("xh", "par"), [(0, 3), (1, 2), (2, 1), (3, 0)])]

    count = lax.axis_size(ZH)
    listed = lax.dynamic_slice_in_dim(block_lists, half * depth, depth, 0).reshape(count, depth // count, -1)
    listed = lax.dynamic_index_in_dim(listed, parity, 1, keepdims=False)
    step = jnp.arange(enc_blocks, dtype=jnp.int32)
    ids = jnp.concatenate(
        [((h * count + place) * 2 + p) * enc_blocks + step for p in (parity, 1 - parity) for h in (half, 1 - half)]
    )
    member = jnp.any(listed[:, :, None] == ids[None, None, :], axis=1).astype(jnp.int32).reshape(-1)

    bundle = jnp.concatenate([behind, near, ahead, across], axis=0)
    above = moved(bundle[: 2 * BLOCK], Z, -2)
    below = moved(bundle[BLOCK : 3 * BLOCK], Z, 2)

    early = forward(member, tables[:2], [bundle], None)
    pieces = [bundle, above, below]
    parts, stats = forward(member, tables, pieces, early)
    parts = lax.all_to_all(parts, ZH, 0, 0, tiled=True)
    sums, chances, slopes = local(member, stats, tables, pieces)
    parts, sums, chances, slopes = lax.optimization_barrier((parts, sums, chances, slopes))

    d_query, scaled = scale(parts, stats, sums, pieces)
    from_next = moved(gather(scaled, chances, slopes, 1, bf16, 1)[0], "par", 1)
    grads, side = gather(scaled, chances, slopes, 0, f32, 2)
    d_query, grads = lax.optimization_barrier((d_query, grads))
    d_query = lax.all_to_all(d_query, ZH, 0, 0, tiled=True)
    grads, side, from_next, key_weight, value_weight = lax.optimization_barrier(
        (grads, side, from_next, key_weight, value_weight)
    )
    far_key_weight = moved(key_weight, "core", 1)
    far_value_weight = moved(value_weight, "core", 1)
    from_half = moved((side + from_next[enc_rows:].astype(f32)).astype(bf16), "xh", 1)
    grads = (grads + from_next[:enc_rows].astype(f32) + from_half.astype(f32)).astype(bf16)
    from_core = moved(lax.dynamic_slice_in_dim(grads, (1 - core) * (enc_rows // 2), enc_rows // 2, 0), "core", 1)

    cores = lax.axis_size("core")
    weights = (key_weight, value_weight, far_key_weight, far_value_weight)
    memory = project(core[None], grads, from_core, *weights)
    memory, d_query = lax.optimization_barrier((memory, d_query))
    memory = lax.all_to_all(memory, HEAD, 0, 0, tiled=True)
    memory = memory.reshape(-1, cores, *memory.shape[1:]).astype(f32)
    d_memory = jnp.sum(memory, axis=0).reshape(keys.shape).astype(bf16)
    d_queries = jnp.sum(d_query.astype(f32), axis=0).astype(bf16)
    return d_queries, d_memory


def solution(mesh):
    fine = Mesh(mesh.devices.reshape(SIZES), AXES)
    placed = P(CTX, HEAD)
    return jax.shard_map(
        body,
        mesh=fine,
        in_specs=(placed, placed, placed, placed, P(None, HEAD), P(None, HEAD), P()),
        out_specs=(placed, placed),
        check_vma=False,
    )
```

```python
from functools import partial

import jax
import jax.numpy as jnp
from jax import lax
from jax.experimental import pallas as pl
from jax.experimental.pallas import tpu as pltpu
from jax.sharding import Mesh, PartitionSpec as P

HEAD_DIM = 64
BLOCK = 128
AXES = ("xh", "zh", "par", "xl", "y", "core")
SIZES = (2, 8, 2, 2, 4, 2)
Z = ("zh", "par")
CTX = ("xh", "zh", "par")
HEAD = ("xl", "y", "core")
BIG = 1e30

OWN = (2, 0, -2, 4)
LATER = (3, 1, -1, -3)
SLOTS = OWN + LATER

VMEM = pl.BlockSpec(memory_space=pltpu.VMEM)
ANY = pl.BlockSpec(memory_space=pl.ANY)
SMEM = pl.BlockSpec(memory_space=pltpu.SMEM)


def cost(flops, exps):
    return pl.CostEstimate(flops=4 * flops, bytes_accessed=1 << 20, transcendentals=exps)


def dot_nt(a, b):
    return lax.dot_general(a, b, (((1,), (1,)), ((), ())), preferred_element_type=jnp.float32)


def dot_nn(a, b):
    return lax.dot_general(a, b, (((1,), (0,)), ((), ())), preferred_element_type=jnp.float32)


def split_heads(rows):
    low = lax.broadcasted_iota(jnp.int32, rows.shape, 1) < HEAD_DIM
    zero = jnp.zeros_like(rows)
    return jnp.concatenate([jnp.where(low, rows, zero), jnp.where(low, zero, rows)], axis=0)


def room(mib):
    return pltpu.CompilerParams(vmem_limit_bytes=mib << 20)


def in_hbm(*arrays):
    return [pltpu.with_memory_space_constraint(x, pltpu.HBM) for x in arrays]


def fetch(pairs, sems):
    copies = [pltpu.make_async_copy(source, target, sems.at[i]) for i, (source, target) in enumerate(pairs)]
    for copy in copies:
        copy.start()
    return copies


def stacked(pieces, held):
    at, pairs = 0, []
    for piece in pieces:
        pairs.append((piece, held.at[pl.ds(at, piece.shape[0])]))
        at += piece.shape[0]
    return pairs


def join_kernel(left, right, out, sems):
    width = left.shape[1]
    for copy in fetch([(left, out.at[:, pl.ds(0, width)]), (right, out.at[:, pl.ds(width, width)])], sems):
        copy.wait()


def join(left, right):
    return pl.pallas_call(
        join_kernel,
        out_shape=jax.ShapeDtypeStruct((left.shape[0], 2 * left.shape[1]), left.dtype),
        in_specs=[ANY] * 2,
        out_specs=VMEM,
        scratch_shapes=[pltpu.SemaphoreType.DMA((2,))],
        compiler_params=room(4),
        name="join",
    )(*in_hbm(left, right))


def pair_places(p):
    here, count = lax.axis_index("zh"), lax.axis_size("zh")
    found = []
    for steps in (SLOTS[::2], SLOTS[1::2]):
        step = jnp.int32(steps[-1])
        for i, other in enumerate(steps[:-1]):
            step = jnp.where(p == i, other, step)
        found.append(lax.rem(here + step + count, count))
    return found


def load_targets(pieces, held):
    at = 0
    for piece in pieces:
        held[at : at + piece.shape[0], :] = piece[...]
        at += piece.shape[0]


def away(member, first, second, block, blocks):
    seg = (lax.broadcasted_iota(jnp.int32, (1, 4 * BLOCK), 1) // BLOCK) % 2
    one = jnp.where(member[first * blocks + block] > 0, 0.0, BIG)
    two = jnp.where(member[second * blocks + block] > 0, 0.0, BIG)
    return jnp.where(seg == 0, one, two)


def part_stats(kv, query, out, member, first, second, base, blocks):
    logits = dot_nt(kv[:, :BLOCK], query)
    prob = dot_nt(kv[:, BLOCK:], out)
    here = kv.shape[0] // BLOCK
    off = [away(member, first, second, base + b, blocks) for b in range(here)]
    peak = jnp.full((1, 4 * BLOCK), -1e3, jnp.float32)
    for b in range(here):
        part = logits[b * BLOCK : (b + 1) * BLOCK]
        peak = jnp.maximum(peak, jnp.max(part, axis=0, keepdims=True) - off[b])
    total = jnp.zeros((1, 4 * BLOCK), jnp.float32)
    weighted = jnp.zeros((1, 4 * BLOCK), jnp.float32)
    for b in range(here):
        part = slice(b * BLOCK, (b + 1) * BLOCK)
        raised = jnp.exp(logits[part] - (peak + off[b]))
        total = total + jnp.sum(raised, axis=0, keepdims=True)
        weighted = weighted + jnp.sum(raised * prob[part], axis=0, keepdims=True)
    some = total > 0.0
    log_total = jnp.where(some, peak + jnp.log(jnp.where(some, total, 1.0)), -BIG)
    mean = jnp.where(some, weighted / jnp.where(some, total, 1.0), 0.0)
    return log_total, mean


def union(parts):
    top = parts[0][0]
    for log, _ in parts[1:]:
        top = jnp.maximum(top, log)
    total = jnp.zeros_like(top)
    mean = jnp.zeros_like(top)
    for log, part in parts:
        weight = jnp.exp(log - top)
        total = total + weight
        mean = mean + weight * part
    return top + jnp.log(total), mean / total


def forward_kernel(base, member, *rest):
    tables = rest[:4]
    *pieces, before, result, stats, held, kv = rest[4:]
    load_targets(pieces, held)
    load_targets(tables[:2], kv.at[0])
    load_targets(tables[2:], kv.at[1])
    blocks = 2 * kv.shape[1] // BLOCK
    pairs = held.shape[0] // (2 * BLOCK)
    half = stats.shape[0] // 2
    if before is not None:
        stats[...] = before[...]

    def step(p, carry):
        rows = pl.ds(pl.multiple_of(p * 2 * BLOCK, 2 * BLOCK), 2 * BLOCK)
        first, second = pair_places(base // 2 + p)
        query = split_heads(held[rows, :BLOCK])
        out = split_heads(held[rows, BLOCK:])
        log_total, mean = union(
            [
                part_stats(kv.at[0], query, out, member, first, second, 0, blocks),
                part_stats(kv.at[1], query, out, member, first, second, blocks // 2, blocks),
            ]
        )
        for h in range(2):
            for s, place in enumerate((first, second)):
                lanes = slice((2 * h + s) * BLOCK, (2 * h + s + 1) * BLOCK)
                stats[pl.ds(2 * place + h, 1), :] = log_total[:, lanes]
                stats[pl.ds(half + 2 * place + h, 1), :] = mean[:, lanes]
        return carry

    lax.fori_loop(0, pairs, step, 0)
    if result is not None:
        high = stats[:half, :].astype(jnp.bfloat16)
        low = (stats[:half, :] - high.astype(jnp.float32)).astype(jnp.bfloat16)
        message = jnp.concatenate([high, low, stats[half:, :].astype(jnp.bfloat16)], axis=0)
        for peer in range(result.shape[0]):
            result[peer] = message


def forward(base, member, tables, pieces, before):
    count = len(SLOTS)
    rows = sum(p.shape[0] for p in pieces)
    enc = sum(t.shape[0] for t in tables)
    given = [member, *tables, *pieces]
    local = jax.ShapeDtypeStruct((4 * count, BLOCK), jnp.float32)
    if before is None:
        shapes = [local]
        def kernel(*refs):
            ins, outs = refs[: len(given)], refs[len(given) :]
            forward_kernel(base, *ins, None, None, *outs)
    else:
        given.append(before)
        shapes = [jax.ShapeDtypeStruct((count, 6 * count, BLOCK), jnp.bfloat16), local]
        kernel = partial(forward_kernel, base)
    return pl.pallas_call(
        kernel,
        out_shape=shapes,
        in_specs=[SMEM] + [VMEM] * (len(given) - 1),
        out_specs=[VMEM] * len(shapes),
        scratch_shapes=[
            pltpu.VMEM((rows, 2 * BLOCK), jnp.bfloat16),
            pltpu.VMEM((2, enc // 2, 2 * BLOCK), jnp.bfloat16),
        ],
        compiler_params=room(20),
        cost_estimate=cost(2 * rows * enc * 4 * BLOCK, rows * enc * 2),
        name="forward",
    )(*given)


def merge_stats(parts, stats):
    rows = stats.shape[0] // 2
    given = []
    for i in range(parts.shape[0]):
        part = parts[i].astype(jnp.float32)
        given.append((part[:rows] + part[rows : 2 * rows], part[2 * rows :]))
    stats[:rows, :], stats[rows:, :] = union(given)


def lanes_of(stats, first, second, start):
    spots = [start + 2 * place + h for h in range(2) for place in (first, second)]
    return jnp.concatenate([stats[pl.ds(s, 1), :] for s in spots], axis=1)


def local_kernel(member, stats_ref, *rest):
    tables, pieces = rest[:4], rest[4:7]
    sums, chances, slopes, kv, held, stats, turned, sems = rest[7:]
    side, p = pl.program_id(0), pl.program_id(1)
    enc = kv.shape[1]

    @pl.when((side == 0) & (p == 0))
    def _():
        pairs = stacked(tables[:2], kv.at[0]) + stacked(tables[2:], kv.at[1])
        pairs += stacked(pieces, held) + [(stats_ref, stats)]
        for copy in fetch(pairs, sems):
            copy.wait()

    @pl.when(p == 0)
    def _():
        turned[...] = kv[side, :, :BLOCK].T

    blocks = enc // BLOCK
    half = stats.shape[0] // 2
    rows = pl.ds(pl.multiple_of(p * 2 * BLOCK, 2 * BLOCK), 2 * BLOCK)
    first, second = pair_places(p)
    log_total = lanes_of(stats, first, second, 0)
    log_total = jnp.where(log_total > -0.5 * BIG, log_total, BIG)
    mean = lanes_of(stats, first, second, half)
    logits = dot_nt(kv[side, :, :BLOCK], split_heads(held[rows, :BLOCK]))
    prob = dot_nt(kv[side, :, BLOCK:], split_heads(held[rows, BLOCK:]))
    for b in range(blocks):
        part = slice(b * BLOCK, (b + 1) * BLOCK)
        off = away(member, first, second, side * blocks + b, 2 * blocks)
        chance = jnp.exp(logits[part] - (log_total + off))
        chances[0, part, :] = chance.astype(jnp.bfloat16)
        slopes[0, part, :] = (chance * (prob[part] - mean)).astype(jnp.bfloat16)
    for i, table in enumerate((slopes, chances)):
        for h in range(2):
            dims = slice(h * HEAD_DIM, (h + 1) * HEAD_DIM)
            lanes = slice(2 * h * BLOCK, 2 * (h + 1) * BLOCK)
            sums[0, i, dims, :] = dot_nn(turned[dims, :], table[0, :, lanes])


def local(member, stats, tables, pieces):
    rows = sum(p.shape[0] for p in pieces)
    enc = sum(t.shape[0] for t in tables) // 2
    pairs = rows // (2 * BLOCK)
    table = pltpu.HBM((2 * pairs, enc, 4 * BLOCK), jnp.bfloat16)
    given = in_hbm(member, stats, *tables, *pieces)
    return pl.pallas_call(
        local_kernel,
        grid=(2, pairs),
        out_shape=[pltpu.HBM((2 * pairs, 2, BLOCK, 2 * BLOCK), jnp.float32)] + [table] * 2,
        in_specs=[SMEM] + [ANY] * (len(given) - 1),
        out_specs=[pl.BlockSpec((1, 2, BLOCK, 2 * BLOCK), lambda side, p: (side * pairs + p, 0, 0, 0))]
        + [pl.BlockSpec((1, enc, 4 * BLOCK), lambda side, p: (side * pairs + p, 0, 0))] * 2,
        scratch_shapes=[
            pltpu.VMEM((2, enc, 2 * BLOCK), jnp.bfloat16),
            pltpu.VMEM((rows, 2 * BLOCK), jnp.bfloat16),
            pltpu.VMEM(stats.shape, stats.dtype),
            pltpu.VMEM((BLOCK, enc), jnp.bfloat16),
            pltpu.SemaphoreType.DMA((len(given) - 1,)),
        ],
        compiler_params=room(20),
        cost_estimate=cost(3 * rows * 2 * enc * 4 * BLOCK, rows * enc * 4),
        name="local",
    )(*given)


def scale_kernel(parts, stats_ref, sums_ref, *rest):
    pieces = rest[:3]
    d_query, scaled, held, whole, stats, sums, sems = rest[3:]
    copies = fetch(stacked(pieces, held) + [(stats_ref, stats), (sums_ref, sums)], sems)
    merge_stats(parts, whole)
    parity = lax.axis_index("par")
    for copy in copies:
        copy.wait()
    half = stats.shape[0] // 2
    pairs = held.shape[0] // (2 * BLOCK)

    def step(p, carry):
        rows = pl.ds(pl.multiple_of(p * 2 * BLOCK, 2 * BLOCK), 2 * BLOCK)
        first, second = pair_places(p)
        share = jnp.exp(lanes_of(stats, first, second, 0) - lanes_of(whole, first, second, 0))
        shift = lanes_of(whole, first, second, half) - lanes_of(stats, first, second, half)

        def by_dim(row):
            head = (HEAD_DIM, 2 * BLOCK)
            return jnp.concatenate(
                [jnp.broadcast_to(row[:, h * 2 * BLOCK : (h + 1) * 2 * BLOCK], head) for h in range(2)], axis=0
            )

        share, shift = by_dim(share), by_dim(shift)
        slope = sums[p, 0] + sums[pairs + p, 0]
        chance = sums[p, 1] + sums[pairs + p, 1]
        grad = (share * (slope - shift * chance)).T.astype(jnp.bfloat16)
        part = BLOCK // 2
        for i, place in enumerate((first, second)):
            for j, to in enumerate((parity, 1 - parity)):
                d_query[2 * place + to] = grad[(2 * i + j) * part : (2 * i + j + 1) * part]
        share, shift = share.T, shift.T
        query = held[rows, :BLOCK].astype(jnp.float32) * share
        out = held[rows, BLOCK:].astype(jnp.float32) * share
        scaled[rows, :BLOCK] = out.astype(jnp.bfloat16)
        scaled[rows, BLOCK : 2 * BLOCK] = (-shift * query).astype(jnp.bfloat16)
        scaled[rows, 2 * BLOCK :] = query.astype(jnp.bfloat16)
        return carry

    lax.fori_loop(0, pairs, step, 0)


def scale(parts, stats, sums, pieces):
    count = len(SLOTS)
    rows = sum(p.shape[0] for p in pieces)
    given = [parts, *in_hbm(stats, sums, *pieces)]
    return pl.pallas_call(
        scale_kernel,
        out_shape=[
            pltpu.HBM((2 * count, BLOCK // 2, BLOCK), jnp.bfloat16),
            pltpu.HBM((rows, 3 * BLOCK), jnp.bfloat16),
        ],
        in_specs=[VMEM] + [ANY] * (len(given) - 1),
        out_specs=[VMEM] * 2,
        scratch_shapes=[
            pltpu.VMEM((rows, 2 * BLOCK), jnp.bfloat16),
            pltpu.VMEM((4 * count, BLOCK), jnp.float32),
            pltpu.VMEM(stats.shape, stats.dtype),
            pltpu.VMEM(sums.shape, sums.dtype),
            pltpu.SemaphoreType.DMA((len(given) - 1,)),
        ],
        compiler_params=room(16),
        cost_estimate=cost(1 << 27, 1 << 16),
        name="scale",
    )(*given)


def gather_kernel(scaled, chance, slope, sent, d_key, d_value):
    p = pl.program_id(0)
    value = key = None
    for i in range(chance.shape[0]):
        rows = slice(2 * i * BLOCK, 2 * (i + 1) * BLOCK)
        out, lack, query = (split_heads(scaled[rows, j * BLOCK : (j + 1) * BLOCK]) for j in range(3))
        both = dot_nn(chance[i], jnp.concatenate([out, lack], axis=1))
        more, least = both[:, :BLOCK], both[:, BLOCK:] + dot_nn(slope[i], query)
        value, key = (more, least) if value is None else (value + more, key + least)

    @pl.when(p == 0)
    def _():
        d_value[...] = value
        d_key[...] = key

    @pl.when(p > 0)
    def _():
        d_value[...] += value
        d_key[...] += key

    @pl.when(p == pl.num_programs(0) - 1)
    def _():
        sent[:, :BLOCK] = d_key[...].astype(sent.dtype)
        sent[:, BLOCK:] = d_value[...].astype(sent.dtype)


def gather(scaled, chance, slope, side, kind):
    pairs, enc, lanes = chance.shape
    pairs, step = pairs // 2, 2
    steps = pairs // step
    table = pl.BlockSpec((step, enc, lanes), lambda p: (side * steps + p, 0, 0))
    given = in_hbm(scaled, chance, slope)
    return pl.pallas_call(
        gather_kernel,
        grid=(steps,),
        out_shape=jax.ShapeDtypeStruct((enc, 2 * BLOCK), kind),
        in_specs=[pl.BlockSpec((step * 2 * BLOCK, scaled.shape[1]), lambda p: (p, 0)), table, table],
        out_specs=VMEM,
        scratch_shapes=[pltpu.VMEM((enc, BLOCK), jnp.float32)] * 2,
        compiler_params=room(20),
        cost_estimate=cost(3 * pairs * enc * lanes * BLOCK, 0),
        name="gather",
    )(*given)


def project_kernel(core, grads, from_core, kw, vw, far_kw, far_vw, memory):
    rows = from_core.shape[0]
    mine = grads[pl.ds(pl.multiple_of(core[0] * rows, rows), rows), :]
    other = from_core[...]
    for j in range(0, memory.shape[0], 2):
        part = slice(j * BLOCK, (j + 2) * BLOCK)
        total = dot_nt(mine[:, :BLOCK], kw[part, :]) + dot_nt(mine[:, BLOCK:], vw[part, :])
        total = total + dot_nt(other[:, :BLOCK], far_kw[part, :]) + dot_nt(other[:, BLOCK:], far_vw[part, :])
        memory[j] = total[:, :BLOCK].astype(jnp.bfloat16)
        memory[j + 1] = total[:, BLOCK:].astype(jnp.bfloat16)


def project(core, *given):
    return pl.pallas_call(
        project_kernel,
        out_shape=jax.ShapeDtypeStruct((given[2].shape[0] // BLOCK, given[1].shape[0], BLOCK), jnp.bfloat16),
        in_specs=[SMEM] + [VMEM] * len(given),
        out_specs=VMEM,
        compiler_params=room(8),
        name="project",
    )(core, *given)


def moved(value, axis, steps):
    count = lax.axis_size(axis)
    return lax.ppermute(value, axis, [(i, (i + steps) % count) for i in range(count)])


def body(queries, keys, values, d_out, key_weight, value_weight, block_lists):
    f32, bf16 = jnp.float32, jnp.bfloat16
    half = lax.axis_index("xh")
    place = lax.axis_index("zh")
    parity = lax.axis_index("par")
    core = lax.axis_index("core")
    depth = lax.axis_size(Z)
    enc_rows = keys.shape[0]
    enc_blocks = enc_rows // BLOCK

    near = join(queries, d_out)
    ahead = moved(near, Z, 4)
    behind = moved(near, Z, -4)
    across = moved(near, Z, 8)
    own = join(keys, values)
    late, ahead, behind = lax.optimization_barrier((own, ahead, behind))
    tables = [
        own,
        moved(own, "xh", 1),
        moved(own, "par", 1),
        lax.ppermute(late, ("xh", "par"), [(0, 3), (1, 2), (2, 1), (3, 0)]),
    ]

    count = lax.axis_size("zh")
    listed = lax.dynamic_slice_in_dim(block_lists, half * depth, depth, 0).reshape(count, depth // count, -1)
    listed = lax.dynamic_index_in_dim(listed, parity, 1, keepdims=False)
    step = jnp.arange(enc_blocks, dtype=jnp.int32)
    ids = jnp.concatenate(
        [((h * count + place) * 2 + p) * enc_blocks + step for p in (parity, 1 - parity) for h in (half, 1 - half)]
    )
    member = jnp.any(listed[:, :, None] == ids[None, None, :], axis=1).astype(jnp.int32).reshape(-1)

    bundle = jnp.concatenate([behind, near, ahead, across], axis=0)
    above = moved(bundle[: 2 * BLOCK], Z, -2)
    below = moved(bundle[BLOCK : 3 * BLOCK], Z, 2)

    (early,) = forward(0, member, tables, [bundle], None)
    parts, stats = forward(len(OWN), member, tables, [above, below], early)
    pieces = [bundle, above, below]
    parts = lax.all_to_all(parts, "zh", 0, 0, tiled=True)
    sums, chances, slopes = local(member, stats, tables, pieces)
    parts, sums, chances, slopes = lax.optimization_barrier((parts, sums, chances, slopes))

    d_query, scaled = scale(parts, stats, sums, pieces)
    from_next = moved(gather(scaled, chances, slopes, 1, bf16), "par", 1)
    grads = gather(scaled, chances, slopes, 0, f32)
    d_query, grads = lax.optimization_barrier((d_query, grads))
    d_query = lax.all_to_all(d_query, Z, 0, 0, tiled=True)
    grads, from_next, key_weight, value_weight = lax.optimization_barrier(
        (grads, from_next, key_weight, value_weight)
    )
    far_key_weight = moved(key_weight, "core", 1)
    far_value_weight = moved(value_weight, "core", 1)
    from_half = moved((grads[enc_rows:] + from_next[enc_rows:].astype(f32)).astype(bf16), "xh", 1)
    grads = grads[:enc_rows] + from_next[:enc_rows].astype(f32) + from_half.astype(f32)
    grads = grads.astype(bf16)
    from_core = moved(lax.dynamic_slice_in_dim(grads, (1 - core) * (enc_rows // 2), enc_rows // 2, 0), "core", 1)

    cores = lax.axis_size("core")
    weights = (key_weight, value_weight, far_key_weight, far_value_weight)
    memory = project(core[None], grads, from_core, *weights)
    memory, d_query = lax.optimization_barrier((memory, d_query))
    memory = lax.all_to_all(memory, HEAD, 0, 0, tiled=True)
    memory = memory.reshape(-1, cores, *memory.shape[1:]).astype(f32)
    d_memory = jnp.sum(memory, axis=0).reshape(keys.shape).astype(bf16)
    d_query = jnp.sum(d_query.reshape(count, 2, *d_query.shape[1:]).astype(f32), axis=0).astype(bf16)
    first = lax.dynamic_index_in_dim(d_query, parity, 0, keepdims=False)
    second = moved(lax.dynamic_index_in_dim(d_query, 1 - parity, 0, keepdims=False), "par", 1)
    d_queries = jnp.concatenate([first, second], axis=0)
    return d_queries, d_memory


def solution(mesh):
    fine = Mesh(mesh.devices.reshape(SIZES), AXES)
    placed = P(CTX, HEAD)
    return jax.shard_map(
        body,
        mesh=fine,
        in_specs=(placed, placed, placed, placed, P(None, HEAD), P(None, HEAD), P()),
        out_specs=(placed, placed),
        check_vma=False,
    )
```

```python
from functools import partial

import jax
import jax.numpy as jnp
from jax import lax
from jax.experimental import pallas as pl
from jax.experimental.pallas import tpu as pltpu
from jax.sharding import Mesh, PartitionSpec as P

HEAD_DIM = 64
BLOCK = 128
AXES = ("xh", "zh", "par", "xl", "y", "core")
SIZES = (2, 8, 2, 2, 4, 2)
Z = ("zh", "par")
CTX = ("xh", "zh", "par")
HEAD = ("xl", "y", "core")
BIG = 1e30

OWN = (2, 0, -2, 4)
LATER = (3, 1, -1, -3)
SLOTS = OWN + LATER

VMEM = pl.BlockSpec(memory_space=pltpu.VMEM)
ANY = pl.BlockSpec(memory_space=pl.ANY)
SMEM = pl.BlockSpec(memory_space=pltpu.SMEM)


def cost(flops, exps):
    return pl.CostEstimate(flops=4 * flops, bytes_accessed=1 << 20, transcendentals=exps)


def dot_nt(a, b):
    return lax.dot_general(a, b, (((1,), (1,)), ((), ())), preferred_element_type=jnp.float32)


def dot_nn(a, b):
    return lax.dot_general(a, b, (((1,), (0,)), ((), ())), preferred_element_type=jnp.float32)


def split_heads(rows):
    low = lax.broadcasted_iota(jnp.int32, rows.shape, 1) < HEAD_DIM
    zero = jnp.zeros_like(rows)
    return jnp.concatenate([jnp.where(low, rows, zero), jnp.where(low, zero, rows)], axis=0)


def room(mib):
    return pltpu.CompilerParams(vmem_limit_bytes=mib << 20)


def in_hbm(*arrays):
    return [pltpu.with_memory_space_constraint(x, pltpu.HBM) for x in arrays]


def fetch(pairs, sems):
    copies = [pltpu.make_async_copy(source, target, sems.at[i]) for i, (source, target) in enumerate(pairs)]
    for copy in copies:
        copy.start()
    return copies


def stacked(pieces, held):
    at, pairs = 0, []
    for piece in pieces:
        pairs.append((piece, held.at[pl.ds(at, piece.shape[0])]))
        at += piece.shape[0]
    return pairs


def join_kernel(left, right, out, sems):
    width = left.shape[1]
    for copy in fetch([(left, out.at[:, pl.ds(0, width)]), (right, out.at[:, pl.ds(width, width)])], sems):
        copy.wait()


def join(left, right):
    return pl.pallas_call(
        join_kernel,
        out_shape=jax.ShapeDtypeStruct((left.shape[0], 2 * left.shape[1]), left.dtype),
        in_specs=[ANY] * 2,
        out_specs=VMEM,
        scratch_shapes=[pltpu.SemaphoreType.DMA((2,))],
        compiler_params=room(4),
        name="join",
    )(*in_hbm(left, right))


def pair_places(p):
    here, count = lax.axis_index("zh"), lax.axis_size("zh")
    found = []
    for steps in (SLOTS[::2], SLOTS[1::2]):
        step = jnp.int32(steps[-1])
        for i, other in enumerate(steps[:-1]):
            step = jnp.where(p == i, other, step)
        found.append(lax.rem(here + step + count, count))
    return found


def load_targets(pieces, held):
    at = 0
    for piece in pieces:
        held[at : at + piece.shape[0], :] = piece[...]
        at += piece.shape[0]


def away(member, first, second, block, blocks):
    seg = (lax.broadcasted_iota(jnp.int32, (1, 4 * BLOCK), 1) // BLOCK) % 2
    one = jnp.where(member[first * blocks + block] > 0, 0.0, BIG)
    two = jnp.where(member[second * blocks + block] > 0, 0.0, BIG)
    return jnp.where(seg == 0, one, two)


def part_stats(kv, query, out, member, first, second, base, blocks):
    logits = dot_nt(kv[:, :BLOCK], query)
    prob = dot_nt(kv[:, BLOCK:], out)
    here = kv.shape[0] // BLOCK
    off = [away(member, first, second, base + b, blocks) for b in range(here)]
    peak = jnp.full((1, 4 * BLOCK), -1e3, jnp.float32)
    for b in range(here):
        part = logits[b * BLOCK : (b + 1) * BLOCK]
        peak = jnp.maximum(peak, jnp.max(part, axis=0, keepdims=True) - off[b])
    total = jnp.zeros((1, 4 * BLOCK), jnp.float32)
    weighted = jnp.zeros((1, 4 * BLOCK), jnp.float32)
    for b in range(here):
        part = slice(b * BLOCK, (b + 1) * BLOCK)
        raised = jnp.exp(logits[part] - (peak + off[b]))
        total = total + jnp.sum(raised, axis=0, keepdims=True)
        weighted = weighted + jnp.sum(raised * prob[part], axis=0, keepdims=True)
    some = total > 0.0
    log_total = jnp.where(some, peak + jnp.log(jnp.where(some, total, 1.0)), -BIG)
    mean = jnp.where(some, weighted / jnp.where(some, total, 1.0), 0.0)
    return log_total, mean


def union(parts):
    top = parts[0][0]
    for log, _ in parts[1:]:
        top = jnp.maximum(top, log)
    total = jnp.zeros_like(top)
    mean = jnp.zeros_like(top)
    for log, part in parts:
        weight = jnp.exp(log - top)
        total = total + weight
        mean = mean + weight * part
    return top + jnp.log(total), mean / total


def forward_kernel(base, member, *rest):
    tables = rest[:4]
    *pieces, before, result, stats, held, kv = rest[4:]
    load_targets(pieces, held)
    load_targets(tables[:2], kv.at[0])
    load_targets(tables[2:], kv.at[1])
    blocks = 2 * kv.shape[1] // BLOCK
    pairs = held.shape[0] // (2 * BLOCK)
    half = stats.shape[0] // 2
    if before is not None:
        stats[...] = before[...]

    def step(p, carry):
        rows = pl.ds(pl.multiple_of(p * 2 * BLOCK, 2 * BLOCK), 2 * BLOCK)
        first, second = pair_places(base // 2 + p)
        query = split_heads(held[rows, :BLOCK])
        out = split_heads(held[rows, BLOCK:])
        log_total, mean = union(
            [
                part_stats(kv.at[0], query, out, member, first, second, 0, blocks),
                part_stats(kv.at[1], query, out, member, first, second, blocks // 2, blocks),
            ]
        )
        for h in range(2):
            for s, place in enumerate((first, second)):
                lanes = slice((2 * h + s) * BLOCK, (2 * h + s + 1) * BLOCK)
                stats[pl.ds(2 * place + h, 1), :] = log_total[:, lanes]
                stats[pl.ds(half + 2 * place + h, 1), :] = mean[:, lanes]
        return carry

    for p in range(pairs):
        step(p, 0)
    if result is not None:
        high = stats[:half, :].astype(jnp.bfloat16)
        low = (stats[:half, :] - high.astype(jnp.float32)).astype(jnp.bfloat16)
        message = jnp.concatenate([high, low, stats[half:, :].astype(jnp.bfloat16)], axis=0)
        for peer in range(result.shape[0]):
            result[peer] = message


def forward(base, member, tables, pieces, before):
    count = len(SLOTS)
    rows = sum(p.shape[0] for p in pieces)
    enc = sum(t.shape[0] for t in tables)
    given = [member, *tables, *pieces]
    local = jax.ShapeDtypeStruct((4 * count, BLOCK), jnp.float32)
    if before is None:
        shapes = [local]
        def kernel(*refs):
            ins, outs = refs[: len(given)], refs[len(given) :]
            forward_kernel(base, *ins, None, None, *outs)
    else:
        given.append(before)
        shapes = [jax.ShapeDtypeStruct((count, 6 * count, BLOCK), jnp.bfloat16), local]
        kernel = partial(forward_kernel, base)
    return pl.pallas_call(
        kernel,
        out_shape=shapes,
        in_specs=[SMEM] + [VMEM] * (len(given) - 1),
        out_specs=[VMEM] * len(shapes),
        scratch_shapes=[
            pltpu.VMEM((rows, 2 * BLOCK), jnp.bfloat16),
            pltpu.VMEM((2, enc // 2, 2 * BLOCK), jnp.bfloat16),
        ],
        compiler_params=room(32),
        cost_estimate=cost(2 * rows * enc * 4 * BLOCK, rows * enc * 2),
        name="forward",
    )(*given)


def merge_stats(parts, stats):
    rows = stats.shape[0] // 2
    given = []
    for i in range(parts.shape[0]):
        part = parts[i].astype(jnp.float32)
        given.append((part[:rows] + part[rows : 2 * rows], part[2 * rows :]))
    stats[:rows, :], stats[rows:, :] = union(given)


def lanes_of(stats, first, second, start):
    spots = [start + 2 * place + h for h in range(2) for place in (first, second)]
    return jnp.concatenate([stats[pl.ds(s, 1), :] for s in spots], axis=1)


def local_kernel(member, stats_ref, *rest):
    tables, pieces = rest[:4], rest[4:7]
    sums, chances, slopes, kv, held, stats, turned, sems = rest[7:]
    side, p = pl.program_id(0), pl.program_id(1)
    enc = kv.shape[1]

    @pl.when((side == 0) & (p == 0))
    def _():
        pairs = stacked(tables[:2], kv.at[0]) + stacked(tables[2:], kv.at[1])
        pairs += stacked(pieces, held) + [(stats_ref, stats)]
        for copy in fetch(pairs, sems):
            copy.wait()

    @pl.when(p == 0)
    def _():
        turned[...] = kv[side, :, :BLOCK].T

    blocks = enc // BLOCK
    half = stats.shape[0] // 2
    rows = pl.ds(pl.multiple_of(p * 2 * BLOCK, 2 * BLOCK), 2 * BLOCK)
    first, second = pair_places(p)
    log_total = lanes_of(stats, first, second, 0)
    log_total = jnp.where(log_total > -0.5 * BIG, log_total, BIG)
    mean = lanes_of(stats, first, second, half)
    logits = dot_nt(kv[side, :, :BLOCK], split_heads(held[rows, :BLOCK]))
    prob = dot_nt(kv[side, :, BLOCK:], split_heads(held[rows, BLOCK:]))
    for b in range(blocks):
        part = slice(b * BLOCK, (b + 1) * BLOCK)
        off = away(member, first, second, side * blocks + b, 2 * blocks)
        chance = jnp.exp(logits[part] - (log_total + off))
        chances[0, part, :] = chance.astype(jnp.bfloat16)
        slopes[0, part, :] = (chance * (prob[part] - mean)).astype(jnp.bfloat16)
    for i, table in enumerate((slopes, chances)):
        for h in range(2):
            dims = slice(h * HEAD_DIM, (h + 1) * HEAD_DIM)
            lanes = slice(2 * h * BLOCK, 2 * (h + 1) * BLOCK)
            sums[0, i, dims, :] = dot_nn(turned[dims, :], table[0, :, lanes])


def local(member, stats, tables, pieces):
    rows = sum(p.shape[0] for p in pieces)
    enc = sum(t.shape[0] for t in tables) // 2
    pairs = rows // (2 * BLOCK)
    table = pltpu.HBM((2 * pairs, enc, 4 * BLOCK), jnp.bfloat16)
    given = in_hbm(member, stats, *tables, *pieces)
    return pl.pallas_call(
        local_kernel,
        grid=(2, pairs),
        out_shape=[pltpu.HBM((2 * pairs, 2, BLOCK, 2 * BLOCK), jnp.float32)] + [table] * 2,
        in_specs=[SMEM] + [ANY] * (len(given) - 1),
        out_specs=[pl.BlockSpec((1, 2, BLOCK, 2 * BLOCK), lambda side, p: (side * pairs + p, 0, 0, 0))]
        + [pl.BlockSpec((1, enc, 4 * BLOCK), lambda side, p: (side * pairs + p, 0, 0))] * 2,
        scratch_shapes=[
            pltpu.VMEM((2, enc, 2 * BLOCK), jnp.bfloat16),
            pltpu.VMEM((rows, 2 * BLOCK), jnp.bfloat16),
            pltpu.VMEM(stats.shape, stats.dtype),
            pltpu.VMEM((BLOCK, enc), jnp.bfloat16),
            pltpu.SemaphoreType.DMA((len(given) - 1,)),
        ],
        compiler_params=room(20),
        cost_estimate=cost(3 * rows * 2 * enc * 4 * BLOCK, rows * enc * 4),
        name="local",
    )(*given)


def scale_kernel(parts, stats_ref, sums_ref, *rest):
    pieces = rest[:3]
    d_query, scaled, held, whole, stats, sums, sems = rest[3:]
    copies = fetch(stacked(pieces, held) + [(stats_ref, stats), (sums_ref, sums)], sems)
    merge_stats(parts, whole)
    parity = lax.axis_index("par")
    for copy in copies:
        copy.wait()
    half = stats.shape[0] // 2
    pairs = held.shape[0] // (2 * BLOCK)

    def step(p, carry):
        rows = pl.ds(pl.multiple_of(p * 2 * BLOCK, 2 * BLOCK), 2 * BLOCK)
        first, second = pair_places(p)
        share = jnp.exp(lanes_of(stats, first, second, 0) - lanes_of(whole, first, second, 0))
        shift = lanes_of(whole, first, second, half) - lanes_of(stats, first, second, half)

        def by_dim(row):
            head = (HEAD_DIM, 2 * BLOCK)
            return jnp.concatenate(
                [jnp.broadcast_to(row[:, h * 2 * BLOCK : (h + 1) * 2 * BLOCK], head) for h in range(2)], axis=0
            )

        share, shift = by_dim(share), by_dim(shift)
        slope = sums[p, 0] + sums[pairs + p, 0]
        chance = sums[p, 1] + sums[pairs + p, 1]
        grad = (share * (slope - shift * chance)).T.astype(jnp.bfloat16)
        part = BLOCK // 2
        for i, place in enumerate((first, second)):
            for j, to in enumerate((parity, 1 - parity)):
                d_query[2 * place + to] = grad[(2 * i + j) * part : (2 * i + j + 1) * part]
        share, shift = share.T, shift.T
        query = held[rows, :BLOCK].astype(jnp.float32) * share
        out = held[rows, BLOCK:].astype(jnp.float32) * share
        scaled[rows, :BLOCK] = out.astype(jnp.bfloat16)
        scaled[rows, BLOCK : 2 * BLOCK] = (-shift * query).astype(jnp.bfloat16)
        scaled[rows, 2 * BLOCK :] = query.astype(jnp.bfloat16)
        return carry

    for p in range(pairs):
        step(p, 0)


def scale(parts, stats, sums, pieces):
    count = len(SLOTS)
    rows = sum(p.shape[0] for p in pieces)
    given = [parts, *in_hbm(stats, sums, *pieces)]
    return pl.pallas_call(
        scale_kernel,
        out_shape=[
            pltpu.HBM((2 * count, BLOCK // 2, BLOCK), jnp.bfloat16),
            pltpu.HBM((rows, 3 * BLOCK), jnp.bfloat16),
        ],
        in_specs=[VMEM] + [ANY] * (len(given) - 1),
        out_specs=[VMEM] * 2,
        scratch_shapes=[
            pltpu.VMEM((rows, 2 * BLOCK), jnp.bfloat16),
            pltpu.VMEM((4 * count, BLOCK), jnp.float32),
            pltpu.VMEM(stats.shape, stats.dtype),
            pltpu.VMEM(sums.shape, sums.dtype),
            pltpu.SemaphoreType.DMA((len(given) - 1,)),
        ],
        compiler_params=room(16),
        cost_estimate=cost(1 << 27, 1 << 16),
        name="scale",
    )(*given)


def gather_kernel(scaled, chance, slope, sent, d_key, d_value):
    p = pl.program_id(0)
    value = key = None
    for i in range(chance.shape[0]):
        rows = slice(2 * i * BLOCK, 2 * (i + 1) * BLOCK)
        out, lack, query = (split_heads(scaled[rows, j * BLOCK : (j + 1) * BLOCK]) for j in range(3))
        both = dot_nn(chance[i], jnp.concatenate([out, lack], axis=1))
        more, least = both[:, :BLOCK], both[:, BLOCK:] + dot_nn(slope[i], query)
        value, key = (more, least) if value is None else (value + more, key + least)

    @pl.when(p == 0)
    def _():
        d_value[...] = value
        d_key[...] = key

    @pl.when(p > 0)
    def _():
        d_value[...] += value
        d_key[...] += key

    @pl.when(p == pl.num_programs(0) - 1)
    def _():
        sent[:, :BLOCK] = d_key[...].astype(sent.dtype)
        sent[:, BLOCK:] = d_value[...].astype(sent.dtype)


def gather(scaled, chance, slope, side, kind):
    pairs, enc, lanes = chance.shape
    pairs, step = pairs // 2, 2
    steps = pairs // step
    table = pl.BlockSpec((step, enc, lanes), lambda p: (side * steps + p, 0, 0))
    given = in_hbm(scaled, chance, slope)
    return pl.pallas_call(
        gather_kernel,
        grid=(steps,),
        out_shape=jax.ShapeDtypeStruct((enc, 2 * BLOCK), kind),
        in_specs=[pl.BlockSpec((step * 2 * BLOCK, scaled.shape[1]), lambda p: (p, 0)), table, table],
        out_specs=VMEM,
        scratch_shapes=[pltpu.VMEM((enc, BLOCK), jnp.float32)] * 2,
        compiler_params=room(20),
        cost_estimate=cost(3 * pairs * enc * lanes * BLOCK, 0),
        name="gather",
    )(*given)


def project_kernel(core, grads, from_core, kw, vw, far_kw, far_vw, memory):
    rows = from_core.shape[0]
    mine = grads[pl.ds(pl.multiple_of(core[0] * rows, rows), rows), :]
    other = from_core[...]
    for j in range(0, memory.shape[0], 2):
        part = slice(j * BLOCK, (j + 2) * BLOCK)
        total = dot_nt(mine[:, :BLOCK], kw[part, :]) + dot_nt(mine[:, BLOCK:], vw[part, :])
        total = total + dot_nt(other[:, :BLOCK], far_kw[part, :]) + dot_nt(other[:, BLOCK:], far_vw[part, :])
        memory[j] = total[:, :BLOCK].astype(jnp.bfloat16)
        memory[j + 1] = total[:, BLOCK:].astype(jnp.bfloat16)


def project(core, *given):
    return pl.pallas_call(
        project_kernel,
        out_shape=jax.ShapeDtypeStruct((given[2].shape[0] // BLOCK, given[1].shape[0], BLOCK), jnp.bfloat16),
        in_specs=[SMEM] + [VMEM] * len(given),
        out_specs=VMEM,
        compiler_params=room(8),
        name="project",
    )(core, *given)


def moved(value, axis, steps):
    count = lax.axis_size(axis)
    return lax.ppermute(value, axis, [(i, (i + steps) % count) for i in range(count)])


def body(queries, keys, values, d_out, key_weight, value_weight, block_lists):
    f32, bf16 = jnp.float32, jnp.bfloat16
    half = lax.axis_index("xh")
    place = lax.axis_index("zh")
    parity = lax.axis_index("par")
    core = lax.axis_index("core")
    depth = lax.axis_size(Z)
    enc_rows = keys.shape[0]
    enc_blocks = enc_rows // BLOCK

    near = join(queries, d_out)
    ahead = moved(near, Z, 4)
    behind = moved(near, Z, -4)
    across = moved(near, Z, 8)
    own = join(keys, values)
    late, ahead, behind = lax.optimization_barrier((own, ahead, behind))
    tables = [
        own,
        moved(own, "xh", 1),
        moved(own, "par", 1),
        lax.ppermute(late, ("xh", "par"), [(0, 3), (1, 2), (2, 1), (3, 0)]),
    ]

    count = lax.axis_size("zh")
    listed = lax.dynamic_slice_in_dim(block_lists, half * depth, depth, 0).reshape(count, depth // count, -1)
    listed = lax.dynamic_index_in_dim(listed, parity, 1, keepdims=False)
    step = jnp.arange(enc_blocks, dtype=jnp.int32)
    ids = jnp.concatenate(
        [((h * count + place) * 2 + p) * enc_blocks + step for p in (parity, 1 - parity) for h in (half, 1 - half)]
    )
    member = jnp.any(listed[:, :, None] == ids[None, None, :], axis=1).astype(jnp.int32).reshape(-1)

    bundle = jnp.concatenate([behind, near, ahead, across], axis=0)
    above = moved(bundle[: 2 * BLOCK], Z, -2)
    below = moved(bundle[BLOCK : 3 * BLOCK], Z, 2)

    (early,) = forward(0, member, tables, [bundle], None)
    parts, stats = forward(len(OWN), member, tables, [above, below], early)
    pieces = [bundle, above, below]
    parts = lax.all_to_all(parts, "zh", 0, 0, tiled=True)
    sums, chances, slopes = local(member, stats, tables, pieces)
    parts, sums, chances, slopes = lax.optimization_barrier((parts, sums, chances, slopes))

    d_query, scaled = scale(parts, stats, sums, pieces)
    from_next = moved(gather(scaled, chances, slopes, 1, bf16), "par", 1)
    grads = gather(scaled, chances, slopes, 0, f32)
    d_query, grads = lax.optimization_barrier((d_query, grads))
    d_query = lax.all_to_all(d_query, Z, 0, 0, tiled=True)
    grads, from_next, key_weight, value_weight = lax.optimization_barrier(
        (grads, from_next, key_weight, value_weight)
    )
    far_key_weight = moved(key_weight, "core", 1)
    far_value_weight = moved(value_weight, "core", 1)
    from_half = moved((grads[enc_rows:] + from_next[enc_rows:].astype(f32)).astype(bf16), "xh", 1)
    grads = grads[:enc_rows] + from_next[:enc_rows].astype(f32) + from_half.astype(f32)
    grads = grads.astype(bf16)
    from_core = moved(lax.dynamic_slice_in_dim(grads, (1 - core) * (enc_rows // 2), enc_rows // 2, 0), "core", 1)

    cores = lax.axis_size("core")
    weights = (key_weight, value_weight, far_key_weight, far_value_weight)
    memory = project(core[None], grads, from_core, *weights)
    memory, d_query = lax.optimization_barrier((memory, d_query))
    memory = lax.all_to_all(memory, HEAD, 0, 0, tiled=True)
    memory = memory.reshape(-1, cores, *memory.shape[1:]).astype(f32)
    d_memory = jnp.sum(memory, axis=0).reshape(keys.shape).astype(bf16)
    d_query = jnp.sum(d_query.reshape(count, 2, *d_query.shape[1:]).astype(f32), axis=0).astype(bf16)
    first = lax.dynamic_index_in_dim(d_query, parity, 0, keepdims=False)
    second = moved(lax.dynamic_index_in_dim(d_query, 1 - parity, 0, keepdims=False), "par", 1)
    d_queries = jnp.concatenate([first, second], axis=0)
    return d_queries, d_memory


def solution(mesh):
    fine = Mesh(mesh.devices.reshape(SIZES), AXES)
    placed = P(CTX, HEAD)
    return jax.shard_map(
        body,
        mesh=fine,
        in_specs=(placed, placed, placed, placed, P(None, HEAD), P(None, HEAD), P()),
        out_specs=(placed, placed),
        check_vma=False,
    )
```
